512 devices in a mesh: shot: 16 (over x_lo, z), tile: 32 (over y, x_hi, core).
Axes of the slice: x: 4 (x_hi: 2, x_lo: 2; x = x_hi * 2 + x_lo), y: 8, z: 8, core: 2. Of those that a mesh axis runs over, the one named last changes fastest.
Arguments:
- latent: bfloat16 [96, 16, 64, 64], P('tile', 'shot'), may hold values from -6 to 6
- kernel: bfloat16 [27, 64, 64], replicated, may hold values from -0.15625 to 0.15625
- conv_bias: float32 [64], replicated, may hold values from -3 to 3
- head_weight: bfloat16 [64], replicated, may hold values from -0.75 to 0.75
- density: float32 [192, 32, 128], P('tile'), may hold values from 1 to 2.5
- wave_prev: float32 [16, 192, 32, 128], P('shot', 'tile'), may hold values from -6 to 6
- wave_now: float32 [16, 192, 32, 128], P('shot', 'tile'), may hold values from -6 to 6
- adjoint_next: float32 [16, 192, 32, 128], P('shot', 'tile'), may hold values from -6 to 6
- adjoint_after: float32 [16, 192, 32, 128], P('shot', 'tile'), may hold values from -6 to 6
- source_cell: int32 [16], P('shot'), may hold values from 0 to 786431
- wavelet: float32 [16, 3], P('shot'), may hold values from -24 to 24
- receiver_cells: int32 [16, 128], P('shot'), may hold values from 0 to 786431
- observed: float32 [16, 3, 128], P('shot'), may hold values from -6 to 6
Outputs:
- latent_grad: float32 [96, 16, 64, 64], P('tile', 'shot')
- kernel_grad: float32 [27, 64, 64], replicated
- head_grad: float32 [64], replicated
- bias_grad: float32 [64], replicated
The draws below stay inside these ranges and needn't reach their ends.
All inputs are finite; a program needn't handle non-finite values.
Results may differ from the reference program's by a relative error of at most 0.0034.
The reference program's roundings to bfloat16 on the way count: a program that leaves them out, or rounds other values in their place, can miss the bound.
Values may be sent and summed in bfloat16 or wider, within the bound.
No kernel may reach another device: no remote copies, remote signals or barrier semaphores. Data moves between devices by JAX's collectives and lax.ppermute only.
A program may use at most 64 MiB of HBM per device.

```python
import jax
import jax.numpy as jnp
from jax import lax

C = 64
GY = 128
REC = 128
STEPS = 3
SHOTS = 16
GX = 192
GZ = 32


def place_ends(entries, own_key, least, high):
    index_at = [jax.random.randint(jax.random.fold_in(own_key, axis), (), 0, length) for axis, length in enumerate(entries.shape)]
    longest = entries.shape.index(max(entries.shape))
    next_to = index_at[:longest] + [(index_at[longest] + 1) % entries.shape[longest]] + index_at[longest + 1:]
    return entries.at[tuple(index_at)].set(least).at[tuple(next_to)].set(high)


def steps_of(stream_key, shape, shards, least, largest):
    factor_of = 1.0
    for position, shards_of in shards:
        heights = jax.random.uniform(jax.random.fold_in(jax.random.fold_in(stream_key, 6), position), (shards_of,), jnp.float32, least / len(shards), largest / len(shards))
        factor_of = factor_of * jnp.repeat(jnp.exp(heights), shape[position] // shards_of).reshape((-1,) + (1,) * (len(shape) - 1 - position))
    return factor_of


def centred(rng, dims, width, reach, cuts=(), held_as=jnp.bfloat16):
    entries = width * jax.random.normal(rng, dims, jnp.float32)
    if cuts:
        entries = entries * steps_of(rng, dims, cuts, -0.22, 0.18)
    return jnp.clip(entries, -reach, reach).astype(held_as)


def setup_inputs(seed: int = 0) -> dict:
    arg_keys = jax.random.split(jax.random.key(seed), 14)
    return {
        "latent": centred(arg_keys[0], (GX // 2, GZ // 2, C, GY // 2), 1.0, 6.0, ((0, 32), (1, 16))),
        "kernel": centred(arg_keys[1], (27, C, C), (27 * C) ** -0.5, 0.15625),
        "conv_bias": centred(arg_keys[2], (C,), 0.5, 3.0, (), jnp.float32),
        "head_weight": centred(arg_keys[3], (C,), C ** -0.5, 0.75),
        "density": jnp.clip(1.0 + 1.5 * jax.random.uniform(arg_keys[4], (GX, GZ, GY), jnp.float32) ** steps_of(arg_keys[4], (GX, GZ, GY), ((0, 32),), -0.2, 0.2), 1.0, 2.5),
        "wave_prev": centred(arg_keys[5], (SHOTS, GX, GZ, GY), 1.0, 6.0, ((0, 16), (1, 32)), jnp.float32),
        "wave_now": centred(arg_keys[6], (SHOTS, GX, GZ, GY), 1.0, 6.0, ((0, 16), (1, 32)), jnp.float32),
        "adjoint_next": centred(arg_keys[7], (SHOTS, GX, GZ, GY), 1.0, 6.0, ((0, 16), (1, 32)), jnp.float32),
        "adjoint_after": centred(arg_keys[8], (SHOTS, GX, GZ, GY), 1.0, 6.0, ((0, 16), (1, 32)), jnp.float32),
        "source_cell": place_ends(jax.random.randint(arg_keys[9], (SHOTS,), 0, GX * GZ * GY), jax.random.fold_in(arg_keys[9], 1), 0, (GX * GZ * GY) - 1).astype(jnp.int32),
        "wavelet": centred(arg_keys[10], (SHOTS, STEPS), 4.0, 24.0, ((0, 16),), jnp.float32),
        "receiver_cells": place_ends(jax.random.randint(arg_keys[11], (SHOTS, REC), 0, GX * GZ * GY), jax.random.fold_in(arg_keys[11], 1), 0, (GX * GZ * GY) - 1).astype(jnp.int32),
        "observed": centred(arg_keys[12], (SHOTS, STEPS, REC), 1.0, 6.0, ((0, 16),), jnp.float32),
    }


courant = 0.005
speed_low = 1.5
speed_span = 3.0


def upsample(coarse):
    coarse_x, coarse_z, channels, coarse_y = coarse.shape
    spread = jnp.broadcast_to(coarse[:, None, :, None, :, :, None], (coarse_x, 2, coarse_z, 2, channels, coarse_y, 2))
    return spread.reshape(coarse_x * 2, coarse_z * 2, channels, coarse_y * 2)


def fold_children(fine):
    fine_x, fine_z, channels, fine_y = fine.shape
    grouped = fine.reshape(fine_x // 2, 2, fine_z // 2, 2, channels, fine_y // 2, 2)
    return jnp.sum(grouped, axis=(1, 3, 6))


def shifted_stack(padded, start_x, start_z, starts_y, cells_x, cells_z, cells_y):
    return jnp.concatenate([padded[start_x:start_x + cells_x, start_z:start_z + cells_z, :, start_y:start_y + cells_y] for start_y in starts_y], axis=2)


def convolve(padded, kernel):
    cells_x = padded.shape[0] - 2
    cells_z = padded.shape[1] - 2
    channels = padded.shape[2]
    cells_y = padded.shape[3] - 2
    tap_table = kernel.astype(jnp.float32).reshape(3, 3, 3, channels, channels)
    result = jnp.zeros((cells_x, cells_z, channels, cells_y), jnp.float32)
    for offset_x in range(3):
        for offset_z in range(3):
            stacked = shifted_stack(padded, offset_x, offset_z, (0, 1, 2), cells_x, cells_z, cells_y).astype(jnp.float32)
            matrix = jnp.transpose(tap_table[offset_x, offset_z], (1, 0, 2)).reshape(channels, 3 * channels)
            result = result + jnp.einsum('ok,abky->aboy', matrix, stacked, precision=lax.Precision.HIGHEST)
    return result


def kernel_terms(padded, grad_low):
    cells_x, cells_z, channels, cells_y = grad_low.shape
    grads = grad_low.astype(jnp.float32)
    pieces = []
    for offset_x in range(3):
        for offset_z in range(3):
            stacked = shifted_stack(padded, offset_x, offset_z, (0, 1, 2), cells_x, cells_z, cells_y).astype(jnp.float32)
            product = jnp.einsum('aboy,abky->ok', grads, stacked, precision=lax.Precision.HIGHEST)
            pieces.append(jnp.transpose(product.reshape(channels, 3, channels), (1, 0, 2)))
    return jnp.stack(pieces).reshape(27, channels, channels)


def transposed(grad_padded, kernel):
    cells_x = grad_padded.shape[0] - 2
    cells_z = grad_padded.shape[1] - 2
    channels = grad_padded.shape[2]
    cells_y = grad_padded.shape[3] - 2
    tap_table = kernel.astype(jnp.float32).reshape(3, 3, 3, channels, channels)
    result = jnp.zeros((cells_x, cells_z, channels, cells_y), jnp.float32)
    for offset_x in range(3):
        for offset_z in range(3):
            stacked = shifted_stack(grad_padded, 2 - offset_x, 2 - offset_z, (2, 1, 0), cells_x, cells_z, cells_y).astype(jnp.float32)
            matrix = tap_table[offset_x, offset_z].reshape(3 * channels, channels)
            result = result + jnp.einsum('kc,abky->abcy', matrix, stacked, precision=lax.Precision.HIGHEST)
    return result


def neighbours(padded):
    return (padded[2:, 1:-1, 1:-1], padded[:-2, 1:-1, 1:-1], padded[1:-1, 2:, 1:-1],
            padded[1:-1, :-2, 1:-1], padded[1:-1, 1:-1, 2:], padded[1:-1, 1:-1, :-2])


def face_weights(padded_buoyancy):
    centre = padded_buoyancy[1:-1, 1:-1, 1:-1]
    return tuple(0.5 * (centre + beside) for beside in neighbours(padded_buoyancy))


def apply_faces(padded, faces):
    centre = padded[1:-1, 1:-1, 1:-1]
    result = jnp.zeros_like(centre)
    for weight, beside in zip(faces, neighbours(padded)):
        result = result + weight * (beside - centre)
    return result


def decoder_input(latent_pad, index):
    window = lax.dynamic_slice_in_dim(latent_pad, index, 3, 0)
    fine = upsample(window)[1:-1, 1:-1]
    return jnp.pad(fine, ((0, 0), (0, 0), (0, 0), (1, 1)))


def activations(padded, kernel, conv_bias, head_weight):
    pre_act = convolve(padded, kernel) + conv_bias[None, None, :, None]
    hidden = jax.nn.silu(pre_act).astype(jnp.bfloat16)
    logit = jnp.einsum('abcy,c->aby', hidden.astype(jnp.float32), head_weight.astype(jnp.float32), precision=lax.Precision.HIGHEST)
    return pre_act, hidden, logit


def reference(latent, kernel, conv_bias, head_weight, density, wave_prev, wave_now, adjoint_next, adjoint_after, source_cell, wavelet, receiver_cells, observed):
    latent_pad = jnp.pad(latent, ((1, 1), (1, 1), (0, 0), (0, 0)))
    coarse_rows = jnp.arange(latent.shape[0], dtype=jnp.int32)
    grid_shape = density.shape

    def forward_row(index):
        padded = decoder_input(latent_pad, index)
        pre_act, hidden, logit = activations(padded, kernel, conv_bias, head_weight)
        return speed_low + speed_span * jax.nn.sigmoid(logit)

    velocity = lax.map(forward_row, coarse_rows).reshape(grid_shape)
    buoyancy = 1.0 / density
    faces = face_weights(jnp.pad(buoyancy, 1))
    coefficient = courant * velocity * velocity * density
    factor = 2.0 * courant * velocity * density

    def laplace(field):
        return apply_faces(jnp.pad(field, 1), faces)

    def one_shot(running, inputs):
        previous, current, following, beyond, source, pulses, receivers, records = inputs
        laplacians = []
        residuals = []
        for instant in range(STEPS):
            laplacian = laplace(current)
            laplacians.append(laplacian)
            advanced = 2.0 * current - previous + coefficient * laplacian
            advanced = advanced.reshape(-1).at[source].add(pulses[instant]).reshape(grid_shape)
            residuals.append(advanced.reshape(-1)[receivers] - records[instant])
            previous, current = current, advanced
        laplacians.append(laplace(current))
        coef_grad = following * laplacians[STEPS]
        for instant in reversed(range(STEPS)):
            preceding = 2.0 * following - beyond + laplace(coefficient * following)
            preceding = preceding.reshape(-1).at[receivers].add(residuals[instant]).reshape(grid_shape)
            coef_grad = coef_grad + preceding * laplacians[instant]
            beyond, following = following, preceding
        return running + coef_grad * factor, None

    velocity_grad, ignored = lax.scan(one_shot, jnp.zeros(grid_shape, jnp.float32),
                                      (wave_prev, wave_now, adjoint_next, adjoint_after, source_cell, wavelet, receiver_cells, observed))

    def backward_row(index):
        padded = decoder_input(latent_pad, index)
        pre_act, hidden, logit = activations(padded, kernel, conv_bias, head_weight)
        squash = jax.nn.sigmoid(logit)
        rows_grad = lax.dynamic_slice_in_dim(velocity_grad, index * 2, 2, 0)
        logit_grad = rows_grad * speed_span * squash * (1.0 - squash)
        head_part = jnp.einsum('abcy,aby->c', hidden.astype(jnp.float32), logit_grad, precision=lax.Precision.HIGHEST)
        gate = jax.nn.sigmoid(pre_act)
        pre_grad = logit_grad[:, :, None, :] * head_weight.astype(jnp.float32)[None, None, :, None] * (gate * (1.0 + pre_act * (1.0 - gate)))
        bias_part = jnp.sum(pre_grad, axis=(0, 1, 3))
        grad_low = pre_grad.astype(jnp.bfloat16)
        kernel_part = kernel_terms(padded, grad_low)
        return grad_low, kernel_part, head_part, bias_part

    grads_low, kernel_parts, head_parts, bias_parts = lax.map(backward_row, coarse_rows)
    kernel_grad = jnp.sum(kernel_parts, axis=0)
    head_grad = jnp.sum(head_parts, axis=0)
    bias_grad = jnp.sum(bias_parts, axis=0)
    channels = latent.shape[2]
    grad_full = grads_low.reshape(grid_shape[0], grid_shape[1], channels, grid_shape[2])
    grad_padded = jnp.pad(grad_full, ((1, 1), (1, 1), (0, 0), (1, 1)))

    def latent_row(index):
        window = lax.dynamic_slice_in_dim(grad_padded, index * 2, 4, 0)
        return fold_children(transposed(window, kernel))[0]

    latent_grad = lax.map(latent_row, coarse_rows)
    return latent_grad, kernel_grad, head_grad, bias_grad
```

```python
import functools

import jax
import jax.numpy as jnp
from jax import lax
from jax.experimental import pallas as pl
from jax.experimental.pallas import tpu as pltpu
from jax.sharding import Mesh
from jax.sharding import PartitionSpec as P

SHOT = ("xlo", "z")
TILE = ("y", "xhi", "core")
NEAR = ("xlo", "xhi", "core")
F32 = jnp.float32
BF16 = jnp.bfloat16
courant = 0.005
speed_low = 1.5
speed_span = 3.0
ROWS = 112
NT = (((1,), (1,)), ((), ()))


def sigmoid(v):
    return 1.0 / (1.0 + jnp.exp(-v))


def split(v, parts):
    out = []
    for _ in range(parts):
        piece = v.astype(BF16)
        out.append(piece)
        v = v - piece.astype(F32)
    return out


def spread_matrix():
    coarse = lax.broadcasted_iota(jnp.int32, (64, 384), 0)
    lane = lax.broadcasted_iota(jnp.int32, (64, 384), 1)
    fine = (lane & 127) + (lane >> 7) - 1
    return jnp.where((fine >> 1) == coarse, 1.0, 0.0).astype(BF16)


Z_LINE = ((0, 0, 1), (0, 1, 1), (1, 1, 2), (1, 2, 2))


def decode_kernel(
    z_prev, own, z_next, wall, bias, head, speed_out, pre_out, logit_out, lines_out, lines, sums, row_logit
):
    spread = spread_matrix()
    for zi, ref in enumerate((z_prev, own, z_next)):
        fine = jnp.dot(ref[...].reshape(576, 64), spread, preferred_element_type=F32).astype(BF16)
        for x in range(9):
            for e in range(3):
                lines[x, 64 * e : 64 * e + 64, 128 * zi : 128 * zi + 128] = fine[
                    64 * x : 64 * x + 64, 128 * e : 128 * e + 128
                ]
        for x in range(2, 7):
            lines_out[zi, :, 128 * (x - 2) : 128 * (x - 1)] = lines[x, :, 128 * zi : 128 * zi + 128]

    def products(x, carry):
        product = jnp.dot(wall[...], lines[x], preferred_element_type=F32)
        for a in range(3):
            for zz in range(4):
                total = None
                for b in range(3):
                    zi = Z_LINE[zz][b]
                    term = product[64 * (3 * a + b) : 64 * (3 * a + b) + 64, 128 * zi : 128 * zi + 128]
                    total = term if total is None else total + term
                sums[x, 4 * a + zz] = total
        return carry

    lax.fori_loop(0, 9, products, 0)
    bias_wide = jnp.broadcast_to(bias[...], (64, 128))
    head_wide = jnp.broadcast_to(head[...], (64, 128))

    def line(r, zz):
        return (
            sums[(r - 1) // 2, zz] + sums[r // 2, 4 + zz] + sums[(r + 1) // 2, 8 + zz] + bias_wide
        )

    def logit_of(pre):
        hidden = (pre * sigmoid(pre)).astype(BF16).astype(F32)
        return jnp.sum(hidden * head_wide, axis=0, keepdims=True)

    def inner(k, carry):
        r = k + 5
        for zz in range(4):
            pre = line(r, zz)
            pre_out[k, zz] = pre
            logit = logit_of(pre)
            logit_out[pl.ds(4 * k + zz, 1), :] = logit
            if zz in (1, 2):
                row_logit[pl.ds(2 * (r - 1) + zz - 1, 1), :] = logit
        return carry

    lax.fori_loop(0, 8, inner, 0)

    def outer(k, carry):
        r = jnp.where(k < 4, k + 1, k + 9)
        for zz in (1, 2):
            row_logit[pl.ds(2 * (r - 1) + zz - 1, 1), :] = logit_of(line(r, zz))
        return carry

    lax.fori_loop(0, 8, outer, 0)
    speed = speed_low + speed_span * sigmoid(row_logit[...])
    for s in range(16):
        speed_out[s] = speed


def wave_kernel(
    place,
    source,
    pulses,
    left,
    right,
    density,
    wave_prev,
    wave_now,
    adj_next,
    adj_after,
    speeds,
    receivers,
    observed,
    send,
    buoy,
    faces,
    coef,
    speed,
    maps,
    u2,
    u3,
    u4,
    laps,
    lam4,
    lam3,
    grads,
):
    def windowed(ref, offset, first):
        def get(w):
            if w < 6:
                return left[offset + w - first]
            if w < 12:
                return ref[w - 6]
            return right[offset + w - 12]

        return get

    dens = windowed(density, 18, 0)
    u1 = windowed(wave_now.at[0], 0, 0)
    u0 = windowed(wave_prev.at[0], 6, 1)
    lam5 = windowed(adj_next.at[0], 11, 2)
    lam6 = windowed(adj_after.at[0], 15, 3)

    z_at = lax.broadcasted_iota(jnp.int32, (32, 128), 0)
    y_at = lax.broadcasted_iota(jnp.int32, (32, 128), 1)
    cell = z_at * 128 + y_at
    z_top, z_bottom, y_top, y_bottom = z_at < 31, z_at > 0, y_at < 127, y_at > 0

    def shifts(f):
        return (
            jnp.where(z_top, pltpu.roll(f, 31, 0), 0.0),
            jnp.where(z_bottom, pltpu.roll(f, 1, 0), 0.0),
            jnp.where(y_top, pltpu.roll(f, 127, 1), 0.0),
            jnp.where(y_bottom, pltpu.roll(f, 1, 1), 0.0),
        )

    tile = place[0]
    local = receivers[...] - (tile * 6 - 3) * 4096
    at_row = lax.broadcasted_iota(jnp.int32, (384, 128), 0) == (local >> 7)
    at_y = lax.broadcasted_iota(jnp.int32, (128, 128), 0) == (local & 127)
    picks = [jnp.where(at_y, 1.0, 0.0).astype(BF16)]
    for n in range(3):
        for piece in split(observed[0, n : n + 1, :], 3):
            picks.append(jnp.where(at_y, piece.astype(F32), 0.0).astype(BF16))
    maps[...] = lax.dot_general(
        jnp.where(at_row, 1.0, 0.0).astype(BF16),
        jnp.concatenate(picks, axis=0),
        NT,
        preferred_element_type=F32,
    )

    for w in range(18):
        d = dens(w)
        buoy[w] = jnp.where(d > 0.0, 1.0 / d, 0.0)
    for w in range(1, 17):
        centre = buoy[w]
        inside = jnp.where(centre > 0.0, 0.5, 0.0)
        for i, beside in enumerate((buoy[w + 1], buoy[w - 1]) + shifts(centre)):
            faces[i, w] = inside * (centre + beside)
        for j in range(2):
            speed[w, pl.ds(j, 16, 2), :] = speeds[pl.ds(2 * (w - 1) + j, 16, 32), :]
        v = speed[w]
        coef[w] = courant * v * v * dens(w)

    def laplace(f, w):
        centre = f(w)
        total = None
        for i, beside in enumerate((f(w + 1), f(w - 1)) + shifts(centre)):
            term = faces[i, w] * (beside - centre)
            total = term if total is None else total + term
        return total

    source_cell = source[0] - (tile * 6 - 6) * 4096

    def forward(f, before, n, rows, out):
        for w in rows:
            lap = laplace(f, w)
            if 5 <= w <= 12:
                laps[n, w - 5] = lap
            pulse = jnp.where(cell == source_cell - w * 4096, pulses[0, n], 0.0)
            out[w] = 2.0 * f(w) - before(w) + coef[w] * lap + pulse

    def row_of(ref):
        return lambda w: ref[w]

    forward(u1, u0, 0, range(1, 17), u2)
    forward(row_of(u2), u1, 1, range(2, 16), u3)
    forward(row_of(u3), row_of(u2), 2, range(3, 15), u4)

    def residual(u, n, w):
        at = slice(32 * (w - 3), 32 * (w - 2))
        count = maps[at, 0:128]
        records = [maps[at, 128 * i : 128 * i + 128] for i in range(1 + 3 * n, 4 + 3 * n)]
        return count * u[w] - (records[0] + records[1] + records[2])

    def backward(f, before, u, n, rows, out):
        for w in rows:
            lap = laplace(lambda v: coef[v] * f(v), w)
            out[w] = 2.0 * f(w) - before(w) + lap + residual(u, n, w)

    backward(lam5, lam6, u4, 2, range(3, 15), lam4)
    backward(row_of(lam4), lam5, u3, 1, range(4, 14), lam3)
    grads[...] = jnp.zeros_like(grads)
    for w in range(5, 13):
        lap4 = laplace(row_of(u4), w)
        lap = laplace(lambda v: coef[v] * lam3[v], w)
        lam2 = 2.0 * lam3[w] - lam4[w] + lap + residual(u2, 0, w)
        total = lam5(w) * lap4 + lam4[w] * laps[2, w - 5] + lam3[w] * laps[1, w - 5] + lam2 * laps[0, w - 5]
        grads[w - 5, 8:40, :] = total * (2.0 * courant * speed[w] * dens(w))
    for x in range(8):
        for zz in range(4):
            send[pl.ds(4 * x + zz, 16, 32), :] = grads[x, pl.ds(7 + zz, 16, 2), :]


def backward_kernel(
    received, logits, pre_act, lines, head, folded, latent_out, parts_out, low, low_wide, terms, logit_grads
):
    total = received[0]
    for s in range(1, 16):
        total = total + received[s]
    squash = sigmoid(logits[...])
    logit_grads[...] = total * speed_span * squash * (1.0 - squash)
    head_wide = jnp.broadcast_to(head[...], (64, 128))

    def grad_line(x, zz, sums):
        grad = logit_grads[pl.ds(4 * x + zz, 1), :]
        pre = pre_act[x, zz]
        gate = sigmoid(pre)
        pre_grad = grad * head_wide * (gate * (1.0 + pre * (1.0 - gate)))
        rounded = pre_grad.astype(BF16)
        low[x, zz] = rounded
        if sums is not None:
            px = (x - 1) % 2
            low_wide[2 * px + zz - 1, :, 64 * (x - 1 - px) : 64 * (x + 1 - px)] = rounded
            hidden = (pre * gate).astype(BF16).astype(F32)
            return sums[0] + hidden * grad, sums[1] + pre_grad
        return None

    def owned_rows(x, sums):
        grad_line(x, 0, None)
        grad_line(x, 3, None)
        for zz in (1, 2):
            sums = grad_line(x, zz, sums)
        return sums

    for zz in range(4):
        grad_line(0, zz, None)
        grad_line(7, zz, None)
    zero = jnp.zeros((64, 128), F32)
    sums = (zero, zero)
    for x in range(1, 7):
        sums = owned_rows(x, sums)
    head_sum, bias_sum = sums

    ones = jnp.ones((8, 128), BF16)
    row = None
    for piece in split(jnp.concatenate([head_sum, bias_sum], axis=0), 3):
        term = lax.dot_general(ones, piece, NT, preferred_element_type=F32)
        row = term if row is None else row + term
    parts_out[864:872, :] = row
    parts_out[872:896, :] = jnp.zeros((24, 128), F32)

    parities = {-1: (0,), 0: (0, 1), 1: (1,)}
    found = {}
    for dx in (-1, 0, 1):
        for dz in (-1, 0, 1):
            combos = [(px, pz) for px in parities[dx] for pz in parities[dz]]
            if len(combos) == 2 and dx == 0:
                grads = jnp.concatenate([low_wide[2 * px + pz] for px, pz in combos], axis=0)
            else:
                first = 2 * combos[0][0] + combos[0][1]
                grads = low_wide[first : first + len(combos)].reshape(64 * len(combos), 384)
            beside = lines[1 + dz, :, 128 * (1 + dx) : 128 * (4 + dx)]
            product = lax.dot_general(grads, beside, NT, preferred_element_type=F32)
            for i, (px, pz) in enumerate(combos):
                found[dx, px, dz, pz] = at = len(found)
                terms[at] = product[64 * i : 64 * i + 64]
    pairs = {-1: ((-1, 0), (0, 1)), 0: ((0, 0), (0, 1)), 1: ((0, 0), (1, 1))}
    for a in (-1, 0, 1):
        for b in (-1, 0, 1):
            tap = None
            for dx, px in pairs[a]:
                for dz, pz in pairs[b]:
                    term = terms[found[dx, px, dz, pz]]
                    tap = term if tap is None else tap + term
            at = 96 * (3 * (a + 1) + b + 1)
            parts_out[at : at + 64, :] = tap[:, :128]
            parts_out[at + 64 : at + 96, :] = jnp.concatenate([tap[:32, 128:], tap[32:, 128:]], axis=1)

    stacked = []
    for x in range(3):
        around = low[2 * x : 2 * x + 4].reshape(1024, 128)
        product = jnp.dot(folded[...], around, preferred_element_type=F32)
        both = product[:192] + product[192:]
        stacked.append(jnp.concatenate([both[64 * e : 64 * e + 64] for e in range(3)], axis=1))
    stacked = jnp.concatenate(stacked, axis=0)
    spread = spread_matrix()
    result = None
    for piece in split(stacked, 2):
        term = lax.dot_general(piece, spread, NT, preferred_element_type=F32)
        result = term if result is None else result + term
    for x in range(3):
        latent_out[x, 0] = result[64 * x : 64 * x + 64]


def sum_kernel(received, out):
    total = received[0]
    for s in range(1, 8):
        total = total + received[s]
    for s in range(8):
        out[s] = total


def unpack_kernel(rows, kernel_out, head_out, bias_out):
    for tap in range(9):
        at = 96 * tap
        pair = rows[at : at + 64, :]
        kernel_out[3 * tap] = pair[:, :64]
        kernel_out[3 * tap + 1] = pair[:, 64:]
        last = rows[at + 64 : at + 96, :]
        kernel_out[3 * tap + 2, 0:32] = last[:, :64]
        kernel_out[3 * tap + 2, 32:64] = last[:, 64:]
    row = rows[864:865, :]
    head_out[...] = row[:, :64]
    bias_out[...] = row[:, 64:]


def shape(dims, dtype=F32):
    return jax.ShapeDtypeStruct(dims, dtype)


VMEM = pl.BlockSpec(memory_space=pltpu.VMEM)
SMEM = pl.BlockSpec(memory_space=pltpu.SMEM)


def call(kernel, out_shape, in_specs, scratch=(), megabytes=8):
    outs = out_shape if isinstance(out_shape, tuple) else (out_shape,)
    specs = tuple(VMEM for _ in outs)
    return pl.pallas_call(
        kernel,
        out_shape=out_shape,
        in_specs=list(in_specs),
        out_specs=specs if isinstance(out_shape, tuple) else VMEM,
        scratch_shapes=list(scratch),
        compiler_params=pltpu.CompilerParams(vmem_limit_bytes=megabytes << 20),
    )


decode = call(
    decode_kernel,
    (
        shape((16, 32, 128)),
        shape((8, 4, 64, 128)),
        shape((32, 128)),
        shape((3, 192, 640), BF16),
    ),
    [VMEM] * 6,
    [
        pltpu.VMEM((9, 192, 384), BF16),
        pltpu.VMEM((9, 12, 64, 128), F32),
        pltpu.VMEM((32, 128), F32),
    ],
    32,
)
FIELD = pltpu.VMEM((18, 32, 128), F32)
waves = call(
    wave_kernel,
    shape((512, 128)),
    [SMEM] * 3 + [VMEM] * 10,
    [
        FIELD,
        pltpu.VMEM((6, 18, 32, 128), F32),
        FIELD,
        FIELD,
        pltpu.VMEM((384, 1280), F32),
        FIELD,
        FIELD,
        FIELD,
        pltpu.VMEM((3, 8, 32, 128), F32),
        FIELD,
        FIELD,
        pltpu.VMEM((8, 48, 128), F32),
    ],
    32,
)
backward = call(
    backward_kernel,
    (shape((3, 1, 64, 64)), shape((896, 128))),
    [VMEM] * 6,
    [
        pltpu.VMEM((8, 4, 64, 128), BF16),
        pltpu.VMEM((4, 64, 384), BF16),
        pltpu.VMEM((16, 64, 192), F32),
        pltpu.VMEM((32, 128), F32),
    ],
    32,
)


def shifted(block, axes, size):
    low = lax.ppermute(block[0], axes, [(i, i + 1) for i in range(size - 1)])
    high = lax.ppermute(block[1], axes, [(i + 1, i) for i in range(size - 1)])
    return low, high


def folded_taps(kernel):
    taps = kernel.astype(F32).reshape(3, 3, 3, 64, 64)
    taps = jnp.stack([taps[2], taps[1] + taps[2], taps[0] + taps[1], taps[0]])
    taps = jnp.stack([taps[:, 2], taps[:, 1] + taps[:, 2], taps[:, 0] + taps[:, 1], taps[:, 0]], axis=1)
    table = jnp.transpose(taps, (2, 4, 0, 1, 3)).reshape(192, 1024)
    high = lax.reduce_precision(table, 8, 7)
    return jnp.concatenate([high, table - high], axis=0).astype(BF16)


def per_device(
    latent,
    kernel,
    conv_bias,
    head_weight,
    density,
    wave_prev,
    wave_now,
    adjoint_next,
    adjoint_after,
    source_cell,
    wavelet,
    receiver_cells,
    observed,
):
    tile = lax.axis_index(TILE).astype(jnp.int32)
    coarse = latent.reshape(3, 64, 64)
    low, high = shifted((coarse, coarse), TILE, 32)
    nine = jnp.concatenate([low, coarse, high], axis=0)
    z_prev, z_next = shifted((nine, nine), SHOT, 16)
    to_next = jnp.concatenate(
        [wave_now[0], wave_prev[0, 1:], adjoint_next[0, 2:], adjoint_after[0, 3:], density], axis=0
    )
    to_prev = jnp.concatenate(
        [wave_now[0], wave_prev[0, :5], adjoint_next[0, :4], adjoint_after[0, :3], density], axis=0
    )
    left, right = shifted((to_next, to_prev), TILE, 32)

    wall = jnp.transpose(kernel.reshape(9, 3, 64, 64), (0, 2, 1, 3)).reshape(576, 192)
    folded = folded_taps(kernel)
    head = head_weight.astype(F32).reshape(64, 1)
    speed, pre_act, logits, lines = decode(z_prev, nine, z_next, wall, conv_bias.reshape(64, 1), head)
    speeds = lax.all_to_all(speed, SHOT, 0, 0, tiled=True)
    strips = waves(
        tile.reshape(1),
        source_cell,
        wavelet,
        left,
        right,
        density,
        wave_prev,
        wave_now,
        adjoint_next,
        adjoint_after,
        speeds.reshape(512, 128),
        receiver_cells,
        observed,
    )
    received = lax.all_to_all(strips.reshape(16, 32, 128), SHOT, 0, 0, tiled=True)
    latent_grad, parts = backward(received, logits, pre_act, lines, head, folded)

    add = call(sum_kernel, shape((8, ROWS, 128)), [VMEM], (), 8)
    chunks = parts.reshape(8, ROWS, 128)
    for axes in (NEAR, "y", "z"):
        chunks = add(lax.all_to_all(chunks, axes, 0, 0, tiled=True))
    whole = lax.all_to_all(chunks, NEAR, 0, 0, tiled=True)
    kernel_grad, head_grad, bias_grad = call(
        unpack_kernel,
        (shape((27, 64, 64)), shape((1, 64)), shape((1, 64))),
        [VMEM],
        (),
        8,
    )(whole.reshape(896, 128))
    return latent_grad, kernel_grad, head_grad.reshape(64), bias_grad.reshape(64)


def solution(mesh):
    fine_mesh = Mesh(mesh.devices.reshape(2, 8, 8, 2, 2), ("xlo", "z", "y", "xhi", "core"))
    return jax.shard_map(
        per_device,
        mesh=fine_mesh,
        in_specs=(
            P(TILE, SHOT, None, None),
            P(),
            P(),
            P(),
            P(TILE, None, None),
            P(SHOT, TILE, None, None),
            P(SHOT, TILE, None, None),
            P(SHOT, TILE, None, None),
            P(SHOT, TILE, None, None),
            P(SHOT),
            P(SHOT, None),
            P(SHOT, None),
            P(SHOT, None, None),
        ),
        out_specs=(P(TILE, SHOT, None, None), P(), P(), P()),
        check_vma=False,
    )
```

```python
import jax
import jax.numpy as jnp
from jax import lax
from jax.experimental import pallas as pl
from jax.experimental.pallas import tpu as pltpu
from jax.sharding import Mesh
from jax.sharding import PartitionSpec as P

SHOT = ("xlo", "z")
TILE = ("y", "xhi", "core")
F32 = jnp.float32
BF16 = jnp.bfloat16
courant = 0.005
speed_low = 1.5
speed_span = 3.0
ROWS = 56
NT = (((1,), (1,)), ((), ()))


def sigmoid(v):
    return 1.0 / (1.0 + jnp.exp(-v))


def split(v, parts):
    out = []
    for _ in range(parts):
        piece = v.astype(BF16)
        out.append(piece)
        v = v - piece.astype(F32)
    return out


def spread_matrix():
    coarse = lax.broadcasted_iota(jnp.int32, (64, 384), 0)
    lane = lax.broadcasted_iota(jnp.int32, (64, 384), 1)
    fine = (lane & 127) + (lane >> 7) - 1
    return jnp.where((fine >> 1) == coarse, 1.0, 0.0).astype(BF16)


Z_LINE = ((0, 0, 1), (0, 1, 1), (1, 1, 2), (1, 2, 2))


def start_all(copies):
    for copy in copies:
        copy.start()
    return copies


def wait_all(copies):
    for copy in copies:
        copy.wait()


def prepare_kernel(
    wave_now,
    wave_prev,
    adj_next,
    adj_after,
    density,
    kernel_in,
    coarse,
    bias,
    head,
    to_next,
    to_prev,
    middle,
    wall,
    bias_wide,
    head_wide,
    kernel,
    sems,
):
    copies = [
        pltpu.make_async_copy(kernel_in, kernel, sems.at[10]),
        pltpu.make_async_copy(coarse, middle, sems.at[11]),
    ]
    fields = ((wave_now, 6), (wave_prev, 5), (adj_next, 4), (adj_after, 3), (density, 6))
    at = 0
    for i, (ref, rows) in enumerate(fields):
        field = ref if i == 4 else ref.at[0]
        here = pl.ds(at, rows)
        copies.append(pltpu.make_async_copy(field.at[pl.ds(6 - rows, rows)], to_next.at[here], sems.at[i]))
        copies.append(pltpu.make_async_copy(field.at[pl.ds(0, rows)], to_prev.at[here], sems.at[5 + i]))
        at += rows
    start_all(copies)
    bias_wide[...] = jnp.broadcast_to(bias[...], (128, 64)).T
    head_wide[...] = jnp.broadcast_to(head[...].astype(F32), (128, 64)).T
    copies[0].wait()
    for j in range(9):
        wall[64 * j : 64 * j + 64, :] = jnp.concatenate([kernel[3 * j + e] for e in range(3)], axis=1)
    wait_all(copies[1:])


def join_kernel(low, middle, high, out):
    for i, ref in enumerate((low, middle, high)):
        out[3 * i : 3 * i + 3] = ref[...]


def fold_taps(kernel, folded):
    reach = ((2,), (1, 2), (0, 1), (0,))
    for i in range(4):
        for j in range(0, 4, 2):
            blocks = []
            for jj in (j, j + 1):
                row = []
                for e in range(3):
                    total = None
                    for a in reach[i]:
                        for b in reach[jj]:
                            term = kernel[9 * a + 3 * b + e].astype(F32)
                            total = term if total is None else total + term
                    row.append(total)
                blocks.append(jnp.concatenate(row, axis=1))
            table = jnp.concatenate(blocks, axis=0).T
            high, low = split(table, 2)
            at = 64 * (4 * i + j)
            folded[0:192, at : at + 128] = high
            folded[192:384, at : at + 128] = low


def z_sums(product, rows, store):
    for a in range(3):
        for zz in rows:
            total = None
            for b in range(3):
                zi = Z_LINE[zz][b]
                term = product[64 * (3 * a + b) : 64 * (3 * a + b) + 64, 128 * zi : 128 * zi + 128]
                total = term if total is None else total + term
            store(a, zz, total)


def decode_kernel(
    z_prev, own, z_next, wall, bias, head, left, right, speed_out, lines_out, lines, sums, row_logit
):
    spread = spread_matrix()
    for zi, ref in enumerate((z_prev, own, z_next)):
        fine = jnp.dot(ref[...].reshape(576, 64), spread, preferred_element_type=F32).astype(BF16)
        for x in range(9):
            for e in range(3):
                piece = fine[64 * x : 64 * x + 64, 128 * e : 128 * e + 128]
                lines[x, 64 * e : 64 * e + 64, 128 * zi : 128 * zi + 128] = piece
                if 2 <= x <= 6:
                    lines_out[zi, 64 * e : 64 * e + 64, 128 * (x - 2) : 128 * (x - 1)] = piece

    def products(x, carry):
        product = jnp.dot(wall[...], lines[x], preferred_element_type=F32)

        def store(a, zz, total):
            sums[x, 2 * a + zz - 1] = total

        z_sums(product, (1, 2), store)
        return carry

    lax.fori_loop(0, 9, products, 0, unroll=3)

    def rows(k, carry):
        r = k + 1
        for j in range(2):
            pre = sums[(r - 1) // 2, j] + sums[r // 2, 2 + j] + sums[(r + 1) // 2, 4 + j] + bias[...]
            hidden = (pre * sigmoid(pre)).astype(BF16).astype(F32)
            row_logit[pl.ds(2 * k + j, 1), :] = jnp.sum(hidden * head[...], axis=0, keepdims=True)
        return carry

    lax.fori_loop(0, 16, rows, 0, unroll=2)
    speed = speed_low + speed_span * sigmoid(row_logit[...])
    for s in range(16):
        speed_out[s] = speed


def slopes_kernel(
    lines, wall_in, bias_in, head_in, kernel_in, after, slope_out, folded, wall, bias, head, kernel, sums, sems
):
    copies = start_all(
        [
            pltpu.make_async_copy(source, target, sems.at[i])
            for i, (source, target) in enumerate(
                ((wall_in, wall), (bias_in, bias), (head_in, head), (kernel_in, kernel))
            )
        ]
    )
    wait_all(copies)
    for x in range(5):
        columns = [lines[zi, :, 128 * x : 128 * x + 128] for zi in range(3)]
        product = jnp.dot(wall[...], jnp.concatenate(columns, axis=1), preferred_element_type=F32)

        def store(a, zz, total):
            sums[x, 4 * a + zz] = total

        z_sums(product, range(4), store)

    def rows(k, carry):
        r = k + 1
        for zz in range(4):
            pre = sums[(r - 1) // 2, zz] + sums[r // 2, 4 + zz] + sums[(r + 1) // 2, 8 + zz] + bias[...]
            gate = sigmoid(pre)
            hidden = (pre * gate).astype(BF16)
            slope_out[4 * k + zz] = head[...] * (gate * (1.0 + pre * (1.0 - gate)))
            hidden = hidden.astype(F32)
            if zz in (1, 2):
                slope_out[32 + 2 * k + zz - 1] = hidden
            logit = jnp.sum(hidden * head[...], axis=0, keepdims=True)
            slope_out[48, pl.ds(4 * k + zz, 1), :] = logit
        return carry

    lax.fori_loop(0, 8, rows, 0)
    slope_out[48, 0:32, :] = sigmoid(slope_out[48, 0:32, :])
    slope_out[48, 32:64, :] = jnp.zeros((32, 128), F32)
    fold_taps(kernel, folded)


def shifts(f):
    z_at = lax.broadcasted_iota(jnp.int32, (32, 128), 0)
    y_at = lax.broadcasted_iota(jnp.int32, (32, 128), 1)
    return (
        jnp.where(z_at < 31, pltpu.roll(f, 31, 0), 0.0),
        jnp.where(z_at > 0, pltpu.roll(f, 1, 0), 0.0),
        jnp.where(y_at < 127, pltpu.roll(f, 127, 1), 0.0),
        jnp.where(y_at > 0, pltpu.roll(f, 1, 1), 0.0),
    )


def windowed(left, own, right, field, offset, first):
    def get(w):
        if w < 6:
            return left[offset + w - first]
        if w < 12:
            return own[6 * field + w - 6]
        return right[offset + w - 12]

    return get


def records_kernel(place, receivers_in, observed_in, after, counts, receivers, observed, sems):
    wait_all(
        start_all(
            [
                pltpu.make_async_copy(receivers_in, receivers, sems.at[0]),
                pltpu.make_async_copy(observed_in, observed, sems.at[1]),
            ]
        )
    )
    local = receivers[...] - (place[0] * 6 - 3) * 4096
    at_row = lax.broadcasted_iota(jnp.int32, (384, 128), 0) == (local >> 7)
    at_y = lax.broadcasted_iota(jnp.int32, (128, 128), 0) == (local & 127)
    picks = [jnp.where(at_y, 1.0, 0.0).astype(BF16)]
    for n in range(3):
        for piece in split(observed[n], 3):
            picks.append(jnp.where(at_y, piece.astype(F32), 0.0).astype(BF16))
    maps = lax.dot_general(
        jnp.where(at_row, 1.0, 0.0).astype(BF16),
        jnp.concatenate(picks, axis=0),
        NT,
        preferred_element_type=F32,
    )
    counts[0] = maps[:, 0:128]
    for n in range(3):
        at = 128 + 384 * n
        counts[1 + n] = maps[:, at : at + 128] + maps[:, at + 128 : at + 256] + maps[:, at + 256 : at + 384]


def wave_kernel(
    place,
    source,
    pulses_in,
    left,
    right,
    wave_now,
    wave_prev,
    adj_next,
    adj_after,
    density,
    speeds,
    counts_in,
    send_out,
    own,
    counts,
    pulses,
    faces,
    buoy,
    coef,
    speed,
    u2,
    u3,
    u4,
    laps,
    lam4,
    lam3,
    grads,
    sems,
):
    fields = (wave_now.at[0], wave_prev.at[0], adj_next.at[0], adj_after.at[0], density)
    copies = start_all(
        [pltpu.make_async_copy(f, own.at[pl.ds(6 * i, 6)], sems.at[i]) for i, f in enumerate(fields)]
        + [
            pltpu.make_async_copy(pulses_in, pulses, sems.at[5]),
            pltpu.make_async_copy(counts_in, counts, sems.at[6]),
        ]
    )
    send = send_out.reshape(512, 128)
    u1 = windowed(left, own, right, 0, 0, 0)
    u0 = windowed(left, own, right, 1, 6, 1)
    lam5 = windowed(left, own, right, 2, 11, 2)
    lam6 = windowed(left, own, right, 3, 15, 3)
    dens = windowed(left, own, right, 4, 18, 0)
    cell = lax.broadcasted_iota(jnp.int32, (32, 128), 0) * 128 + lax.broadcasted_iota(
        jnp.int32, (32, 128), 1
    )

    for w in range(1, 17):
        for j in range(2):
            speed[w, pl.ds(j, 16, 2), :] = speeds[pl.ds(2 * (w - 1) + j, 16, 32), :]
    grads[...] = jnp.zeros_like(grads)
    wait_all(copies)
    for w in range(18):
        d = dens(w)
        buoy[w] = jnp.where(d > 0.0, 1.0 / d, 0.0)
    for w in range(1, 17):
        v = speed[w]
        coef[w] = courant * v * v * dens(w)
        centre = buoy[w]
        inside = jnp.where(centre > 0.0, 0.5, 0.0)
        for i, beside in enumerate((buoy[w + 1], buoy[w - 1]) + shifts(centre)):
            faces[i, w] = inside * (centre + beside)

    def laplace(f, w):
        centre = f(w)
        total = None
        for i, beside in enumerate((f(w + 1), f(w - 1)) + shifts(centre)):
            term = faces[i, w] * (beside - centre)
            total = term if total is None else total + term
        return total

    source_cell = source[0] - (place[0] * 6 - 6) * 4096

    def forward(f, before, n, rows, out):
        for w in rows:
            lap = laplace(f, w)
            if 5 <= w <= 12:
                laps[n, w - 5] = lap
            pulse = jnp.where(cell == source_cell - w * 4096, pulses[0, n], 0.0)
            out[w] = 2.0 * f(w) - before(w) + coef[w] * lap + pulse

    def row_of(ref):
        return lambda w: ref[w]

    forward(u1, u0, 0, range(1, 17), u2)
    forward(row_of(u2), u1, 1, range(2, 16), u3)
    forward(row_of(u3), row_of(u2), 2, range(3, 15), u4)

    def residual(u, n, w):
        at = slice(32 * (w - 3), 32 * (w - 2))
        return counts[0, at, :] * u[w] - counts[1 + n, at, :]

    def backward(f, before, u, n, rows, out):
        for w in rows:
            lap = laplace(lambda v: coef[v] * f(v), w)
            out[w] = 2.0 * f(w) - before(w) + lap + residual(u, n, w)

    backward(lam5, lam6, u4, 2, range(3, 15), lam4)
    backward(row_of(lam4), lam5, u3, 1, range(4, 14), lam3)
    for w in range(5, 13):
        lap4 = laplace(row_of(u4), w)
        lap = laplace(lambda v: coef[v] * lam3[v], w)
        lam2 = 2.0 * lam3[w] - lam4[w] + lap + residual(u2, 0, w)
        total = lam5(w) * lap4 + lam4[w] * laps[2, w - 5] + lam3[w] * laps[1, w - 5] + lam2 * laps[0, w - 5]
        grads[w - 5, 8:40, :] = total * (2.0 * courant * speed[w] * dens(w))
    for x in range(8):
        for zz in range(4):
            send[pl.ds(4 * x + zz, 16, 32), :] = grads[x, pl.ds(7 + zz, 16, 2), :]


def backward_kernel(
    received, slopes, lines, folded, latent_out, parts_out, low, low_wide, terms, logit_grads
):
    total = received[0]
    for s in range(1, 16):
        total = total + received[s]
    squash = slopes[48, 0:32, :]
    logit_grads[...] = total * speed_span * squash * (1.0 - squash)
    head_sum = jnp.zeros((64, 128), F32)
    bias_sum = jnp.zeros((64, 128), F32)
    for x in range(8):
        for zz in range(4):
            grad = logit_grads[4 * x + zz : 4 * x + zz + 1, :]
            pre_grad = grad * slopes[4 * x + zz]
            rounded = pre_grad.astype(BF16)
            low[x, zz] = rounded
            if 1 <= x <= 6 and 1 <= zz <= 2:
                px = (x - 1) % 2
                low_wide[2 * px + zz - 1, :, 64 * (x - 1 - px) : 64 * (x + 1 - px)] = rounded
                head_sum = head_sum + slopes[32 + 2 * x + zz - 1] * grad
                bias_sum = bias_sum + pre_grad

    ones = jnp.ones((8, 128), BF16)
    row = None
    for piece in split(jnp.concatenate([head_sum, bias_sum], axis=0), 3):
        term = lax.dot_general(ones, piece, NT, preferred_element_type=F32)
        row = term if row is None else row + term
    parts_out[864:872, :] = row
    parts_out[872:896, :] = jnp.zeros((24, 128), F32)

    parities = {-1: (0,), 0: (0, 1), 1: (1,)}
    found = {}
    for dx in (-1, 0, 1):
        for dz in (-1, 0, 1):
            combos = [(px, pz) for px in parities[dx] for pz in parities[dz]]
            if len(combos) == 2 and dx == 0:
                grads = jnp.concatenate([low_wide[2 * px + pz] for px, pz in combos], axis=0)
            else:
                first = 2 * combos[0][0] + combos[0][1]
                grads = low_wide[first : first + len(combos)].reshape(64 * len(combos), 384)
            beside = lines[1 + dz, :, 128 * (1 + dx) : 128 * (4 + dx)]
            product = lax.dot_general(grads, beside, NT, preferred_element_type=F32)
            for i, (px, pz) in enumerate(combos):
                found[dx, px, dz, pz] = at = len(found)
                terms[at] = product[64 * i : 64 * i + 64]
    pairs = {-1: ((-1, 0), (0, 1)), 0: ((0, 0), (0, 1)), 1: ((0, 0), (1, 1))}
    for a in (-1, 0, 1):
        for b in (-1, 0, 1):
            tap = None
            for dx, px in pairs[a]:
                for dz, pz in pairs[b]:
                    term = terms[found[dx, px, dz, pz]]
                    tap = term if tap is None else tap + term
            at = 96 * (3 * (a + 1) + b + 1)
            parts_out[at : at + 64, :] = tap[:, :128]
            parts_out[at + 64 : at + 96, :] = jnp.concatenate([tap[:32, 128:], tap[32:, 128:]], axis=1)

    stacked = []
    for x in range(3):
        around = low[2 * x : 2 * x + 4].reshape(1024, 128)
        product = jnp.dot(folded[...], around, preferred_element_type=F32)
        both = product[:192] + product[192:]
        stacked.append(jnp.concatenate([both[64 * e : 64 * e + 64] for e in range(3)], axis=1))
    stacked = jnp.concatenate(stacked, axis=0)
    spread = spread_matrix()
    result = None
    for piece in split(stacked, 2):
        term = lax.dot_general(piece, spread, NT, preferred_element_type=F32)
        result = term if result is None else result + term
    for x in range(3):
        latent_out[x, 0] = result[64 * x : 64 * x + 64]


def sum_kernel(received, out):
    total = received[0]
    for s in range(1, received.shape[0]):
        total = total + received[s]
    for s in range(out.shape[0]):
        out[s] = total


def unpack_kernel(rows, kernel_out, head_out, bias_out):
    for tap in range(9):
        at = 96 * tap
        pair = rows[at : at + 64, :]
        kernel_out[3 * tap] = pair[:, :64]
        kernel_out[3 * tap + 1] = pair[:, 64:]
        last = rows[at + 64 : at + 96, :]
        kernel_out[3 * tap + 2, 0:32] = last[:, :64]
        kernel_out[3 * tap + 2, 32:64] = last[:, 64:]
    row = rows[864:865, :]
    head_out[...] = row[:, :64]
    bias_out[...] = row[:, 64:]


def shape(dims, dtype=F32):
    return jax.ShapeDtypeStruct(dims, dtype)


VMEM = pl.BlockSpec(memory_space=pltpu.VMEM)
ANY = pl.BlockSpec(memory_space=pl.ANY)
HBM = pl.BlockSpec(memory_space=pltpu.HBM)
SMEM = pl.BlockSpec(memory_space=pltpu.SMEM)


def call(kernel, out_shape, in_specs, scratch=(), megabytes=8):
    outs = out_shape if isinstance(out_shape, tuple) else (out_shape,)
    specs = tuple(VMEM for _ in outs)
    return pl.pallas_call(
        kernel,
        out_shape=out_shape,
        in_specs=list(in_specs),
        out_specs=specs if isinstance(out_shape, tuple) else VMEM,
        scratch_shapes=list(scratch),
        compiler_params=pltpu.CompilerParams(vmem_limit_bytes=megabytes << 20),
    )


FIELD = pltpu.VMEM((18, 32, 128), F32)
prepare = call(
    prepare_kernel,
    (
        shape((24, 32, 128)),
        shape((24, 32, 128)),
        shape((3, 64, 64), BF16),
        shape((576, 192), BF16),
        shape((64, 128)),
        shape((64, 128)),
    ),
    [HBM] * 7 + [VMEM] * 2,
    [pltpu.VMEM((27, 64, 64), BF16), pltpu.SemaphoreType.DMA((12,))],
    6,
)
join = call(join_kernel, shape((9, 64, 64), BF16), [VMEM] * 3, (), 2)
decode = call(
    decode_kernel,
    (shape((16, 32, 128)), shape((3, 192, 640), BF16)),
    [VMEM] * 6 + [ANY] * 2,
    [
        pltpu.VMEM((9, 192, 384), BF16),
        pltpu.VMEM((9, 6, 64, 128), F32),
        pltpu.VMEM((32, 128), F32),
    ],
    14,
)
slopes = call(
    slopes_kernel,
    (shape((49, 64, 128)), shape((384, 1024), BF16)),
    [VMEM] + [HBM] * 4 + [ANY],
    [
        pltpu.VMEM((576, 192), BF16),
        pltpu.VMEM((64, 128), F32),
        pltpu.VMEM((64, 128), F32),
        pltpu.VMEM((27, 64, 64), BF16),
        pltpu.VMEM((5, 12, 64, 128), F32),
        pltpu.SemaphoreType.DMA((4,)),
    ],
    14,
)
records = call(
    records_kernel,
    shape((4, 384, 128)),
    [SMEM] + [HBM] * 2 + [ANY],
    [
        pltpu.VMEM((1, 128), jnp.int32),
        pltpu.VMEM((3, 1, 128), F32),
        pltpu.SemaphoreType.DMA((2,)),
    ],
    8,
)
waves = call(
    wave_kernel,
    shape((16, 32, 128)),
    [SMEM] * 2 + [HBM] + [VMEM] * 2 + [HBM] * 5 + [VMEM] + [HBM],
    [
        pltpu.VMEM((30, 32, 128), F32),
        pltpu.VMEM((4, 384, 128), F32),
        pltpu.SMEM((1, 3), F32),
        pltpu.VMEM((6, 18, 32, 128), F32),
        FIELD,
        FIELD,
        FIELD,
        FIELD,
        FIELD,
        FIELD,
        pltpu.VMEM((3, 8, 32, 128), F32),
        FIELD,
        FIELD,
        pltpu.VMEM((8, 48, 128), F32),
        pltpu.SemaphoreType.DMA((7,)),
    ],
    14,
)
backward = call(
    backward_kernel,
    (shape((3, 1, 64, 64)), shape((896, 128))),
    [VMEM] * 4,
    [
        pltpu.VMEM((8, 4, 64, 128), BF16),
        pltpu.VMEM((4, 64, 384), BF16),
        pltpu.VMEM((16, 64, 192), F32),
        pltpu.VMEM((32, 128), F32),
    ],
    14,
)


def in_hbm(x):
    return pltpu.with_memory_space_constraint(x, pltpu.HBM)


def shifted(block, axes, size):
    low = lax.ppermute(block[0], axes, [(i, i + 1) for i in range(size - 1)])
    high = lax.ppermute(block[1], axes, [(i + 1, i) for i in range(size - 1)])
    return low, high


def per_device(
    latent,
    kernel,
    conv_bias,
    head_weight,
    density,
    wave_prev,
    wave_now,
    adjoint_next,
    adjoint_after,
    source_cell,
    wavelet,
    receiver_cells,
    observed,
):
    place = lax.axis_index(TILE).astype(jnp.int32).reshape(1)
    coarse = latent.reshape(3, 64, 64)
    low, high = shifted((coarse, coarse), TILE, 32)
    fields = [in_hbm(f) for f in (wave_now, wave_prev, adjoint_next, adjoint_after, density)]
    taps = in_hbm(kernel)
    to_next, to_prev, middle, wall, bias, head = prepare(
        *fields, taps, in_hbm(coarse), conv_bias.reshape(1, 64), head_weight.reshape(1, 64)
    )
    low, high, to_next, to_prev = lax.optimization_barrier((low, high, to_next, to_prev))
    left, right = shifted((to_next, to_prev), TILE, 32)
    nine = join(low, middle, high)
    z_prev, z_next = shifted((nine, nine), SHOT, 16)

    speed, lines = decode(z_prev, nine, z_next, wall, bias, head, left, right)
    speeds = lax.all_to_all(speed, SHOT, 0, 0, tiled=True)
    counts = records(
        place, in_hbm(receiver_cells), in_hbm(jnp.transpose(observed, (1, 0, 2))), in_hbm(speed)
    )
    strips = waves(
        place,
        source_cell,
        in_hbm(wavelet),
        left,
        right,
        *fields,
        speeds.reshape(512, 128),
        in_hbm(counts),
    )
    received = lax.all_to_all(strips, SHOT, 0, 0, tiled=True)
    slope, folded = slopes(lines, in_hbm(wall), in_hbm(bias), in_hbm(head), taps, in_hbm(strips))
    latent_grad, parts = backward(received, slope, lines, folded)

    chunks = lax.all_to_all(parts.reshape(16, ROWS, 128), SHOT, 0, 0, tiled=True)
    for axes, copies in ((("xhi", "core"), 4), ("y", 8)):
        chunks = call(sum_kernel, shape((copies, ROWS, 128)), [VMEM])(chunks)
        chunks = lax.all_to_all(chunks, axes, 0, 0, tiled=True)
    chunks = call(sum_kernel, shape((16, ROWS, 128)), [VMEM])(chunks)
    whole = lax.all_to_all(chunks, SHOT, 0, 0, tiled=True)
    kernel_grad, head_grad, bias_grad = call(
        unpack_kernel, (shape((27, 64, 64)), shape((1, 64)), shape((1, 64))), [VMEM]
    )(whole.reshape(896, 128))
    head_grad = head_grad.reshape(64)
    bias_grad = bias_grad.reshape(64)
    return latent_grad, kernel_grad, head_grad, bias_grad


def solution(mesh):
    fine_mesh = Mesh(mesh.devices.reshape(2, 8, 8, 2, 2), ("xlo", "z", "y", "xhi", "core"))
    return jax.shard_map(
        per_device,
        mesh=fine_mesh,
        in_specs=(
            P(TILE, SHOT, None, None),
            P(),
            P(),
            P(),
            P(TILE, None, None),
            P(SHOT, TILE, None, None),
            P(SHOT, TILE, None, None),
            P(SHOT, TILE, None, None),
            P(SHOT, TILE, None, None),
            P(SHOT),
            P(SHOT, None),
            P(SHOT, None),
            P(SHOT, None, None),
        ),
        out_specs=(P(TILE, SHOT, None, None), P(), P(), P()),
        check_vma=False,
    )
```

```python
import jax
import jax.numpy as jnp
from jax import lax
from jax.experimental import pallas as pl
from jax.experimental.pallas import tpu as pltpu
from jax.sharding import Mesh
from jax.sharding import PartitionSpec as P

SHOT = ("xlo", "z")
TILE = ("y", "xhi", "core")
NEAR = ("xlo", "xhi", "core")
FAR = ("z", "y")
F32 = jnp.float32
BF16 = jnp.bfloat16
courant = 0.005
speed_low = 1.5
speed_span = 3.0
NT = (((1,), (1,)), ((), ()))


def sigmoid(v):
    return 1.0 / (1.0 + jnp.exp(-v))


def split(v, parts):
    out = []
    for _ in range(parts):
        piece = v.astype(BF16)
        out.append(piece)
        v = v - piece.astype(F32)
    return out


def spread_matrix():
    coarse = lax.broadcasted_iota(jnp.int32, (64, 384), 0)
    lane = lax.broadcasted_iota(jnp.int32, (64, 384), 1)
    fine = (lane & 127) + (lane >> 7) - 1
    return jnp.where((fine >> 1) == coarse, 1.0, 0.0).astype(BF16)


Z_LINE = ((0, 0, 1), (0, 1, 1), (1, 1, 2), (1, 2, 2))


def start_all(copies):
    for copy in copies:
        copy.start()
    return copies


def wait_all(copies):
    for copy in copies:
        copy.wait()


def pack_kernel(
    wave_now, wave_prev, adj_next, adj_after, density, latent, to_next, to_prev, coarse, sems
):
    copies = [pltpu.make_async_copy(latent, coarse, sems.at[10])]
    fields = ((wave_now, 6), (wave_prev, 5), (adj_next, 4), (adj_after, 3), (density, 6))
    at = 0
    for i, (ref, rows) in enumerate(fields):
        field = ref if i == 4 else ref.at[0]
        here = pl.ds(at, rows)
        copies.append(pltpu.make_async_copy(field.at[pl.ds(6 - rows, rows)], to_next.at[here], sems.at[i]))
        copies.append(pltpu.make_async_copy(field.at[pl.ds(0, rows)], to_prev.at[here], sems.at[5 + i]))
        at += rows
    start_all(copies)
    copies[0].wait()
    for x in range(3):
        block = coarse[x].astype(F32)
        packed = jnp.concatenate([block[0:32], block[32:64]], axis=1)
        to_next[24 + x] = packed
        to_prev[24 + x] = packed
    wait_all(copies[1:])


def join_kernel(left, coarse, right, out):
    for i, ref in ((0, left), (2, right)):
        for x in range(3):
            packed = ref[24 + x]
            out[3 * i + x] = jnp.concatenate([packed[:, :64], packed[:, 64:]], axis=0).astype(BF16)
    out[3:6] = coarse[...]


def taps_kernel(kernel_in, bias, head, wall, bias_wide, head_wide, kernel, sem):
    copy = pltpu.make_async_copy(kernel_in, kernel, sem)
    copy.start()
    bias_wide[...] = jnp.broadcast_to(bias[...], (128, 64)).T
    head_wide[...] = jnp.broadcast_to(head[...].astype(F32), (128, 64)).T
    copy.wait()
    for j in range(9):
        wall[64 * j : 64 * j + 64, :] = jnp.concatenate([kernel[3 * j + e] for e in range(3)], axis=1)


def fold_taps(kernel, folded):
    reach = ((2,), (1, 2), (0, 1), (0,))
    for i in range(4):
        for j in range(0, 4, 2):
            blocks = []
            for jj in (j, j + 1):
                row = []
                for e in range(3):
                    total = None
                    for a in reach[i]:
                        for b in reach[jj]:
                            term = kernel[9 * a + 3 * b + e].astype(F32)
                            total = term if total is None else total + term
                    row.append(total)
                blocks.append(jnp.concatenate(row, axis=1))
            table = jnp.concatenate(blocks, axis=0).T
            high, low = split(table, 2)
            at = 64 * (4 * i + j)
            folded[0:192, at : at + 128] = high
            folded[192:384, at : at + 128] = low


def z_sums(product, rows, store):
    for a in range(3):
        for zz in rows:
            total = None
            for b in range(3):
                zi = Z_LINE[zz][b]
                term = product[64 * (3 * a + b) : 64 * (3 * a + b) + 64, 128 * zi : 128 * zi + 128]
                total = term if total is None else total + term
            store(a, zz, total)


def decode_kernel(
    z_prev, own, z_next, wall, bias, head, speed_out, lines_out, lines, sums, row_logit
):
    spread = spread_matrix()
    for zi, ref in enumerate((z_prev, own, z_next)):
        fine = jnp.dot(ref[...].reshape(576, 64), spread, preferred_element_type=F32).astype(BF16)
        for x in range(9):
            for e in range(3):
                piece = fine[64 * x : 64 * x + 64, 128 * e : 128 * e + 128]
                lines[x, 64 * e : 64 * e + 64, 128 * zi : 128 * zi + 128] = piece
                if 2 <= x <= 6:
                    lines_out[zi, 64 * e : 64 * e + 64, 128 * (x - 2) : 128 * (x - 1)] = piece

    def products(x, carry):
        product = jnp.dot(wall[...], lines[x], preferred_element_type=F32)

        def store(a, zz, total):
            sums[x, 2 * a + zz - 1] = total

        z_sums(product, (1, 2), store)
        return carry

    lax.fori_loop(0, 9, products, 0, unroll=3)

    def rows(k, carry):
        r = k + 1
        for j in range(2):
            pre = sums[(r - 1) // 2, j] + sums[r // 2, 2 + j] + sums[(r + 1) // 2, 4 + j] + bias[...]
            hidden = (pre * sigmoid(pre)).astype(BF16).astype(F32)
            row_logit[pl.ds(2 * k + j, 1), :] = jnp.sum(hidden * head[...], axis=0, keepdims=True)
        return carry

    lax.fori_loop(0, 16, rows, 0, unroll=2)
    speed = speed_low + speed_span * sigmoid(row_logit[...])
    for s in range(16):
        speed_out[s] = speed


def slopes_kernel(
    lines, wall_in, bias_in, head_in, kernel_in, after, slope_out, folded, wall, bias, head, kernel, sums, sems
):
    copies = start_all(
        [
            pltpu.make_async_copy(source, target, sems.at[i])
            for i, (source, target) in enumerate(
                ((wall_in, wall), (bias_in, bias), (head_in, head), (kernel_in, kernel))
            )
        ]
    )
    wait_all(copies)
    for x in range(5):
        columns = [lines[zi, :, 128 * x : 128 * x + 128] for zi in range(3)]
        product = jnp.dot(wall[...], jnp.concatenate(columns, axis=1), preferred_element_type=F32)

        def store(a, zz, total):
            sums[x, 4 * a + zz] = total

        z_sums(product, range(4), store)

    def rows(k, owned):
        r = k + 1
        for zz in range(4):
            pre = sums[(r - 1) // 2, zz] + sums[r // 2, 4 + zz] + sums[(r + 1) // 2, 8 + zz] + bias[...]
            gate = sigmoid(pre)
            hidden = (pre * gate).astype(BF16).astype(F32)
            slope_out[4 * k + zz] = head[...] * (gate * (1.0 + pre * (1.0 - gate)))
            if owned and zz in (1, 2):
                slope_out[30 + 2 * k + zz - 1] = hidden
            logit = jnp.sum(hidden * head[...], axis=0, keepdims=True)
            slope_out[44, pl.ds(4 * k + zz, 1), :] = logit
        return owned

    rows(0, False)
    lax.fori_loop(1, 7, lambda k, carry: rows(k, True), True)
    rows(7, False)
    slope_out[44, 0:32, :] = sigmoid(slope_out[44, 0:32, :])
    slope_out[44, 32:64, :] = jnp.zeros((32, 128), F32)
    fold_taps(kernel, folded)


def shifts(f):
    z_at = lax.broadcasted_iota(jnp.int32, (32, 128), 0)
    y_at = lax.broadcasted_iota(jnp.int32, (32, 128), 1)
    return (
        jnp.where(z_at < 31, pltpu.roll(f, 31, 0), 0.0),
        jnp.where(z_at > 0, pltpu.roll(f, 1, 0), 0.0),
        jnp.where(y_at < 127, pltpu.roll(f, 127, 1), 0.0),
        jnp.where(y_at > 0, pltpu.roll(f, 1, 1), 0.0),
    )


def windowed(left, own, right, field, offset, first):
    def get(w):
        if w < 6:
            return left[offset + w - first]
        if w < 12:
            return own[6 * field + w - 6]
        return right[offset + w - 12]

    return get


def medium_kernel(
    place,
    wave_now,
    wave_prev,
    adj_next,
    adj_after,
    density,
    receivers_in,
    observed_in,
    after,
    own,
    counts_out,
    counts,
    receivers,
    observed,
    sems,
):
    fields = (wave_now.at[0], wave_prev.at[0], adj_next.at[0], adj_after.at[0], density)
    wait_all(
        start_all(
            [pltpu.make_async_copy(f, own.at[pl.ds(6 * i, 6)], sems.at[i]) for i, f in enumerate(fields)]
            + [
                pltpu.make_async_copy(receivers_in, receivers, sems.at[5]),
                pltpu.make_async_copy(observed_in, observed, sems.at[6]),
            ]
        )
    )
    local = receivers[...] - (place[0] * 6 - 3) * 4096
    at_row = lax.broadcasted_iota(jnp.int32, (384, 128), 0) == (local >> 7)
    at_y = lax.broadcasted_iota(jnp.int32, (128, 128), 0) == (local & 127)
    picks = [jnp.where(at_y, 1.0, 0.0).astype(BF16)]
    for n in range(3):
        for piece in split(observed[n], 3):
            picks.append(jnp.where(at_y, piece.astype(F32), 0.0).astype(BF16))
    maps = lax.dot_general(
        jnp.where(at_row, 1.0, 0.0).astype(BF16),
        jnp.concatenate(picks, axis=0),
        NT,
        preferred_element_type=F32,
    )
    counts[0] = maps[:, 0:128]
    for n in range(3):
        at = 128 + 384 * n
        counts[1 + n] = maps[:, at : at + 128] + maps[:, at + 128 : at + 256] + maps[:, at + 256 : at + 384]
    wait_all(start_all([pltpu.make_async_copy(counts, counts_out, sems.at[7])]))


def wave_kernel(
    place,
    source,
    pulses_in,
    left,
    right,
    speeds,
    own,
    counts_in,
    send_out,
    counts,
    pulses,
    faces,
    buoy,
    coef,
    speed,
    u2,
    u3,
    u4,
    laps,
    lam4,
    lam3,
    grads,
    sems,
):
    copies = start_all(
        [
            pltpu.make_async_copy(pulses_in, pulses, sems.at[0]),
            pltpu.make_async_copy(counts_in, counts, sems.at[1]),
        ]
    )
    send = send_out.reshape(512, 128)
    u1 = windowed(left, own, right, 0, 0, 0)
    u0 = windowed(left, own, right, 1, 6, 1)
    lam5 = windowed(left, own, right, 2, 11, 2)
    lam6 = windowed(left, own, right, 3, 15, 3)
    dens = windowed(left, own, right, 4, 18, 0)
    cell = lax.broadcasted_iota(jnp.int32, (32, 128), 0) * 128 + lax.broadcasted_iota(
        jnp.int32, (32, 128), 1
    )

    for w in range(1, 17):
        for j in range(2):
            speed[w, pl.ds(j, 16, 2), :] = speeds[pl.ds(2 * (w - 1) + j, 16, 32), :]
    grads[...] = jnp.zeros_like(grads)
    for w in range(18):
        d = dens(w)
        buoy[w] = jnp.where(d > 0.0, 1.0 / d, 0.0)
    for w in range(1, 17):
        v = speed[w]
        coef[w] = courant * v * v * dens(w)
        centre = buoy[w]
        inside = jnp.where(centre > 0.0, 0.5, 0.0)
        for i, beside in enumerate((buoy[w + 1], buoy[w - 1]) + shifts(centre)):
            faces[i, w] = inside * (centre + beside)
    copies[0].wait()

    def laplace(f, w):
        centre = f(w)
        total = None
        for i, beside in enumerate((f(w + 1), f(w - 1)) + shifts(centre)):
            term = faces[i, w] * (beside - centre)
            total = term if total is None else total + term
        return total

    source_cell = source[0] - (place[0] * 6 - 6) * 4096

    def forward(f, before, n, rows, out):
        for w in rows:
            lap = laplace(f, w)
            if 5 <= w <= 12:
                laps[n, w - 5] = lap
            pulse = jnp.where(cell == source_cell - w * 4096, pulses[0, n], 0.0)
            out[w] = 2.0 * f(w) - before(w) + coef[w] * lap + pulse

    def row_of(ref):
        return lambda w: ref[w]

    forward(u1, u0, 0, range(1, 17), u2)
    forward(row_of(u2), u1, 1, range(2, 16), u3)
    forward(row_of(u3), row_of(u2), 2, range(3, 15), u4)

    def residual(u, n, w):
        at = slice(32 * (w - 3), 32 * (w - 2))
        return counts[0, at, :] * u[w] - counts[1 + n, at, :]

    def backward(f, before, u, n, rows, out):
        for w in rows:
            lap = laplace(lambda v: coef[v] * f(v), w)
            out[w] = 2.0 * f(w) - before(w) + lap + residual(u, n, w)

    copies[1].wait()
    backward(lam5, lam6, u4, 2, range(3, 15), lam4)
    backward(row_of(lam4), lam5, u3, 1, range(4, 14), lam3)
    for w in range(5, 13):
        lap4 = laplace(row_of(u4), w)
        lap = laplace(lambda v: coef[v] * lam3[v], w)
        lam2 = 2.0 * lam3[w] - lam4[w] + lap + residual(u2, 0, w)
        total = lam5(w) * lap4 + lam4[w] * laps[2, w - 5] + lam3[w] * laps[1, w - 5] + lam2 * laps[0, w - 5]
        grads[w - 5, 8:40, :] = total * (2.0 * courant * speed[w] * dens(w))
    for x in range(8):
        for zz in range(4):
            send[pl.ds(4 * x + zz, 16, 32), :] = grads[x, pl.ds(7 + zz, 16, 2), :]


def backward_kernel(
    received, slopes, lines, folded, latent_out, parts_out, low, low_wide, terms, logit_grads
):
    total = received[0]
    for s in range(1, 16):
        total = total + received[s]
    squash = slopes[44, 0:32, :]
    logit_grads[...] = total * speed_span * squash * (1.0 - squash)
    head_sum = jnp.zeros((64, 128), F32)
    bias_sum = jnp.zeros((64, 128), F32)
    for x in range(8):
        for zz in range(4):
            grad = logit_grads[4 * x + zz : 4 * x + zz + 1, :]
            pre_grad = grad * slopes[4 * x + zz]
            rounded = pre_grad.astype(BF16)
            low[x, zz] = rounded
            if 1 <= x <= 6 and 1 <= zz <= 2:
                px = (x - 1) % 2
                low_wide[2 * px + zz - 1, :, 64 * (x - 1 - px) : 64 * (x + 1 - px)] = rounded
                head_sum = head_sum + slopes[30 + 2 * x + zz - 1] * grad
                bias_sum = bias_sum + pre_grad

    ones = jnp.ones((8, 128), BF16)
    row = None
    for piece in split(jnp.concatenate([head_sum, bias_sum], axis=0), 3):
        term = lax.dot_general(ones, piece, NT, preferred_element_type=F32)
        row = term if row is None else row + term
    parts_out[864:872, :] = row
    parts_out[872:1024, :] = jnp.zeros((152, 128), F32)

    parities = {-1: (0,), 0: (0, 1), 1: (1,)}
    found = {}
    for dx in (-1, 0, 1):
        for dz in (-1, 0, 1):
            combos = [(px, pz) for px in parities[dx] for pz in parities[dz]]
            if len(combos) == 2 and dx == 0:
                grads = jnp.concatenate([low_wide[2 * px + pz] for px, pz in combos], axis=0)
            else:
                first = 2 * combos[0][0] + combos[0][1]
                grads = low_wide[first : first + len(combos)].reshape(64 * len(combos), 384)
            beside = lines[1 + dz, :, 128 * (1 + dx) : 128 * (4 + dx)]
            product = lax.dot_general(grads, beside, NT, preferred_element_type=F32)
            for i, (px, pz) in enumerate(combos):
                found[dx, px, dz, pz] = at = len(found)
                terms[at] = product[64 * i : 64 * i + 64]
    pairs = {-1: ((-1, 0), (0, 1)), 0: ((0, 0), (0, 1)), 1: ((0, 0), (1, 1))}
    for a in (-1, 0, 1):
        for b in (-1, 0, 1):
            tap = None
            for dx, px in pairs[a]:
                for dz, pz in pairs[b]:
                    term = terms[found[dx, px, dz, pz]]
                    tap = term if tap is None else tap + term
            at = 96 * (3 * (a + 1) + b + 1)
            parts_out[at : at + 64, :] = tap[:, :128]
            parts_out[at + 64 : at + 96, :] = jnp.concatenate([tap[:32, 128:], tap[32:, 128:]], axis=1)

    stacked = []
    for x in range(3):
        around = low[2 * x : 2 * x + 4].reshape(1024, 128)
        product = jnp.dot(folded[...], around, preferred_element_type=F32)
        both = product[:192] + product[192:]
        stacked.append(jnp.concatenate([both[64 * e : 64 * e + 64] for e in range(3)], axis=1))
    stacked = jnp.concatenate(stacked, axis=0)
    spread = spread_matrix()
    result = None
    for piece in split(stacked, 2):
        term = lax.dot_general(piece, spread, NT, preferred_element_type=F32)
        result = term if result is None else result + term
    for x in range(3):
        latent_out[x, 0] = result[64 * x : 64 * x + 64]


def sum_kernel(received, out):
    total = received[0]
    for s in range(1, 8):
        total = total + received[s]
    out[...] = total


def sum_pairs_kernel(received, out):
    total = received[0:8, :]
    for s in range(1, 16):
        total = total + received[8 * s : 8 * s + 8, :]
    pair = total[0:2] + total[2:4] + total[4:6] + total[6:8]
    pairs = jnp.concatenate([pair] * 4, axis=0)
    for s in range(16):
        out[8 * s : 8 * s + 8, :] = pairs


def repeat_kernel(chunk, out):
    for s in range(8):
        out[s] = chunk[...]


def unpack_kernel(rows, kernel_out, head_out, bias_out):
    for tap in range(9):
        at = 96 * tap
        pair = rows[at : at + 64, :]
        kernel_out[3 * tap] = pair[:, :64]
        kernel_out[3 * tap + 1] = pair[:, 64:]
        last = rows[at + 64 : at + 96, :]
        kernel_out[3 * tap + 2, 0:32] = last[:, :64]
        kernel_out[3 * tap + 2, 32:64] = last[:, 64:]
    row = rows[864:865, :]
    head_out[...] = row[:, :64]
    bias_out[...] = row[:, 64:]


def shape(dims, dtype=F32):
    return jax.ShapeDtypeStruct(dims, dtype)


VMEM = pl.BlockSpec(memory_space=pltpu.VMEM)
ANY = pl.BlockSpec(memory_space=pl.ANY)
HBM = pl.BlockSpec(memory_space=pltpu.HBM)
SMEM = pl.BlockSpec(memory_space=pltpu.SMEM)


def call(kernel, out_shape, in_specs, scratch=(), megabytes=8):
    outs = out_shape if isinstance(out_shape, tuple) else (out_shape,)
    specs = tuple(HBM if hasattr(out, "memory_space") else VMEM for out in outs)
    return pl.pallas_call(
        kernel,
        out_shape=out_shape,
        in_specs=list(in_specs),
        out_specs=specs if isinstance(out_shape, tuple) else VMEM,
        scratch_shapes=list(scratch),
        compiler_params=pltpu.CompilerParams(vmem_limit_bytes=megabytes << 20),
    )


FIELD = pltpu.VMEM((18, 32, 128), F32)
pack = call(
    pack_kernel,
    (shape((27, 32, 128)), shape((27, 32, 128)), shape((3, 64, 64), BF16)),
    [HBM] * 6,
    [pltpu.SemaphoreType.DMA((11,))],
    4,
)
join = call(join_kernel, shape((9, 64, 64), BF16), [VMEM] * 3, (), 4)
widen = call(
    taps_kernel,
    (shape((576, 192), BF16), shape((64, 128)), shape((64, 128))),
    [HBM] + [VMEM] * 2,
    [pltpu.VMEM((27, 64, 64), BF16), pltpu.SemaphoreType.DMA],
    4,
)
decode = call(
    decode_kernel,
    (shape((16, 32, 128)), shape((3, 192, 640), BF16)),
    [VMEM] * 6,
    [
        pltpu.VMEM((9, 192, 384), BF16),
        pltpu.VMEM((9, 6, 64, 128), F32),
        pltpu.VMEM((32, 128), F32),
    ],
    14,
)
slopes = call(
    slopes_kernel,
    (shape((45, 64, 128)), shape((384, 1024), BF16)),
    [VMEM] + [HBM] * 4 + [ANY],
    [
        pltpu.VMEM((576, 192), BF16),
        pltpu.VMEM((64, 128), F32),
        pltpu.VMEM((64, 128), F32),
        pltpu.VMEM((27, 64, 64), BF16),
        pltpu.VMEM((5, 12, 64, 128), F32),
        pltpu.SemaphoreType.DMA((4,)),
    ],
    14,
)
medium = call(
    medium_kernel,
    (shape((30, 32, 128)), pltpu.HBM((4, 384, 128), F32)),
    [SMEM] + [HBM] * 7 + [ANY],
    [
        pltpu.VMEM((4, 384, 128), F32),
        pltpu.VMEM((1, 128), jnp.int32),
        pltpu.VMEM((3, 1, 128), F32),
        pltpu.SemaphoreType.DMA((8,)),
    ],
    8,
)
waves = call(
    wave_kernel,
    shape((16, 32, 128)),
    [SMEM] * 2 + [HBM] + [VMEM] * 4 + [HBM],
    [
        pltpu.VMEM((4, 384, 128), F32),
        pltpu.SMEM((1, 3), F32),
        pltpu.VMEM((6, 18, 32, 128), F32),
        FIELD,
        FIELD,
        FIELD,
        FIELD,
        FIELD,
        FIELD,
        pltpu.VMEM((3, 8, 32, 128), F32),
        FIELD,
        FIELD,
        pltpu.VMEM((8, 48, 128), F32),
        pltpu.SemaphoreType.DMA((2,)),
    ],
    14,
)
backward = call(
    backward_kernel,
    (shape((3, 1, 64, 64)), shape((1024, 128))),
    [VMEM] * 4,
    [
        pltpu.VMEM((8, 4, 64, 128), BF16),
        pltpu.VMEM((4, 64, 384), BF16),
        pltpu.VMEM((16, 64, 192), F32),
        pltpu.VMEM((32, 128), F32),
    ],
    14,
)


def in_hbm(x):
    return pltpu.with_memory_space_constraint(x, pltpu.HBM)


def shifted(block, axes, size):
    low = lax.ppermute(block[0], axes, [(i, i + 1) for i in range(size - 1)])
    high = lax.ppermute(block[1], axes, [(i + 1, i) for i in range(size - 1)])
    return low, high


def per_device(
    latent,
    kernel,
    conv_bias,
    head_weight,
    density,
    wave_prev,
    wave_now,
    adjoint_next,
    adjoint_after,
    source_cell,
    wavelet,
    receiver_cells,
    observed,
):
    place = lax.axis_index(TILE).astype(jnp.int32).reshape(1)
    fields = [in_hbm(f) for f in (wave_now, wave_prev, adjoint_next, adjoint_after, density)]
    taps = in_hbm(kernel)
    to_next, to_prev, coarse = pack(*fields, in_hbm(latent.reshape(3, 64, 64)))
    left, right = shifted((to_next, to_prev), TILE, 32)
    wall, bias, head = widen(taps, conv_bias.reshape(1, 64), head_weight.reshape(1, 64))
    nine = join(left, coarse, right)
    z_prev, z_next = shifted((nine, nine), SHOT, 16)

    speed, lines = decode(z_prev, nine, z_next, wall, bias, head)
    speeds = lax.all_to_all(speed, SHOT, 0, 0, tiled=True)
    records = jnp.transpose(observed, (1, 0, 2))
    own, counts = medium(place, *fields, in_hbm(receiver_cells), in_hbm(records), in_hbm(speed))
    strips = waves(
        place,
        source_cell,
        in_hbm(wavelet),
        left,
        right,
        speeds.reshape(512, 128),
        own,
        in_hbm(counts),
    )
    received = lax.all_to_all(strips, SHOT, 0, 0, tiled=True)
    slope, folded = slopes(lines, in_hbm(wall), in_hbm(bias), in_hbm(head), taps, in_hbm(strips))
    latent_grad, parts = backward(received, slope, lines, folded)

    chunks = lax.all_to_all(parts.reshape(8, 128, 128), NEAR, 0, 0, tiled=True)
    chunk = call(sum_kernel, shape((128, 128)), [VMEM])(chunks)
    pairs = lax.all_to_all(chunk.reshape(64, 2, 128), FAR, 0, 0, tiled=True)
    pairs = call(sum_pairs_kernel, shape((128, 128)), [VMEM])(pairs.reshape(128, 128))
    chunk = lax.all_to_all(pairs.reshape(64, 2, 128), FAR, 0, 0, tiled=True)
    chunks = call(repeat_kernel, shape((8, 128, 128)), [VMEM])(chunk.reshape(128, 128))
    whole = lax.all_to_all(chunks, NEAR, 0, 0, tiled=True)
    kernel_grad, head_grad, bias_grad = call(
        unpack_kernel, (shape((27, 64, 64)), shape((1, 64)), shape((1, 64))), [VMEM]
    )(whole.reshape(1024, 128))
    head_grad = head_grad.reshape(64)
    bias_grad = bias_grad.reshape(64)
    return latent_grad, kernel_grad, head_grad, bias_grad


def solution(mesh):
    fine_mesh = Mesh(mesh.devices.reshape(2, 8, 8, 2, 2), ("xlo", "z", "y", "xhi", "core"))
    return jax.shard_map(
        per_device,
        mesh=fine_mesh,
        in_specs=(
            P(TILE, SHOT, None, None),
            P(),
            P(),
            P(),
            P(TILE, None, None),
            P(SHOT, TILE, None, None),
            P(SHOT, TILE, None, None),
            P(SHOT, TILE, None, None),
            P(SHOT, TILE, None, None),
            P(SHOT),
            P(SHOT, None),
            P(SHOT, None),
            P(SHOT, None, None),
        ),
        out_specs=(P(TILE, SHOT, None, None), P(), P(), P()),
        check_vma=False,
    )
```

```python
import jax
import jax.numpy as jnp
from jax import lax
from jax.experimental import pallas as pl
from jax.experimental.pallas import tpu as pltpu
from jax.sharding import Mesh
from jax.sharding import PartitionSpec as P

SHOT = ("xlo", "z")
TILE = ("y", "xhi", "core")
NEAR = ("xlo", "z", "xhi", "core")
F32 = jnp.float32
BF16 = jnp.bfloat16
courant = 0.005
speed_low = 1.5
speed_span = 3.0
NT = (((1,), (1,)), ((), ()))


def sigmoid(v):
    return 1.0 / (1.0 + jnp.exp(-v))


def split(v, parts):
    out = []
    for _ in range(parts):
        piece = v.astype(BF16)
        out.append(piece)
        v = v - piece.astype(F32)
    return out


def spread_matrix():
    coarse = lax.broadcasted_iota(jnp.int32, (64, 384), 0)
    lane = lax.broadcasted_iota(jnp.int32, (64, 384), 1)
    fine = (lane & 127) + (lane >> 7) - 1
    return jnp.where((fine >> 1) == coarse, 1.0, 0.0).astype(BF16)


Z_LINE = ((0, 0, 1), (0, 1, 1), (1, 1, 2), (1, 2, 2))


def start_all(copies):
    for copy in copies:
        copy.start()
    return copies


def wait_all(copies):
    for copy in copies:
        copy.wait()


def pack_kernel(
    wave_now, wave_prev, adj_next, adj_after, density, latent, to_next, to_prev, coarse, sems
):
    copies = [pltpu.make_async_copy(latent, coarse, sems.at[10])]
    fields = ((wave_now, 6), (wave_prev, 5), (adj_next, 4), (adj_after, 3), (density, 6))
    at = 0
    for i, (ref, rows) in enumerate(fields):
        field = ref if i == 4 else ref.at[0]
        here = pl.ds(at, rows)
        copies.append(pltpu.make_async_copy(field.at[pl.ds(6 - rows, rows)], to_next.at[here], sems.at[i]))
        copies.append(pltpu.make_async_copy(field.at[pl.ds(0, rows)], to_prev.at[here], sems.at[5 + i]))
        at += rows
    wait_all(start_all(copies))


def join_kernel(low, middle, high, out):
    for i, ref in enumerate((low, middle, high)):
        for x in range(3):
            out[3 * i + x] = jnp.concatenate([ref[x, 0:32], ref[x, 32:64]], axis=1)


def taps_kernel(kernel_in, bias, head, wall, bias_wide, head_wide, kernel, sem):
    copy = pltpu.make_async_copy(kernel_in, kernel, sem)
    copy.start()
    bias_wide[...] = jnp.broadcast_to(bias[...], (128, 64)).T
    head_wide[...] = jnp.broadcast_to(head[...].astype(F32), (128, 64)).T
    copy.wait()
    for j in range(9):
        wall[64 * j : 64 * j + 64, :] = jnp.concatenate([kernel[3 * j + e] for e in range(3)], axis=1)


def fold_taps(kernel, folded):
    reach = ((2,), (1, 2), (0, 1), (0,))
    for i in range(4):
        for j in range(0, 4, 2):
            blocks = []
            for jj in (j, j + 1):
                row = []
                for e in range(3):
                    total = None
                    for a in reach[i]:
                        for b in reach[jj]:
                            term = kernel[9 * a + 3 * b + e].astype(F32)
                            total = term if total is None else total + term
                    row.append(total)
                blocks.append(jnp.concatenate(row, axis=1))
            table = jnp.concatenate(blocks, axis=0).T
            high, low = split(table, 2)
            at = 64 * (4 * i + j)
            folded[0:192, at : at + 128] = high
            folded[192:384, at : at + 128] = low


def z_sums(product, rows, store):
    for a in range(3):
        for zz in rows:
            total = None
            for b in range(3):
                zi = Z_LINE[zz][b]
                term = product[64 * (3 * a + b) : 64 * (3 * a + b) + 64, 128 * zi : 128 * zi + 128]
                total = term if total is None else total + term
            store(a, zz, total)


def decode_kernel(
    z_prev, own, z_next, wall, bias, head, speed_out, lines_out, lines, sums, row_logit
):
    spread = spread_matrix()
    for zi, ref in enumerate((z_prev, own, z_next)):
        packed = [ref[x] for x in range(9)]
        rows = jnp.concatenate([half for p in packed for half in (p[:, :64], p[:, 64:])], axis=0)
        fine = jnp.dot(rows, spread, preferred_element_type=F32).astype(BF16)
        for x in range(9):
            for e in range(3):
                piece = fine[64 * x : 64 * x + 64, 128 * e : 128 * e + 128]
                lines[x, 64 * e : 64 * e + 64, 128 * zi : 128 * zi + 128] = piece
                if 2 <= x <= 6:
                    lines_out[zi, 64 * e : 64 * e + 64, 128 * (x - 2) : 128 * (x - 1)] = piece

    def products(x, carry):
        product = jnp.dot(wall[...], lines[x], preferred_element_type=F32)

        def store(a, zz, total):
            sums[x, 2 * a + zz - 1] = total

        z_sums(product, (1, 2), store)
        return carry

    lax.fori_loop(0, 9, products, 0, unroll=3)

    def rows(k, carry):
        r = k + 1
        for j in range(2):
            pre = sums[(r - 1) // 2, j] + sums[r // 2, 2 + j] + sums[(r + 1) // 2, 4 + j] + bias[...]
            hidden = (pre * sigmoid(pre)).astype(BF16).astype(F32)
            row_logit[pl.ds(2 * k + j, 1), :] = jnp.sum(hidden * head[...], axis=0, keepdims=True)
        return carry

    lax.fori_loop(0, 16, rows, 0, unroll=2)
    speed = speed_low + speed_span * sigmoid(row_logit[...])
    for s in range(16):
        speed_out[s] = speed


def slopes_kernel(
    lines, wall_in, bias_in, head_in, kernel_in, after, slope_out, folded, wall, bias, head, kernel, sums, sems
):
    copies = start_all(
        [
            pltpu.make_async_copy(source, target, sems.at[i])
            for i, (source, target) in enumerate(
                ((wall_in, wall), (bias_in, bias), (head_in, head), (kernel_in, kernel))
            )
        ]
    )
    wait_all(copies)
    for x in range(5):
        columns = [lines[zi, :, 128 * x : 128 * x + 128] for zi in range(3)]
        product = jnp.dot(wall[...], jnp.concatenate(columns, axis=1), preferred_element_type=F32)

        def store(a, zz, total):
            sums[x, 4 * a + zz] = total

        z_sums(product, range(4), store)

    def rows(k, owned):
        r = k + 1
        for zz in range(4):
            pre = sums[(r - 1) // 2, zz] + sums[r // 2, 4 + zz] + sums[(r + 1) // 2, 8 + zz] + bias[...]
            gate = sigmoid(pre)
            hidden = (pre * gate).astype(BF16).astype(F32)
            slope_out[4 * k + zz] = head[...] * (gate * (1.0 + pre * (1.0 - gate)))
            if owned and zz in (1, 2):
                slope_out[30 + 2 * k + zz - 1] = hidden
            logit = jnp.sum(hidden * head[...], axis=0, keepdims=True)
            slope_out[44, pl.ds(4 * k + zz, 1), :] = logit
        return owned

    rows(0, False)
    lax.fori_loop(1, 7, lambda k, carry: rows(k, True), True)
    rows(7, False)
    slope_out[44, 0:32, :] = sigmoid(slope_out[44, 0:32, :])
    slope_out[44, 32:64, :] = jnp.zeros((32, 128), F32)
    fold_taps(kernel, folded)


def shifts(f):
    z_at = lax.broadcasted_iota(jnp.int32, (32, 128), 0)
    y_at = lax.broadcasted_iota(jnp.int32, (32, 128), 1)
    return (
        jnp.where(z_at < 31, pltpu.roll(f, 31, 0), 0.0),
        jnp.where(z_at > 0, pltpu.roll(f, 1, 0), 0.0),
        jnp.where(y_at < 127, pltpu.roll(f, 127, 1), 0.0),
        jnp.where(y_at > 0, pltpu.roll(f, 1, 1), 0.0),
    )


def windowed(left, own, right, field, offset, first):
    def get(w):
        if w < 6:
            return left[offset + w - first]
        if w < 12:
            return own[6 * field + w - 6]
        return right[offset + w - 12]

    return get


def medium_kernel(
    place,
    wave_now,
    wave_prev,
    adj_next,
    adj_after,
    density,
    receivers_in,
    observed_in,
    after,
    left,
    right,
    own,
    counts_out,
    counts,
    receivers,
    observed,
    sems,
):
    fields = (wave_now.at[0], wave_prev.at[0], adj_next.at[0], adj_after.at[0], density)
    wait_all(
        start_all(
            [pltpu.make_async_copy(f, own.at[pl.ds(6 * i, 6)], sems.at[i]) for i, f in enumerate(fields)]
            + [
                pltpu.make_async_copy(receivers_in, receivers, sems.at[5]),
                pltpu.make_async_copy(observed_in, observed, sems.at[6]),
            ]
        )
    )
    local = receivers[...] - (place[0] * 6 - 3) * 4096
    at_row = lax.broadcasted_iota(jnp.int32, (384, 128), 0) == (local >> 7)
    at_y = lax.broadcasted_iota(jnp.int32, (128, 128), 0) == (local & 127)
    picks = [jnp.where(at_y, 1.0, 0.0).astype(BF16)]
    for n in range(3):
        for piece in split(observed[n], 3):
            picks.append(jnp.where(at_y, piece.astype(F32), 0.0).astype(BF16))
    maps = lax.dot_general(
        jnp.where(at_row, 1.0, 0.0).astype(BF16),
        jnp.concatenate(picks, axis=0),
        NT,
        preferred_element_type=F32,
    )
    counts[0] = maps[:, 0:128]
    for n in range(3):
        at = 128 + 384 * n
        counts[1 + n] = maps[:, at : at + 128] + maps[:, at + 128 : at + 256] + maps[:, at + 256 : at + 384]
    wait_all(start_all([pltpu.make_async_copy(counts, counts_out, sems.at[7])]))


def wave_kernel(
    place,
    source,
    pulses_in,
    left,
    right,
    speeds,
    own,
    counts_in,
    send_out,
    counts,
    pulses,
    faces,
    buoy,
    coef,
    speed,
    u2,
    u3,
    u4,
    laps,
    lam4,
    lam3,
    grads,
    sems,
):
    copies = start_all(
        [
            pltpu.make_async_copy(pulses_in, pulses, sems.at[0]),
            pltpu.make_async_copy(counts_in, counts, sems.at[1]),
        ]
    )
    send = send_out.reshape(512, 128)
    u1 = windowed(left, own, right, 0, 0, 0)
    u0 = windowed(left, own, right, 1, 6, 1)
    lam5 = windowed(left, own, right, 2, 11, 2)
    lam6 = windowed(left, own, right, 3, 15, 3)
    dens = windowed(left, own, right, 4, 18, 0)
    cell = lax.broadcasted_iota(jnp.int32, (32, 128), 0) * 128 + lax.broadcasted_iota(
        jnp.int32, (32, 128), 1
    )

    for w in range(1, 17):
        for j in range(2):
            speed[w, pl.ds(j, 16, 2), :] = speeds[pl.ds(2 * (w - 1) + j, 16, 32), :]
    grads[...] = jnp.zeros_like(grads)
    for w in range(18):
        d = dens(w)
        buoy[w] = jnp.where(d > 0.0, 1.0 / d, 0.0)
    for w in range(1, 17):
        v = speed[w]
        coef[w] = courant * v * v * dens(w)
        centre = buoy[w]
        inside = jnp.where(centre > 0.0, 0.5, 0.0)
        for i, beside in enumerate((buoy[w + 1], buoy[w - 1]) + shifts(centre)):
            faces[i, w] = inside * (centre + beside)
    copies[0].wait()

    def laplace(f, w):
        centre = f(w)
        total = None
        for i, beside in enumerate((f(w + 1), f(w - 1)) + shifts(centre)):
            term = faces[i, w] * (beside - centre)
            total = term if total is None else total + term
        return total

    source_cell = source[0] - (place[0] * 6 - 6) * 4096

    def forward(f, before, n, rows, out):
        for w in rows:
            lap = laplace(f, w)
            if 5 <= w <= 12:
                laps[n, w - 5] = lap
            pulse = jnp.where(cell == source_cell - w * 4096, pulses[0, n], 0.0)
            out[w] = 2.0 * f(w) - before(w) + coef[w] * lap + pulse

    def row_of(ref):
        return lambda w: ref[w]

    forward(u1, u0, 0, range(1, 17), u2)
    forward(row_of(u2), u1, 1, range(2, 16), u3)
    forward(row_of(u3), row_of(u2), 2, range(3, 15), u4)

    def residual(u, n, w):
        at = slice(32 * (w - 3), 32 * (w - 2))
        return counts[0, at, :] * u[w] - counts[1 + n, at, :]

    def backward(f, before, u, n, rows, out):
        for w in rows:
            lap = laplace(lambda v: coef[v] * f(v), w)
            out[w] = 2.0 * f(w) - before(w) + lap + residual(u, n, w)

    copies[1].wait()
    backward(lam5, lam6, u4, 2, range(3, 15), lam4)
    backward(row_of(lam4), lam5, u3, 1, range(4, 14), lam3)
    for w in range(5, 13):
        lap4 = laplace(row_of(u4), w)
        lap = laplace(lambda v: coef[v] * lam3[v], w)
        lam2 = 2.0 * lam3[w] - lam4[w] + lap + residual(u2, 0, w)
        total = lam5(w) * lap4 + lam4[w] * laps[2, w - 5] + lam3[w] * laps[1, w - 5] + lam2 * laps[0, w - 5]
        grads[w - 5, 8:40, :] = total * (2.0 * courant * speed[w] * dens(w))
    for x in range(8):
        for zz in range(4):
            send[pl.ds(4 * x + zz, 16, 32), :] = grads[x, pl.ds(7 + zz, 16, 2), :]


def backward_kernel(
    received, slopes, lines, folded, latent_out, parts_out, low, low_wide, terms, logit_grads
):
    total = received[0]
    for s in range(1, 16):
        total = total + received[s]
    squash = slopes[44, 0:32, :]
    logit_grads[...] = total * speed_span * squash * (1.0 - squash)
    head_sum = jnp.zeros((64, 128), F32)
    bias_sum = jnp.zeros((64, 128), F32)
    for x in range(8):
        for zz in range(4):
            grad = logit_grads[4 * x + zz : 4 * x + zz + 1, :]
            pre_grad = grad * slopes[4 * x + zz]
            rounded = pre_grad.astype(BF16)
            low[x, zz] = rounded
            if 1 <= x <= 6 and 1 <= zz <= 2:
                px = (x - 1) % 2
                low_wide[2 * px + zz - 1, :, 64 * (x - 1 - px) : 64 * (x + 1 - px)] = rounded
                head_sum = head_sum + slopes[30 + 2 * x + zz - 1] * grad
                bias_sum = bias_sum + pre_grad

    ones = jnp.ones((8, 128), BF16)
    row = None
    for piece in split(jnp.concatenate([head_sum, bias_sum], axis=0), 3):
        term = lax.dot_general(ones, piece, NT, preferred_element_type=F32)
        row = term if row is None else row + term
    parts_out[864:872, :] = row
    parts_out[872:1024, :] = jnp.zeros((152, 128), F32)

    parities = {-1: (0,), 0: (0, 1), 1: (1,)}
    found = {}
    for dx in (-1, 0, 1):
        for dz in (-1, 0, 1):
            combos = [(px, pz) for px in parities[dx] for pz in parities[dz]]
            if len(combos) == 2 and dx == 0:
                grads = jnp.concatenate([low_wide[2 * px + pz] for px, pz in combos], axis=0)
            else:
                first = 2 * combos[0][0] + combos[0][1]
                grads = low_wide[first : first + len(combos)].reshape(64 * len(combos), 384)
            beside = lines[1 + dz, :, 128 * (1 + dx) : 128 * (4 + dx)]
            product = lax.dot_general(grads, beside, NT, preferred_element_type=F32)
            for i, (px, pz) in enumerate(combos):
                found[dx, px, dz, pz] = at = len(found)
                terms[at] = product[64 * i : 64 * i + 64]
    pairs = {-1: ((-1, 0), (0, 1)), 0: ((0, 0), (0, 1)), 1: ((0, 0), (1, 1))}
    for a in (-1, 0, 1):
        for b in (-1, 0, 1):
            tap = None
            for dx, px in pairs[a]:
                for dz, pz in pairs[b]:
                    term = terms[found[dx, px, dz, pz]]
                    tap = term if tap is None else tap + term
            at = 96 * (3 * (a + 1) + b + 1)
            parts_out[at : at + 64, :] = tap[:, :128]
            parts_out[at + 64 : at + 96, :] = jnp.concatenate([tap[:32, 128:], tap[32:, 128:]], axis=1)

    stacked = []
    for x in range(3):
        around = low[2 * x : 2 * x + 4].reshape(1024, 128)
        product = jnp.dot(folded[...], around, preferred_element_type=F32)
        both = product[:192] + product[192:]
        stacked.append(jnp.concatenate([both[64 * e : 64 * e + 64] for e in range(3)], axis=1))
    stacked = jnp.concatenate(stacked, axis=0)
    spread = spread_matrix()
    result = None
    for piece in split(stacked, 2):
        term = lax.dot_general(piece, spread, NT, preferred_element_type=F32)
        result = term if result is None else result + term
    for x in range(3):
        latent_out[x, 0] = result[64 * x : 64 * x + 64]


def sum_kernel(received, out):
    total = received[0]
    for s in range(1, received.shape[0]):
        total = total + received[s]
    total = total.astype(out.dtype)
    for s in range(out.shape[0]):
        out[s] = total


def unpack_kernel(rows, kernel_out, head_out, bias_out):
    for tap in range(9):
        at = 96 * tap
        pair = rows[at : at + 64, :].astype(F32)
        kernel_out[3 * tap] = pair[:, :64]
        kernel_out[3 * tap + 1] = pair[:, 64:]
        last = rows[at + 64 : at + 96, :].astype(F32)
        kernel_out[3 * tap + 2, 0:32] = last[:, :64]
        kernel_out[3 * tap + 2, 32:64] = last[:, 64:]
    row = rows[864:880, :].astype(F32)[0:1]
    head_out[...] = row[:, :64]
    bias_out[...] = row[:, 64:]


def shape(dims, dtype=F32):
    return jax.ShapeDtypeStruct(dims, dtype)


VMEM = pl.BlockSpec(memory_space=pltpu.VMEM)
ANY = pl.BlockSpec(memory_space=pl.ANY)
HBM = pl.BlockSpec(memory_space=pltpu.HBM)
SMEM = pl.BlockSpec(memory_space=pltpu.SMEM)


def call(kernel, out_shape, in_specs, scratch=(), megabytes=8, flops=None):
    outs = out_shape if isinstance(out_shape, tuple) else (out_shape,)
    specs = tuple(HBM if hasattr(out, "memory_space") else VMEM for out in outs)
    return pl.pallas_call(
        kernel,
        out_shape=out_shape,
        in_specs=list(in_specs),
        out_specs=specs if isinstance(out_shape, tuple) else VMEM,
        scratch_shapes=list(scratch),
        compiler_params=pltpu.CompilerParams(vmem_limit_bytes=megabytes << 20),
        cost_estimate=flops and pl.CostEstimate(flops=flops, bytes_accessed=0, transcendentals=0),
    )


FIELD = pltpu.VMEM((18, 32, 128), F32)
pack = call(
    pack_kernel,
    (shape((24, 32, 128)), shape((24, 32, 128)), shape((3, 64, 64), BF16)),
    [HBM] * 6,
    [pltpu.SemaphoreType.DMA((11,))],
    4,
)
join = call(join_kernel, shape((9, 32, 128), BF16), [VMEM] * 3, (), 2)
widen = call(
    taps_kernel,
    (shape((576, 192), BF16), shape((64, 128)), shape((64, 128))),
    [HBM] + [VMEM] * 2,
    [pltpu.VMEM((27, 64, 64), BF16), pltpu.SemaphoreType.DMA],
    4,
)
decode = call(
    decode_kernel,
    (shape((16, 32, 128)), shape((3, 192, 640), BF16)),
    [VMEM] * 6,
    [
        pltpu.VMEM((9, 192, 384), BF16),
        pltpu.VMEM((9, 6, 64, 128), F32),
        pltpu.VMEM((32, 128), F32),
    ],
    14,
    500_000_000,
)
slopes = call(
    slopes_kernel,
    (shape((45, 64, 128)), shape((384, 1024), BF16)),
    [VMEM] + [HBM] * 4 + [ANY],
    [
        pltpu.VMEM((576, 192), BF16),
        pltpu.VMEM((64, 128), F32),
        pltpu.VMEM((64, 128), F32),
        pltpu.VMEM((27, 64, 64), BF16),
        pltpu.VMEM((5, 12, 64, 128), F32),
        pltpu.SemaphoreType.DMA((4,)),
    ],
    14,
)
medium = call(
    medium_kernel,
    (shape((30, 32, 128)), pltpu.HBM((4, 384, 128), F32)),
    [SMEM] + [HBM] * 7 + [ANY] * 3,
    [
        pltpu.VMEM((4, 384, 128), F32),
        pltpu.VMEM((1, 128), jnp.int32),
        pltpu.VMEM((3, 1, 128), F32),
        pltpu.SemaphoreType.DMA((8,)),
    ],
    8,
    2_000_000_000,
)
waves = call(
    wave_kernel,
    shape((16, 32, 128)),
    [SMEM] * 2 + [HBM] + [VMEM] * 4 + [HBM],
    [
        pltpu.VMEM((4, 384, 128), F32),
        pltpu.SMEM((1, 3), F32),
        pltpu.VMEM((6, 18, 32, 128), F32),
        FIELD,
        FIELD,
        FIELD,
        FIELD,
        FIELD,
        FIELD,
        pltpu.VMEM((3, 8, 32, 128), F32),
        FIELD,
        FIELD,
        pltpu.VMEM((8, 48, 128), F32),
        pltpu.SemaphoreType.DMA((2,)),
    ],
    14,
)
backward = call(
    backward_kernel,
    (shape((3, 1, 64, 64)), shape((1024, 128))),
    [VMEM] * 4,
    [
        pltpu.VMEM((8, 4, 64, 128), BF16),
        pltpu.VMEM((4, 64, 384), BF16),
        pltpu.VMEM((16, 64, 192), F32),
        pltpu.VMEM((32, 128), F32),
    ],
    14,
)


def in_hbm(x):
    return pltpu.with_memory_space_constraint(x, pltpu.HBM)


def shifted(block, axes, size):
    low = lax.ppermute(block[0], axes, [(i, i + 1) for i in range(size - 1)])
    high = lax.ppermute(block[1], axes, [(i + 1, i) for i in range(size - 1)])
    return low, high


def per_device(
    latent,
    kernel,
    conv_bias,
    head_weight,
    density,
    wave_prev,
    wave_now,
    adjoint_next,
    adjoint_after,
    source_cell,
    wavelet,
    receiver_cells,
    observed,
):
    place = lax.axis_index(TILE).astype(jnp.int32).reshape(1)
    fields = [in_hbm(f) for f in (wave_now, wave_prev, adjoint_next, adjoint_after, density)]
    taps = in_hbm(kernel)
    coarse = latent.reshape(3, 64, 64)
    low, high = shifted((coarse, coarse), TILE, 32)
    to_next, to_prev, middle = pack(*fields, in_hbm(coarse))
    wall, bias, head = widen(taps, conv_bias.reshape(1, 64), head_weight.reshape(1, 64))
    nine = join(low, middle, high)
    z_prev, z_next = shifted((nine, nine), SHOT, 16)
    to_next, to_prev, nine = lax.optimization_barrier((to_next, to_prev, nine))
    left, right = shifted((to_next, to_prev), TILE, 32)

    speed, lines = decode(z_prev, nine, z_next, wall, bias, head)
    speeds = lax.all_to_all(speed, SHOT, 0, 0, tiled=True)
    records = jnp.transpose(observed, (1, 0, 2))
    own, counts = medium(
        place, *fields, in_hbm(receiver_cells), in_hbm(records), in_hbm(speed), left, right
    )
    strips = waves(
        place,
        source_cell,
        in_hbm(wavelet),
        left,
        right,
        speeds.reshape(512, 128),
        own,
        in_hbm(counts),
    )
    received = lax.all_to_all(strips, SHOT, 0, 0, tiled=True)
    slope, folded = slopes(lines, in_hbm(wall), in_hbm(bias), in_hbm(head), taps, in_hbm(strips))
    latent_grad, parts = backward(received, slope, lines, folded)

    pieces = lax.all_to_all(parts.reshape(64, 16, 128), NEAR, 0, 0, tiled=True)
    pieces = call(sum_kernel, shape((8, 16, 128)), [VMEM])(pieces)
    pieces = lax.all_to_all(pieces, "y", 0, 0, tiled=True)
    pieces = call(sum_kernel, shape((64, 16, 128), BF16), [VMEM])(pieces)
    whole = lax.all_to_all(pieces, NEAR, 0, 0, tiled=True)
    kernel_grad, head_grad, bias_grad = call(
        unpack_kernel, (shape((27, 64, 64)), shape((1, 64)), shape((1, 64))), [VMEM]
    )(whole.reshape(1024, 128))
    head_grad = head_grad.reshape(64)
    bias_grad = bias_grad.reshape(64)
    return latent_grad, kernel_grad, head_grad, bias_grad


def solution(mesh):
    fine_mesh = Mesh(mesh.devices.reshape(2, 8, 8, 2, 2), ("xlo", "z", "y", "xhi", "core"))
    return jax.shard_map(
        per_device,
        mesh=fine_mesh,
        in_specs=(
            P(TILE, SHOT, None, None),
            P(),
            P(),
            P(),
            P(TILE, None, None),
            P(SHOT, TILE, None, None),
            P(SHOT, TILE, None, None),
            P(SHOT, TILE, None, None),
            P(SHOT, TILE, None, None),
            P(SHOT),
            P(SHOT, None),
            P(SHOT, None),
            P(SHOT, None, None),
        ),
        out_specs=(P(TILE, SHOT, None, None), P(), P(), P()),
        check_vma=False,
    )
```

```python
import jax
import jax.numpy as jnp
from jax import lax
from jax.experimental import pallas as pl
from jax.experimental.pallas import tpu as pltpu
from jax.sharding import Mesh
from jax.sharding import PartitionSpec as P

SHOT = ("xlo", "z")
TILE = ("y", "xhi", "core")
NEAR = ("xlo", "z", "xhi", "core")
F32 = jnp.float32
BF16 = jnp.bfloat16
courant = 0.005
speed_low = 1.5
speed_span = 3.0
NT = (((1,), (1,)), ((), ()))


def sigmoid(v):
    return 1.0 / (1.0 + jnp.exp(-v))


def split(v, parts):
    out = []
    for _ in range(parts):
        piece = v.astype(BF16)
        out.append(piece)
        v = v - piece.astype(F32)
    return out


def spread_matrix():
    coarse = lax.broadcasted_iota(jnp.int32, (64, 384), 0)
    lane = lax.broadcasted_iota(jnp.int32, (64, 384), 1)
    fine = (lane & 127) + (lane >> 7) - 1
    return jnp.where((fine >> 1) == coarse, 1.0, 0.0).astype(BF16)


Z_LINE = ((0, 0, 1), (0, 1, 1), (1, 1, 2), (1, 2, 2))


def start_all(copies):
    for copy in copies:
        copy.start()
    return copies


def wait_all(copies):
    for copy in copies:
        copy.wait()


def pack_kernel(
    wave_now,
    wave_prev,
    adj_next,
    adj_after,
    density,
    latent,
    kernel_in,
    bias,
    head,
    to_next,
    to_prev,
    coarse,
    wall,
    bias_wide,
    head_wide,
    kernel,
    sems,
):
    copies = [
        pltpu.make_async_copy(kernel_in, kernel, sems.at[11]),
        pltpu.make_async_copy(latent, coarse, sems.at[10]),
    ]
    fields = ((wave_now, 6), (wave_prev, 5), (adj_next, 4), (adj_after, 3), (density, 6))
    at = 0
    for i, (ref, rows) in enumerate(fields):
        field = ref if i == 4 else ref.at[0]
        here = pl.ds(at, rows)
        copies.append(pltpu.make_async_copy(field.at[pl.ds(6 - rows, rows)], to_next.at[here], sems.at[i]))
        copies.append(pltpu.make_async_copy(field.at[pl.ds(0, rows)], to_prev.at[here], sems.at[5 + i]))
        at += rows
    start_all(copies)
    bias_wide[...] = jnp.broadcast_to(bias[...], (128, 64)).T
    head_wide[...] = jnp.broadcast_to(head[...].astype(F32), (128, 64)).T
    copies[0].wait()
    for a in range(3):
        for b in range(3):
            at = 64 * (3 * b + a)
            taps = [kernel[9 * a + 3 * b + e] for e in range(3)]
            wall[at : at + 64, :] = jnp.concatenate(taps, axis=1)
    wait_all(copies[1:])


def join_kernel(low, middle, high, out):
    for i, ref in enumerate((low, middle, high)):
        for x in range(3):
            out[3 * i + x] = jnp.concatenate([ref[x, 0:32], ref[x, 32:64]], axis=1)


def fold_taps(kernel, folded):
    reach = ((2,), (1, 2), (0, 1), (0,))
    for i in range(4):
        for j in range(0, 4, 2):
            blocks = []
            for jj in (j, j + 1):
                row = []
                for e in range(3):
                    total = None
                    for a in reach[i]:
                        for b in reach[jj]:
                            term = kernel[9 * a + 3 * b + e].astype(F32)
                            total = term if total is None else total + term
                    row.append(total)
                blocks.append(jnp.concatenate(row, axis=1))
            table = jnp.concatenate(blocks, axis=0).T
            high, low = split(table, 2)
            at = 64 * (4 * i + j)
            folded[0:192, at : at + 128] = high
            folded[192:384, at : at + 128] = low


def z_sums(product, rows, store):
    for a in range(3):
        for zz in rows:
            total = None
            for b in range(3):
                zi = Z_LINE[zz][b]
                term = product[64 * (3 * b + a) : 64 * (3 * b + a) + 64, 128 * zi : 128 * zi + 128]
                total = term if total is None else total + term
            store(a, zz, total)


def decode_kernel(z_prev, own, z_next, wall, bias, head, speed_out, lines_out, lines, sums, row_logit):
    spread = spread_matrix()
    for zi, ref in enumerate((z_prev, own, z_next)):
        packed = [ref[x] for x in range(9)]
        rows = jnp.concatenate([half for p in packed for half in (p[:, :64], p[:, 64:])], axis=0)
        fine = jnp.dot(rows, spread, preferred_element_type=F32).astype(BF16)
        for x in range(9):
            for e in range(3):
                piece = fine[64 * x : 64 * x + 64, 128 * e : 128 * e + 128]
                lines[zi, 64 * e : 64 * e + 64, 128 * x : 128 * x + 128] = piece
                if 2 <= x <= 6:
                    lines_out[zi, 64 * e : 64 * e + 64, 128 * (x - 2) : 128 * (x - 1)] = piece

    for first, count in ((0, 2), (2, 2), (4, 2), (6, 3)):
        at = slice(128 * first, 128 * (first + count))
        before = jnp.dot(wall[0:192, :], lines[0, :, at], preferred_element_type=F32)
        middle = jnp.dot(wall[...], lines[1, :, at], preferred_element_type=F32)
        after = jnp.dot(wall[384:576, :], lines[2, :, at], preferred_element_type=F32)
        for i in range(count):
            col = slice(128 * i, 128 * i + 128)
            for a in range(3):
                low, centre, high = [middle[64 * (3 * b + a) : 64 * (3 * b + a) + 64, col] for b in range(3)]
                block = slice(64 * a, 64 * a + 64)
                sums[first + i, 2 * a] = before[block, col] + (centre + high)
                sums[first + i, 2 * a + 1] = (low + centre) + after[block, col]

    def rows(k, carry):
        r = k + 1
        for j in range(2):
            pre = sums[(r - 1) // 2, j] + sums[r // 2, 2 + j] + sums[(r + 1) // 2, 4 + j] + bias[...]
            hidden = (pre * sigmoid(pre)).astype(BF16).astype(F32)
            row_logit[pl.ds(2 * k + j, 1), :] = jnp.sum(hidden * head[...], axis=0, keepdims=True)
        return carry

    lax.fori_loop(0, 16, rows, 0, unroll=2)
    speed = speed_low + speed_span * sigmoid(row_logit[...])
    for s in range(16):
        speed_out[s] = speed


def slopes_kernel(
    lines, wall_in, bias_in, head_in, kernel_in, after, slope_out, folded, wall, bias, head, kernel, sums, sems
):
    copies = start_all(
        [
            pltpu.make_async_copy(source, target, sems.at[i])
            for i, (source, target) in enumerate(
                ((wall_in, wall), (bias_in, bias), (head_in, head), (kernel_in, kernel))
            )
        ]
    )
    wait_all(copies)
    for x in range(5):
        columns = [lines[zi, :, 128 * x : 128 * x + 128] for zi in range(3)]
        product = jnp.dot(wall[...], jnp.concatenate(columns, axis=1), preferred_element_type=F32)

        def store(a, zz, total):
            sums[x, 4 * a + zz] = total

        z_sums(product, range(4), store)

    def rows(k, owned):
        r = k + 1
        for zz in range(4):
            pre = sums[(r - 1) // 2, zz] + sums[r // 2, 4 + zz] + sums[(r + 1) // 2, 8 + zz] + bias[...]
            gate = sigmoid(pre)
            hidden = (pre * gate).astype(BF16).astype(F32)
            slope_out[4 * k + zz] = head[...] * (gate * (1.0 + pre * (1.0 - gate)))
            if owned and zz in (1, 2):
                slope_out[30 + 2 * k + zz - 1] = hidden
            logit = jnp.sum(hidden * head[...], axis=0, keepdims=True)
            slope_out[44, pl.ds(4 * k + zz, 1), :] = logit
        return owned

    rows(0, False)
    lax.fori_loop(1, 7, lambda k, carry: rows(k, True), True)
    rows(7, False)
    slope_out[44, 0:32, :] = sigmoid(slope_out[44, 0:32, :])
    slope_out[44, 32:64, :] = jnp.zeros((32, 128), F32)
    fold_taps(kernel, folded)


def shifts(f):
    z_at = lax.broadcasted_iota(jnp.int32, (32, 128), 0)
    y_at = lax.broadcasted_iota(jnp.int32, (32, 128), 1)
    return (
        jnp.where(z_at < 31, pltpu.roll(f, 31, 0), 0.0),
        jnp.where(z_at > 0, pltpu.roll(f, 1, 0), 0.0),
        jnp.where(y_at < 127, pltpu.roll(f, 127, 1), 0.0),
        jnp.where(y_at > 0, pltpu.roll(f, 1, 1), 0.0),
    )


def windowed(left, own, right, field, offset, first):
    def get(w):
        if w < 6:
            return left[offset + w - first]
        if w < 12:
            return own[6 * field + w - 6]
        return right[offset + w - 12]

    return get


def medium_kernel(
    place,
    wave_now,
    wave_prev,
    adj_next,
    adj_after,
    density,
    receivers_in,
    observed_in,
    after,
    left,
    right,
    own,
    counts_out,
    counts,
    receivers,
    observed,
    sems,
):
    fields = (wave_now.at[0], wave_prev.at[0], adj_next.at[0], adj_after.at[0], density)
    wait_all(
        start_all(
            [pltpu.make_async_copy(f, own.at[pl.ds(6 * i, 6)], sems.at[i]) for i, f in enumerate(fields)]
            + [
                pltpu.make_async_copy(receivers_in, receivers, sems.at[5]),
                pltpu.make_async_copy(observed_in, observed, sems.at[6]),
            ]
        )
    )
    local = receivers[...] - (place[0] * 6 - 3) * 4096
    at_row = lax.broadcasted_iota(jnp.int32, (384, 128), 0) == (local >> 7)
    at_y = lax.broadcasted_iota(jnp.int32, (128, 128), 0) == (local & 127)
    picks = [jnp.where(at_y, 1.0, 0.0).astype(BF16)]
    for n in range(3):
        for piece in split(observed[n], 3):
            picks.append(jnp.where(at_y, piece.astype(F32), 0.0).astype(BF16))
    maps = lax.dot_general(
        jnp.where(at_row, 1.0, 0.0).astype(BF16),
        jnp.concatenate(picks, axis=0),
        NT,
        preferred_element_type=F32,
    )
    counts[0] = maps[:, 0:128]
    for n in range(3):
        at = 128 + 384 * n
        counts[1 + n] = maps[:, at : at + 128] + maps[:, at + 128 : at + 256] + maps[:, at + 256 : at + 384]
    wait_all(start_all([pltpu.make_async_copy(counts, counts_out, sems.at[7])]))


def wave_kernel(
    place,
    source,
    pulses_in,
    left,
    right,
    speeds,
    own,
    counts_in,
    send_out,
    counts,
    pulses,
    faces,
    buoy,
    coef,
    speed,
    u2,
    u3,
    u4,
    laps,
    lam4,
    lam3,
    grads,
    sems,
):
    copies = start_all(
        [
            pltpu.make_async_copy(pulses_in, pulses, sems.at[0]),
            pltpu.make_async_copy(counts_in, counts, sems.at[1]),
        ]
    )
    send = send_out.reshape(512, 128)
    u1 = windowed(left, own, right, 0, 0, 0)
    u0 = windowed(left, own, right, 1, 6, 1)
    lam5 = windowed(left, own, right, 2, 11, 2)
    lam6 = windowed(left, own, right, 3, 15, 3)
    dens = windowed(left, own, right, 4, 18, 0)
    cell = lax.broadcasted_iota(jnp.int32, (32, 128), 0) * 128 + lax.broadcasted_iota(
        jnp.int32, (32, 128), 1
    )

    for w in range(1, 17):
        for j in range(2):
            speed[w, pl.ds(j, 16, 2), :] = speeds[pl.ds(2 * (w - 1) + j, 16, 32), :]
    grads[...] = jnp.zeros_like(grads)
    for w in range(18):
        d = dens(w)
        buoy[w] = jnp.where(d > 0.0, 1.0 / d, 0.0)
    for w in range(1, 17):
        v = speed[w]
        coef[w] = courant * v * v * dens(w)
        centre = buoy[w]
        inside = jnp.where(centre > 0.0, 0.5, 0.0)
        for i, beside in enumerate((buoy[w + 1], buoy[w - 1]) + shifts(centre)):
            faces[i, w] = inside * (centre + beside)
    copies[0].wait()

    def laplace(f, w):
        centre = f(w)
        total = None
        for i, beside in enumerate((f(w + 1), f(w - 1)) + shifts(centre)):
            term = faces[i, w] * (beside - centre)
            total = term if total is None else total + term
        return total

    source_cell = source[0] - (place[0] * 6 - 6) * 4096

    def forward(f, before, n, rows, out):
        for w in rows:
            lap = laplace(f, w)
            if 5 <= w <= 12:
                laps[n, w - 5] = lap
            pulse = jnp.where(cell == source_cell - w * 4096, pulses[0, n], 0.0)
            out[w] = 2.0 * f(w) - before(w) + coef[w] * lap + pulse

    def row_of(ref):
        return lambda w: ref[w]

    forward(u1, u0, 0, range(1, 17), u2)
    forward(row_of(u2), u1, 1, range(2, 16), u3)
    forward(row_of(u3), row_of(u2), 2, range(3, 15), u4)

    def residual(u, n, w):
        at = slice(32 * (w - 3), 32 * (w - 2))
        return counts[0, at, :] * u[w] - counts[1 + n, at, :]

    def backward(f, before, u, n, rows, out):
        for w in rows:
            lap = laplace(lambda v: coef[v] * f(v), w)
            out[w] = 2.0 * f(w) - before(w) + lap + residual(u, n, w)

    copies[1].wait()
    backward(lam5, lam6, u4, 2, range(3, 15), lam4)
    backward(row_of(lam4), lam5, u3, 1, range(4, 14), lam3)
    for w in range(5, 13):
        lap4 = laplace(row_of(u4), w)
        lap = laplace(lambda v: coef[v] * lam3[v], w)
        lam2 = 2.0 * lam3[w] - lam4[w] + lap + residual(u2, 0, w)
        total = lam5(w) * lap4 + lam4[w] * laps[2, w - 5] + lam3[w] * laps[1, w - 5] + lam2 * laps[0, w - 5]
        grads[w - 5, 8:40, :] = total * (2.0 * courant * speed[w] * dens(w))
    for x in range(8):
        for zz in range(4):
            send[pl.ds(4 * x + zz, 16, 32), :] = grads[x, pl.ds(7 + zz, 16, 2), :]


def in_pairs(block):
    at = lax.broadcasted_iota(jnp.int32, (16, 128), 0)
    rest = block - block.astype(BF16).astype(F32)
    return jnp.where(at == 0, block, jnp.where(at == 1, rest, 0.0))


def backward_kernel(
    received, slopes, lines, folded, latent_out, parts_out, low, low_wide, terms, logit_grads
):
    total = received[0]
    for s in range(1, 16):
        total = total + received[s]
    squash = slopes[44, 0:32, :]
    logit_grads[...] = total * speed_span * squash * (1.0 - squash)
    head_sum = jnp.zeros((64, 128), F32)
    bias_sum = jnp.zeros((64, 128), F32)
    for x in range(8):
        for zz in range(4):
            grad = logit_grads[4 * x + zz : 4 * x + zz + 1, :]
            pre_grad = grad * slopes[4 * x + zz]
            rounded = pre_grad.astype(BF16)
            low[x, zz] = rounded
            if 1 <= x <= 6 and 1 <= zz <= 2:
                px = (x - 1) % 2
                low_wide[2 * px + zz - 1, :, 64 * (x - 1 - px) : 64 * (x + 1 - px)] = rounded
                head_sum = head_sum + slopes[30 + 2 * x + zz - 1] * grad
                bias_sum = bias_sum + pre_grad

    ones = jnp.ones((8, 128), BF16)
    row = None
    for piece in split(jnp.concatenate([head_sum, bias_sum], axis=0), 3):
        term = lax.dot_general(ones, piece, NT, preferred_element_type=F32)
        row = term if row is None else row + term
    parts_out[864:880, :] = in_pairs(jnp.concatenate([row, row], axis=0)).astype(BF16)
    parts_out[880:1024, :] = jnp.zeros((144, 128), BF16)

    parities = {-1: (0,), 0: (0, 1), 1: (1,)}
    found = {}
    for dx in (-1, 0, 1):
        for dz in (-1, 0, 1):
            combos = [(px, pz) for px in parities[dx] for pz in parities[dz]]
            if len(combos) == 2 and dx == 0:
                grads = jnp.concatenate([low_wide[2 * px + pz] for px, pz in combos], axis=0)
            else:
                first = 2 * combos[0][0] + combos[0][1]
                grads = low_wide[first : first + len(combos)].reshape(64 * len(combos), 384)
            beside = lines[1 + dz, :, 128 * (1 + dx) : 128 * (4 + dx)]
            product = lax.dot_general(grads, beside, NT, preferred_element_type=F32)
            for i, (px, pz) in enumerate(combos):
                found[dx, px, dz, pz] = at = len(found)
                terms[at] = product[64 * i : 64 * i + 64]
    pairs = {-1: ((-1, 0), (0, 1)), 0: ((0, 0), (0, 1)), 1: ((0, 0), (1, 1))}
    for a in (-1, 0, 1):
        for b in (-1, 0, 1):
            tap = None
            for dx, px in pairs[a]:
                for dz, pz in pairs[b]:
                    term = terms[found[dx, px, dz, pz]]
                    tap = term if tap is None else tap + term
            at = 96 * (3 * (a + 1) + b + 1)
            parts_out[at : at + 64, :] = tap[:, :128].astype(BF16)
            both = jnp.concatenate([tap[:32, 128:], tap[32:, 128:]], axis=1)
            parts_out[at + 64 : at + 96, :] = both.astype(BF16)

    stacked = []
    for x in range(3):
        around = low[2 * x : 2 * x + 4].reshape(1024, 128)
        product = jnp.dot(folded[...], around, preferred_element_type=F32)
        both = product[:192] + product[192:]
        stacked.append(jnp.concatenate([both[64 * e : 64 * e + 64] for e in range(3)], axis=1))
    stacked = jnp.concatenate(stacked, axis=0)
    spread = spread_matrix()
    result = None
    for piece in split(stacked, 2):
        term = lax.dot_general(piece, spread, NT, preferred_element_type=F32)
        result = term if result is None else result + term
    for x in range(3):
        latent_out[x, 0] = result[64 * x : 64 * x + 64]


def sum_kernel(place, received, out):
    total = received[0].astype(F32)
    for s in range(1, received.shape[0]):
        total = total + received[s].astype(F32)
    if out.dtype == BF16:
        pair = jnp.broadcast_to(total[0:1] + total[1:2], (16, 128))
        total = jnp.where(place[0] == 54, in_pairs(pair), total)
    total = total.astype(out.dtype)
    for s in range(out.shape[0]):
        out[s] = total


def unpack_kernel(rows, kernel_out, head_out, bias_out):
    for tap in range(9):
        at = 96 * tap
        pair = rows[at : at + 64, :].astype(F32)
        kernel_out[3 * tap] = pair[:, :64]
        kernel_out[3 * tap + 1] = pair[:, 64:]
        last = rows[at + 64 : at + 96, :].astype(F32)
        kernel_out[3 * tap + 2, 0:32] = last[:, :64]
        kernel_out[3 * tap + 2, 32:64] = last[:, 64:]
    row = rows[864:880, :].astype(F32)
    row = row[0:1] + row[1:2]
    head_out[...] = row[:, :64]
    bias_out[...] = row[:, 64:]


def shape(dims, dtype=F32):
    return jax.ShapeDtypeStruct(dims, dtype)


VMEM = pl.BlockSpec(memory_space=pltpu.VMEM)
ANY = pl.BlockSpec(memory_space=pl.ANY)
HBM = pl.BlockSpec(memory_space=pltpu.HBM)
SMEM = pl.BlockSpec(memory_space=pltpu.SMEM)


def call(kernel, out_shape, in_specs, scratch=(), megabytes=8, flops=None):
    outs = out_shape if isinstance(out_shape, tuple) else (out_shape,)
    specs = tuple(HBM if hasattr(out, "memory_space") else VMEM for out in outs)
    return pl.pallas_call(
        kernel,
        out_shape=out_shape,
        in_specs=list(in_specs),
        out_specs=specs if isinstance(out_shape, tuple) else VMEM,
        scratch_shapes=list(scratch),
        compiler_params=pltpu.CompilerParams(vmem_limit_bytes=megabytes << 20),
        cost_estimate=flops and pl.CostEstimate(flops=flops, bytes_accessed=0, transcendentals=0),
    )


FIELD = pltpu.VMEM((18, 32, 128), F32)
pack = call(
    pack_kernel,
    (
        shape((24, 32, 128)),
        shape((24, 32, 128)),
        shape((3, 64, 64), BF16),
        shape((576, 192), BF16),
        shape((64, 128)),
        shape((64, 128)),
    ),
    [HBM] * 7 + [VMEM] * 2,
    [pltpu.VMEM((27, 64, 64), BF16), pltpu.SemaphoreType.DMA((12,))],
    6,
)
join = call(join_kernel, shape((9, 32, 128), BF16), [VMEM] * 3, (), 2)
decode = call(
    decode_kernel,
    (shape((16, 32, 128)), shape((3, 192, 640), BF16)),
    [VMEM] * 6,
    [
        pltpu.VMEM((3, 192, 1152), BF16),
        pltpu.VMEM((9, 6, 64, 128), F32),
        pltpu.VMEM((32, 128), F32),
    ],
    14,
    500_000_000,
)
slopes = call(
    slopes_kernel,
    (shape((45, 64, 128)), shape((384, 1024), BF16)),
    [VMEM] + [HBM] * 4 + [ANY],
    [
        pltpu.VMEM((576, 192), BF16),
        pltpu.VMEM((64, 128), F32),
        pltpu.VMEM((64, 128), F32),
        pltpu.VMEM((27, 64, 64), BF16),
        pltpu.VMEM((5, 12, 64, 128), F32),
        pltpu.SemaphoreType.DMA((4,)),
    ],
    14,
)
medium = call(
    medium_kernel,
    (shape((30, 32, 128)), pltpu.HBM((4, 384, 128), F32)),
    [SMEM] + [HBM] * 7 + [ANY] * 3,
    [
        pltpu.VMEM((4, 384, 128), F32),
        pltpu.VMEM((1, 128), jnp.int32),
        pltpu.VMEM((3, 1, 128), F32),
        pltpu.SemaphoreType.DMA((8,)),
    ],
    8,
    2_000_000_000,
)
waves = call(
    wave_kernel,
    shape((16, 32, 128)),
    [SMEM] * 2 + [HBM] + [VMEM] * 4 + [HBM],
    [
        pltpu.VMEM((4, 384, 128), F32),
        pltpu.SMEM((1, 3), F32),
        pltpu.VMEM((6, 18, 32, 128), F32),
        FIELD,
        FIELD,
        FIELD,
        FIELD,
        FIELD,
        FIELD,
        pltpu.VMEM((3, 8, 32, 128), F32),
        FIELD,
        FIELD,
        pltpu.VMEM((8, 48, 128), F32),
        pltpu.SemaphoreType.DMA((2,)),
    ],
    14,
)
backward = call(
    backward_kernel,
    (shape((3, 1, 64, 64)), shape((1024, 128), BF16)),
    [VMEM] * 4,
    [
        pltpu.VMEM((8, 4, 64, 128), BF16),
        pltpu.VMEM((4, 64, 384), BF16),
        pltpu.VMEM((16, 64, 192), F32),
        pltpu.VMEM((32, 128), F32),
    ],
    14,
)


def in_hbm(x):
    return pltpu.with_memory_space_constraint(x, pltpu.HBM)


def shifted(block, axes, size):
    low = lax.ppermute(block[0], axes, [(i, i + 1) for i in range(size - 1)])
    high = lax.ppermute(block[1], axes, [(i + 1, i) for i in range(size - 1)])
    return low, high


def per_device(
    latent,
    kernel,
    conv_bias,
    head_weight,
    density,
    wave_prev,
    wave_now,
    adjoint_next,
    adjoint_after,
    source_cell,
    wavelet,
    receiver_cells,
    observed,
):
    place = lax.axis_index(TILE).astype(jnp.int32).reshape(1)
    fields = [in_hbm(f) for f in (wave_now, wave_prev, adjoint_next, adjoint_after, density)]
    taps = in_hbm(kernel)
    coarse = latent.reshape(3, 64, 64)
    low, high = shifted((coarse, coarse), TILE, 32)
    to_next, to_prev, middle, wall, bias, head = pack(
        *fields, in_hbm(coarse), taps, conv_bias.reshape(1, 64), head_weight.reshape(1, 64)
    )
    nine = join(low, middle, high)
    z_prev, z_next = shifted((nine, nine), SHOT, 16)
    to_next, to_prev, nine = lax.optimization_barrier((to_next, to_prev, nine))
    left, right = shifted((to_next, to_prev), TILE, 32)

    speed, lines = decode(z_prev, nine, z_next, wall, bias, head)
    speeds = lax.all_to_all(speed, SHOT, 0, 0, tiled=True)
    records = jnp.transpose(observed, (1, 0, 2))
    own, counts = medium(
        place, *fields, in_hbm(receiver_cells), in_hbm(records), in_hbm(speed), left, right
    )
    strips = waves(
        place,
        source_cell,
        in_hbm(wavelet),
        left,
        right,
        speeds.reshape(512, 128),
        own,
        in_hbm(counts),
    )
    received = lax.all_to_all(strips, SHOT, 0, 0, tiled=True)
    slope, folded = slopes(lines, in_hbm(wall), in_hbm(bias), in_hbm(head), taps, in_hbm(strips))
    latent_grad, parts = backward(received, slope, lines, folded)

    pieces = lax.all_to_all(parts.reshape(64, 16, 128), NEAR, 0, 0, tiled=True)
    piece = lax.axis_index(NEAR).astype(jnp.int32).reshape(1)
    pieces = call(sum_kernel, shape((8, 16, 128)), [SMEM, VMEM])(piece, pieces)
    pieces = lax.all_to_all(pieces, "y", 0, 0, tiled=True)
    pieces = call(sum_kernel, shape((64, 16, 128), BF16), [SMEM, VMEM])(piece, pieces)
    whole = lax.all_to_all(pieces, NEAR, 0, 0, tiled=True)
    kernel_grad, head_grad, bias_grad = call(
        unpack_kernel, (shape((27, 64, 64)), shape((1, 64)), shape((1, 64))), [VMEM]
    )(whole.reshape(1024, 128))
    head_grad = head_grad.reshape(64)
    bias_grad = bias_grad.reshape(64)
    return latent_grad, kernel_grad, head_grad, bias_grad


def solution(mesh):
    fine_mesh = Mesh(mesh.devices.reshape(2, 8, 8, 2, 2), ("xlo", "z", "y", "xhi", "core"))
    return jax.shard_map(
        per_device,
        mesh=fine_mesh,
        in_specs=(
            P(TILE, SHOT, None, None),
            P(),
            P(),
            P(),
            P(TILE, None, None),
            P(SHOT, TILE, None, None),
            P(SHOT, TILE, None, None),
            P(SHOT, TILE, None, None),
            P(SHOT, TILE, None, None),
            P(SHOT),
            P(SHOT, None),
            P(SHOT, None),
            P(SHOT, None, None),
        ),
        out_specs=(P(TILE, SHOT, None, None), P(), P(), P()),
        check_vma=False,
    )
```

```python
import jax
import jax.numpy as jnp
from jax import lax
from jax.experimental import pallas as pl
from jax.experimental.pallas import tpu as pltpu
from jax.sharding import Mesh
from jax.sharding import PartitionSpec as P

SHOT = ("xlo", "z")
TILE = ("y", "xhi", "core")
NEAR = ("xlo", "z", "xhi", "core")
F32 = jnp.float32
BF16 = jnp.bfloat16
courant = 0.005
speed_low = 1.5
speed_span = 3.0
NT = (((1,), (1,)), ((), ()))


def sigmoid(v):
    return 1.0 / (1.0 + jnp.exp(-v))


def split(v, parts):
    out = []
    for _ in range(parts):
        piece = v.astype(BF16)
        out.append(piece)
        v = v - piece.astype(F32)
    return out


def spread_matrix():
    coarse = lax.broadcasted_iota(jnp.int32, (64, 384), 0)
    lane = lax.broadcasted_iota(jnp.int32, (64, 384), 1)
    fine = (lane & 127) + (lane >> 7) - 1
    return jnp.where((fine >> 1) == coarse, 1.0, 0.0).astype(BF16)


Z_LINE = ((0, 0, 1), (0, 1, 1), (1, 1, 2), (1, 2, 2))


def start_all(copies):
    for copy in copies:
        copy.start()
    return copies


def wait_all(copies):
    for copy in copies:
        copy.wait()


def pack_kernel(
    wave_now,
    wave_prev,
    adj_next,
    adj_after,
    density,
    latent,
    kernel_in,
    bias,
    head,
    to_next,
    to_prev,
    coarse,
    wall,
    bias_wide,
    head_wide,
    kernel,
    sems,
):
    copies = [
        pltpu.make_async_copy(kernel_in, kernel, sems.at[11]),
        pltpu.make_async_copy(latent, coarse, sems.at[10]),
    ]
    fields = ((wave_now, 6), (wave_prev, 5), (adj_next, 4), (adj_after, 3), (density, 6))
    at = 0
    for i, (ref, rows) in enumerate(fields):
        field = ref if i == 4 else ref.at[0]
        here = pl.ds(at, rows)
        copies.append(pltpu.make_async_copy(field.at[pl.ds(6 - rows, rows)], to_next.at[here], sems.at[i]))
        copies.append(pltpu.make_async_copy(field.at[pl.ds(0, rows)], to_prev.at[here], sems.at[5 + i]))
        at += rows
    start_all(copies)
    bias_wide[...] = jnp.broadcast_to(bias[...], (128, 64)).T
    head_wide[...] = jnp.broadcast_to(head[...].astype(F32), (128, 64)).T
    copies[0].wait()
    for a in range(3):
        for b in range(3):
            at = 64 * (3 * b + a)
            taps = [kernel[9 * a + 3 * b + e] for e in range(3)]
            wall[at : at + 64, :] = jnp.concatenate(taps, axis=1)
    wait_all(copies[1:])


def join_kernel(low, middle, high, out):
    for i, ref in enumerate((low, middle, high)):
        for x in range(3):
            out[3 * i + x] = jnp.concatenate([ref[x, 0:32], ref[x, 32:64]], axis=1)


def fold_taps(kernel, folded):
    reach = ((2,), (1, 2), (0, 1), (0,))
    for i in range(4):
        for j in range(0, 4, 2):
            blocks = []
            for jj in (j, j + 1):
                row = []
                for e in range(3):
                    total = None
                    for a in reach[i]:
                        for b in reach[jj]:
                            term = kernel[9 * a + 3 * b + e].astype(F32)
                            total = term if total is None else total + term
                    row.append(total)
                blocks.append(jnp.concatenate(row, axis=1))
            table = jnp.concatenate(blocks, axis=0).T
            high, low = split(table, 2)
            at = 64 * (4 * i + j)
            folded[0:192, at : at + 128] = high
            folded[192:384, at : at + 128] = low


def z_sums(product, rows, store):
    for a in range(3):
        for zz in rows:
            total = None
            for b in range(3):
                zi = Z_LINE[zz][b]
                term = product[64 * (3 * b + a) : 64 * (3 * b + a) + 64, 128 * zi : 128 * zi + 128]
                total = term if total is None else total + term
            store(a, zz, total)


def decode_kernel(z_prev, own, z_next, wall, bias, head, speed_out, lines_out, lines, sums, row_logit):
    spread = spread_matrix()
    for zi, ref in enumerate((z_prev, own, z_next)):
        packed = [ref[x] for x in range(9)]
        rows = jnp.concatenate([half for p in packed for half in (p[:, :64], p[:, 64:])], axis=0)
        fine = jnp.dot(rows, spread, preferred_element_type=F32).astype(BF16)
        for x in range(9):
            for e in range(3):
                piece = fine[64 * x : 64 * x + 64, 128 * e : 128 * e + 128]
                lines[zi, 64 * e : 64 * e + 64, 128 * x : 128 * x + 128] = piece
                if 2 <= x <= 6:
                    lines_out[zi, 64 * e : 64 * e + 64, 128 * (x - 2) : 128 * (x - 1)] = piece

    for first, count in ((0, 2), (2, 2), (4, 2), (6, 3)):
        at = slice(128 * first, 128 * (first + count))
        before = jnp.dot(wall[0:192, :], lines[0, :, at], preferred_element_type=F32)
        middle = jnp.dot(wall[...], lines[1, :, at], preferred_element_type=F32)
        after = jnp.dot(wall[384:576, :], lines[2, :, at], preferred_element_type=F32)
        for i in range(count):
            col = slice(128 * i, 128 * i + 128)
            for a in range(3):
                low, centre, high = [middle[64 * (3 * b + a) : 64 * (3 * b + a) + 64, col] for b in range(3)]
                block = slice(64 * a, 64 * a + 64)
                sums[first + i, 2 * a] = before[block, col] + (centre + high)
                sums[first + i, 2 * a + 1] = (low + centre) + after[block, col]

    def rows(k, carry):
        r = k + 1
        for j in range(2):
            pre = sums[(r - 1) // 2, j] + sums[r // 2, 2 + j] + sums[(r + 1) // 2, 4 + j] + bias[...]
            hidden = (pre * sigmoid(pre)).astype(BF16).astype(F32)
            row_logit[pl.ds(2 * k + j, 1), :] = jnp.sum(hidden * head[...], axis=0, keepdims=True)
        return carry

    lax.fori_loop(0, 16, rows, 0, unroll=2)
    speed = speed_low + speed_span * sigmoid(row_logit[...])
    for s in range(16):
        speed_out[s] = speed


def slopes_kernel(
    lines, wall_in, bias_in, head_in, kernel_in, after, slope_out, folded, wall, bias, head, kernel, sums, sems
):
    copies = start_all(
        [
            pltpu.make_async_copy(source, target, sems.at[i])
            for i, (source, target) in enumerate(
                ((wall_in, wall), (bias_in, bias), (head_in, head), (kernel_in, kernel))
            )
        ]
    )
    wait_all(copies)
    for x in range(5):
        columns = [lines[zi, :, 128 * x : 128 * x + 128] for zi in range(3)]
        product = jnp.dot(wall[...], jnp.concatenate(columns, axis=1), preferred_element_type=F32)

        def store(a, zz, total):
            sums[x, 4 * a + zz] = total

        z_sums(product, range(4), store)

    def rows(k, owned):
        r = k + 1
        for zz in range(4):
            pre = sums[(r - 1) // 2, zz] + sums[r // 2, 4 + zz] + sums[(r + 1) // 2, 8 + zz] + bias[...]
            gate = sigmoid(pre)
            hidden = (pre * gate).astype(BF16).astype(F32)
            slope_out[4 * k + zz] = head[...] * (gate * (1.0 + pre * (1.0 - gate)))
            if owned and zz in (1, 2):
                slope_out[30 + 2 * k + zz - 1] = hidden
            logit = jnp.sum(hidden * head[...], axis=0, keepdims=True)
            slope_out[44, pl.ds(4 * k + zz, 1), :] = logit
        return owned

    rows(0, False)
    lax.fori_loop(1, 7, lambda k, carry: rows(k, True), True)
    rows(7, False)
    slope_out[44, 0:32, :] = sigmoid(slope_out[44, 0:32, :])
    slope_out[44, 32:64, :] = jnp.zeros((32, 128), F32)
    fold_taps(kernel, folded)


def shifts(f):
    z_at = lax.broadcasted_iota(jnp.int32, (32, 128), 0)
    y_at = lax.broadcasted_iota(jnp.int32, (32, 128), 1)
    return (
        jnp.where(z_at < 31, pltpu.roll(f, 31, 0), 0.0),
        jnp.where(z_at > 0, pltpu.roll(f, 1, 0), 0.0),
        jnp.where(y_at < 127, pltpu.roll(f, 127, 1), 0.0),
        jnp.where(y_at > 0, pltpu.roll(f, 1, 1), 0.0),
    )


def windowed(left, own, right, field, offset, first):
    def get(w):
        if w < 6:
            return left[offset + w - first]
        if w < 12:
            return own[6 * field + w - 6]
        return right[offset + w - 12]

    return get


def medium_kernel(
    place,
    wave_now,
    wave_prev,
    adj_next,
    adj_after,
    density,
    receivers_in,
    observed_in,
    after,
    left,
    right,
    own,
    counts_out,
    counts,
    receivers,
    observed,
    sems,
):
    fields = (wave_now.at[0], wave_prev.at[0], adj_next.at[0], adj_after.at[0], density)
    wait_all(
        start_all(
            [pltpu.make_async_copy(f, own.at[pl.ds(6 * i, 6)], sems.at[i]) for i, f in enumerate(fields)]
            + [
                pltpu.make_async_copy(receivers_in, receivers, sems.at[5]),
                pltpu.make_async_copy(observed_in, observed, sems.at[6]),
            ]
        )
    )
    local = receivers[...] - (place[0] * 6 - 3) * 4096
    at_row = lax.broadcasted_iota(jnp.int32, (384, 128), 0) == (local >> 7)
    at_y = lax.broadcasted_iota(jnp.int32, (128, 128), 0) == (local & 127)
    picks = [jnp.where(at_y, 1.0, 0.0).astype(BF16)]
    for n in range(3):
        for piece in split(observed[n], 3):
            picks.append(jnp.where(at_y, piece.astype(F32), 0.0).astype(BF16))
    maps = lax.dot_general(
        jnp.where(at_row, 1.0, 0.0).astype(BF16),
        jnp.concatenate(picks, axis=0),
        NT,
        preferred_element_type=F32,
    )
    counts[0] = maps[:, 0:128]
    for n in range(3):
        at = 128 + 384 * n
        counts[1 + n] = maps[:, at : at + 128] + maps[:, at + 128 : at + 256] + maps[:, at + 256 : at + 384]
    wait_all(start_all([pltpu.make_async_copy(counts, counts_out, sems.at[7])]))


def wave_kernel(
    place,
    source,
    pulses_in,
    left,
    right,
    speeds,
    own,
    counts_in,
    send_out,
    counts,
    pulses,
    faces,
    buoy,
    coef,
    speed,
    u2,
    u3,
    u4,
    laps,
    lam4,
    lam3,
    grads,
    sems,
):
    copies = start_all(
        [
            pltpu.make_async_copy(pulses_in, pulses, sems.at[0]),
            pltpu.make_async_copy(counts_in, counts, sems.at[1]),
        ]
    )
    send = send_out.reshape(512, 128)
    u1 = windowed(left, own, right, 0, 0, 0)
    u0 = windowed(left, own, right, 1, 6, 1)
    lam5 = windowed(left, own, right, 2, 11, 2)
    lam6 = windowed(left, own, right, 3, 15, 3)
    dens = windowed(left, own, right, 4, 18, 0)
    cell = lax.broadcasted_iota(jnp.int32, (32, 128), 0) * 128 + lax.broadcasted_iota(
        jnp.int32, (32, 128), 1
    )

    for w in range(1, 17):
        for j in range(2):
            speed[w, pl.ds(j, 16, 2), :] = speeds[pl.ds(2 * (w - 1) + j, 16, 32), :]
    grads[...] = jnp.zeros_like(grads)
    for w in range(18):
        d = dens(w)
        buoy[w] = jnp.where(d > 0.0, 1.0 / d, 0.0)
    for w in range(1, 17):
        v = speed[w]
        coef[w] = courant * v * v * dens(w)
        centre = buoy[w]
        inside = jnp.where(centre > 0.0, 0.5, 0.0)
        for i, beside in enumerate((buoy[w + 1], buoy[w - 1]) + shifts(centre)):
            faces[i, w] = inside * (centre + beside)
    copies[0].wait()

    def laplace(f, w):
        centre = f(w)
        total = None
        for i, beside in enumerate((f(w + 1), f(w - 1)) + shifts(centre)):
            term = faces[i, w] * (beside - centre)
            total = term if total is None else total + term
        return total

    source_cell = source[0] - (place[0] * 6 - 6) * 4096

    def forward(f, before, n, rows, out):
        for w in rows:
            lap = laplace(f, w)
            if 5 <= w <= 12:
                laps[n, w - 5] = lap
            pulse = jnp.where(cell == source_cell - w * 4096, pulses[0, n], 0.0)
            out[w] = 2.0 * f(w) - before(w) + coef[w] * lap + pulse

    def row_of(ref):
        return lambda w: ref[w]

    forward(u1, u0, 0, range(1, 17), u2)
    forward(row_of(u2), u1, 1, range(2, 16), u3)
    forward(row_of(u3), row_of(u2), 2, range(3, 15), u4)

    def residual(u, n, w):
        at = slice(32 * (w - 3), 32 * (w - 2))
        return counts[0, at, :] * u[w] - counts[1 + n, at, :]

    def backward(f, before, u, n, rows, out):
        for w in rows:
            lap = laplace(lambda v: coef[v] * f(v), w)
            out[w] = 2.0 * f(w) - before(w) + lap + residual(u, n, w)

    copies[1].wait()
    backward(lam5, lam6, u4, 2, range(3, 15), lam4)
    backward(row_of(lam4), lam5, u3, 1, range(4, 14), lam3)
    for w in range(5, 13):
        lap4 = laplace(row_of(u4), w)
        lap = laplace(lambda v: coef[v] * lam3[v], w)
        lam2 = 2.0 * lam3[w] - lam4[w] + lap + residual(u2, 0, w)
        total = lam5(w) * lap4 + lam4[w] * laps[2, w - 5] + lam3[w] * laps[1, w - 5] + lam2 * laps[0, w - 5]
        grads[w - 5, 8:40, :] = total * (2.0 * courant * speed[w] * dens(w))
    for x in range(8):
        for zz in range(4):
            send[pl.ds(4 * x + zz, 16, 32), :] = grads[x, pl.ds(7 + zz, 16, 2), :]


def in_pairs(block):
    at = lax.broadcasted_iota(jnp.int32, (16, 128), 0)
    rest = block - block.astype(BF16).astype(F32)
    return jnp.where(at == 0, block, jnp.where(at == 1, rest, 0.0))


def backward_kernel(
    received, slopes, lines, low_out, parts_out, low, low_wide, terms, logit_grads, sem
):
    total = received[0]
    for s in range(1, 16):
        total = total + received[s]
    squash = slopes[44, 0:32, :]
    logit_grads[...] = total * speed_span * squash * (1.0 - squash)
    head_sum = jnp.zeros((64, 128), F32)
    bias_sum = jnp.zeros((64, 128), F32)
    for x in range(8):
        for zz in range(4):
            grad = logit_grads[4 * x + zz : 4 * x + zz + 1, :]
            pre_grad = grad * slopes[4 * x + zz]
            rounded = pre_grad.astype(BF16)
            low[x, zz] = rounded
            if 1 <= x <= 6 and 1 <= zz <= 2:
                px = (x - 1) % 2
                low_wide[2 * px + zz - 1, :, 64 * (x - 1 - px) : 64 * (x + 1 - px)] = rounded
                head_sum = head_sum + slopes[30 + 2 * x + zz - 1] * grad
                bias_sum = bias_sum + pre_grad

    copy = pltpu.make_async_copy(low, low_out, sem)
    copy.start()

    ones = jnp.ones((8, 128), BF16)
    row = None
    for piece in split(jnp.concatenate([head_sum, bias_sum], axis=0), 3):
        term = lax.dot_general(ones, piece, NT, preferred_element_type=F32)
        row = term if row is None else row + term
    parts_out[864:880, :] = in_pairs(jnp.concatenate([row, row], axis=0)).astype(BF16)
    parts_out[880:1024, :] = jnp.zeros((144, 128), BF16)

    parities = {-1: (0,), 0: (0, 1), 1: (1,)}
    found = {}
    for dx in (-1, 0, 1):
        for dz in (-1, 0, 1):
            combos = [(px, pz) for px in parities[dx] for pz in parities[dz]]
            if len(combos) == 2 and dx == 0:
                grads = jnp.concatenate([low_wide[2 * px + pz] for px, pz in combos], axis=0)
            else:
                first = 2 * combos[0][0] + combos[0][1]
                grads = low_wide[first : first + len(combos)].reshape(64 * len(combos), 384)
            beside = lines[1 + dz, :, 128 * (1 + dx) : 128 * (4 + dx)]
            product = lax.dot_general(grads, beside, NT, preferred_element_type=F32)
            for i, (px, pz) in enumerate(combos):
                found[dx, px, dz, pz] = at = len(found)
                terms[at] = product[64 * i : 64 * i + 64]
    pairs = {-1: ((-1, 0), (0, 1)), 0: ((0, 0), (0, 1)), 1: ((0, 0), (1, 1))}
    for a in (-1, 0, 1):
        for b in (-1, 0, 1):
            tap = None
            for dx, px in pairs[a]:
                for dz, pz in pairs[b]:
                    term = terms[found[dx, px, dz, pz]]
                    tap = term if tap is None else tap + term
            at = 96 * (3 * (a + 1) + b + 1)
            parts_out[at : at + 64, :] = tap[:, :128].astype(BF16)
            both = jnp.concatenate([tap[:32, 128:], tap[32:, 128:]], axis=1)
            parts_out[at + 64 : at + 96, :] = both.astype(BF16)
    copy.wait()


def latent_kernel(low_in, folded, after, latent_out, low, sem):
    copy = pltpu.make_async_copy(low_in, low, sem)
    copy.start()
    copy.wait()
    stacked = []
    for x in range(3):
        around = low[2 * x : 2 * x + 4].reshape(1024, 128)
        product = jnp.dot(folded[...], around, preferred_element_type=F32)
        both = product[:192] + product[192:]
        stacked.append(jnp.concatenate([both[64 * e : 64 * e + 64] for e in range(3)], axis=1))
    stacked = jnp.concatenate(stacked, axis=0)
    spread = spread_matrix()
    result = None
    for piece in split(stacked, 2):
        term = lax.dot_general(piece, spread, NT, preferred_element_type=F32)
        result = term if result is None else result + term
    for x in range(3):
        latent_out[x, 0] = result[64 * x : 64 * x + 64]


def sum_kernel(place, received, out):
    total = received[0].astype(F32)
    for s in range(1, received.shape[0]):
        total = total + received[s].astype(F32)
    if out.dtype == BF16:
        pair = jnp.broadcast_to(total[0:1] + total[1:2], (16, 128))
        total = jnp.where(place[0] == 54, in_pairs(pair), total)
    total = total.astype(out.dtype)
    for s in range(out.shape[0]):
        out[s] = total


def unpack_kernel(rows, kernel_out, head_out, bias_out):
    for tap in range(9):
        at = 96 * tap
        pair = rows[at : at + 64, :].astype(F32)
        kernel_out[3 * tap] = pair[:, :64]
        kernel_out[3 * tap + 1] = pair[:, 64:]
        last = rows[at + 64 : at + 96, :].astype(F32)
        kernel_out[3 * tap + 2, 0:32] = last[:, :64]
        kernel_out[3 * tap + 2, 32:64] = last[:, 64:]
    row = rows[864:880, :].astype(F32)
    row = row[0:1] + row[1:2]
    head_out[...] = row[:, :64]
    bias_out[...] = row[:, 64:]


def shape(dims, dtype=F32):
    return jax.ShapeDtypeStruct(dims, dtype)


VMEM = pl.BlockSpec(memory_space=pltpu.VMEM)
ANY = pl.BlockSpec(memory_space=pl.ANY)
HBM = pl.BlockSpec(memory_space=pltpu.HBM)
SMEM = pl.BlockSpec(memory_space=pltpu.SMEM)


def call(kernel, out_shape, in_specs, scratch=(), megabytes=8, flops=None):
    outs = out_shape if isinstance(out_shape, tuple) else (out_shape,)
    specs = tuple(HBM if hasattr(out, "memory_space") else VMEM for out in outs)
    return pl.pallas_call(
        kernel,
        out_shape=out_shape,
        in_specs=list(in_specs),
        out_specs=specs if isinstance(out_shape, tuple) else VMEM,
        scratch_shapes=list(scratch),
        compiler_params=pltpu.CompilerParams(vmem_limit_bytes=megabytes << 20),
        cost_estimate=flops and pl.CostEstimate(flops=flops, bytes_accessed=0, transcendentals=0),
    )


FIELD = pltpu.VMEM((18, 32, 128), F32)
pack = call(
    pack_kernel,
    (
        shape((24, 32, 128)),
        shape((24, 32, 128)),
        shape((3, 64, 64), BF16),
        shape((576, 192), BF16),
        shape((64, 128)),
        shape((64, 128)),
    ),
    [HBM] * 7 + [VMEM] * 2,
    [pltpu.VMEM((27, 64, 64), BF16), pltpu.SemaphoreType.DMA((12,))],
    6,
)
join = call(join_kernel, shape((9, 32, 128), BF16), [VMEM] * 3, (), 2)
decode = call(
    decode_kernel,
    (shape((16, 32, 128)), shape((3, 192, 640), BF16)),
    [VMEM] * 6,
    [
        pltpu.VMEM((3, 192, 1152), BF16),
        pltpu.VMEM((9, 6, 64, 128), F32),
        pltpu.VMEM((32, 128), F32),
    ],
    14,
    500_000_000,
)
slopes = call(
    slopes_kernel,
    (shape((45, 64, 128)), shape((384, 1024), BF16)),
    [VMEM] + [HBM] * 4 + [ANY],
    [
        pltpu.VMEM((576, 192), BF16),
        pltpu.VMEM((64, 128), F32),
        pltpu.VMEM((64, 128), F32),
        pltpu.VMEM((27, 64, 64), BF16),
        pltpu.VMEM((5, 12, 64, 128), F32),
        pltpu.SemaphoreType.DMA((4,)),
    ],
    14,
)
medium = call(
    medium_kernel,
    (shape((30, 32, 128)), pltpu.HBM((4, 384, 128), F32)),
    [SMEM] + [HBM] * 7 + [ANY] * 3,
    [
        pltpu.VMEM((4, 384, 128), F32),
        pltpu.VMEM((1, 128), jnp.int32),
        pltpu.VMEM((3, 1, 128), F32),
        pltpu.SemaphoreType.DMA((8,)),
    ],
    8,
    2_000_000_000,
)
waves = call(
    wave_kernel,
    shape((16, 32, 128)),
    [SMEM] * 2 + [HBM] + [VMEM] * 4 + [HBM],
    [
        pltpu.VMEM((4, 384, 128), F32),
        pltpu.SMEM((1, 3), F32),
        pltpu.VMEM((6, 18, 32, 128), F32),
        FIELD,
        FIELD,
        FIELD,
        FIELD,
        FIELD,
        FIELD,
        pltpu.VMEM((3, 8, 32, 128), F32),
        FIELD,
        FIELD,
        pltpu.VMEM((8, 48, 128), F32),
        pltpu.SemaphoreType.DMA((2,)),
    ],
    14,
)
backward = call(
    backward_kernel,
    (pltpu.HBM((8, 4, 64, 128), BF16), shape((1024, 128), BF16)),
    [VMEM] * 3,
    [
        pltpu.VMEM((8, 4, 64, 128), BF16),
        pltpu.VMEM((4, 64, 384), BF16),
        pltpu.VMEM((16, 64, 192), F32),
        pltpu.VMEM((32, 128), F32),
        pltpu.SemaphoreType.DMA,
    ],
    14,
)
latent_part = call(
    latent_kernel,
    shape((3, 1, 64, 64)),
    [HBM, VMEM, ANY],
    [pltpu.VMEM((8, 4, 64, 128), BF16), pltpu.SemaphoreType.DMA],
    14,
)


def in_hbm(x):
    return pltpu.with_memory_space_constraint(x, pltpu.HBM)


def shifted(block, axes, size):
    low = lax.ppermute(block[0], axes, [(i, i + 1) for i in range(size - 1)])
    high = lax.ppermute(block[1], axes, [(i + 1, i) for i in range(size - 1)])
    return low, high


def per_device(
    latent,
    kernel,
    conv_bias,
    head_weight,
    density,
    wave_prev,
    wave_now,
    adjoint_next,
    adjoint_after,
    source_cell,
    wavelet,
    receiver_cells,
    observed,
):
    place = lax.axis_index(TILE).astype(jnp.int32).reshape(1)
    fields = [in_hbm(f) for f in (wave_now, wave_prev, adjoint_next, adjoint_after, density)]
    taps = in_hbm(kernel)
    coarse = latent.reshape(3, 64, 64)
    low, high = shifted((coarse, coarse), TILE, 32)
    to_next, to_prev, middle, wall, bias, head = pack(
        *fields, in_hbm(coarse), taps, conv_bias.reshape(1, 64), head_weight.reshape(1, 64)
    )
    nine = join(low, middle, high)
    z_prev, z_next = shifted((nine, nine), SHOT, 16)
    to_next, to_prev, nine = lax.optimization_barrier((to_next, to_prev, nine))
    left, right = shifted((to_next, to_prev), TILE, 32)

    speed, lines = decode(z_prev, nine, z_next, wall, bias, head)
    speeds = lax.all_to_all(speed, SHOT, 0, 0, tiled=True)
    records = jnp.transpose(observed, (1, 0, 2))
    own, counts = medium(
        place, *fields, in_hbm(receiver_cells), in_hbm(records), in_hbm(speed), left, right
    )
    strips = waves(
        place,
        source_cell,
        in_hbm(wavelet),
        left,
        right,
        speeds.reshape(512, 128),
        own,
        in_hbm(counts),
    )
    received = lax.all_to_all(strips, SHOT, 0, 0, tiled=True)
    slope, folded = slopes(lines, in_hbm(wall), in_hbm(bias), in_hbm(head), taps, in_hbm(strips))
    low, parts = backward(received, slope, lines)
    latent_grad = latent_part(in_hbm(low), folded, parts)

    pieces = lax.all_to_all(parts.reshape(64, 16, 128), NEAR, 0, 0, tiled=True)
    piece = lax.axis_index(NEAR).astype(jnp.int32).reshape(1)
    pieces = call(sum_kernel, shape((8, 16, 128)), [SMEM, VMEM])(piece, pieces)
    pieces = lax.all_to_all(pieces, "y", 0, 0, tiled=True)
    pieces = call(sum_kernel, shape((64, 16, 128), BF16), [SMEM, VMEM])(piece, pieces)
    whole = lax.all_to_all(pieces, NEAR, 0, 0, tiled=True)
    kernel_grad, head_grad, bias_grad = call(
        unpack_kernel, (shape((27, 64, 64)), shape((1, 64)), shape((1, 64))), [VMEM]
    )(whole.reshape(1024, 128))
    head_grad = head_grad.reshape(64)
    bias_grad = bias_grad.reshape(64)
    return latent_grad, kernel_grad, head_grad, bias_grad


def solution(mesh):
    fine_mesh = Mesh(mesh.devices.reshape(2, 8, 8, 2, 2), ("xlo", "z", "y", "xhi", "core"))
    return jax.shard_map(
        per_device,
        mesh=fine_mesh,
        in_specs=(
            P(TILE, SHOT, None, None),
            P(),
            P(),
            P(),
            P(TILE, None, None),
            P(SHOT, TILE, None, None),
            P(SHOT, TILE, None, None),
            P(SHOT, TILE, None, None),
            P(SHOT, TILE, None, None),
            P(SHOT),
            P(SHOT, None),
            P(SHOT, None),
            P(SHOT, None, None),
        ),
        out_specs=(P(TILE, SHOT, None, None), P(), P(), P()),
        check_vma=False,
    )
```

```python
import jax
import jax.numpy as jnp
from jax import lax
from jax.experimental import pallas as pl
from jax.experimental.pallas import tpu as pltpu
from jax.sharding import Mesh
from jax.sharding import PartitionSpec as P

SHOT = ("xlo", "z")
TILE = ("y", "xhi", "core")
NEAR = ("xlo", "z", "xhi", "core")
F32 = jnp.float32
BF16 = jnp.bfloat16
courant = 0.005
speed_low = 1.5
speed_span = 3.0
NT = (((1,), (1,)), ((), ()))


def sigmoid(v):
    return 1.0 / (1.0 + jnp.exp(-v))


def split(v, parts):
    out = []
    for _ in range(parts):
        piece = v.astype(BF16)
        out.append(piece)
        v = v - piece.astype(F32)
    return out


def spread_matrix():
    coarse = lax.broadcasted_iota(jnp.int32, (64, 384), 0)
    lane = lax.broadcasted_iota(jnp.int32, (64, 384), 1)
    fine = (lane & 127) + (lane >> 7) - 1
    return jnp.where((fine >> 1) == coarse, 1.0, 0.0).astype(BF16)


Z_LINE = ((0, 0, 1), (0, 1, 1), (1, 1, 2), (1, 2, 2))


def start_all(copies):
    for copy in copies:
        copy.start()
    return copies


def wait_all(copies):
    for copy in copies:
        copy.wait()


def pack_kernel(
    wave_now,
    wave_prev,
    adj_next,
    adj_after,
    density,
    latent,
    kernel_in,
    bias_in,
    head,
    to_next,
    to_prev,
    coarse,
    wall,
    bias_wide,
    head_wide,
    kernel,
    bias,
    sems,
):
    copies = [
        pltpu.make_async_copy(kernel_in, kernel, sems.at[11]),
        pltpu.make_async_copy(bias_in, bias, sems.at[12]),
        pltpu.make_async_copy(latent, coarse, sems.at[10]),
    ]
    fields = ((wave_now, 6), (wave_prev, 5), (adj_next, 4), (adj_after, 3), (density, 6))
    at = 0
    for i, (ref, rows) in enumerate(fields):
        field = ref if i == 4 else ref.at[0]
        here = pl.ds(at, rows)
        copies.append(pltpu.make_async_copy(field.at[pl.ds(6 - rows, rows)], to_next.at[here], sems.at[i]))
        copies.append(pltpu.make_async_copy(field.at[pl.ds(0, rows)], to_prev.at[here], sems.at[5 + i]))
        at += rows
    start_all(copies)
    head_wide[...] = jnp.broadcast_to(head[...].astype(F32), (128, 64)).T
    wait_all(copies[:2])
    bias_wide[...] = jnp.broadcast_to(bias[...], (128, 64)).T
    for a in range(3):
        for b in range(3):
            at = 64 * (3 * b + a)
            taps = [kernel[9 * a + 3 * b + e] for e in range(3)]
            wall[at : at + 64, :] = jnp.concatenate(taps, axis=1)
    wait_all(copies[2:])


def join_kernel(high, middle, low, out):
    for i, ref in enumerate((low, middle, high)):
        for x in range(3):
            out[3 * i + x] = jnp.concatenate([ref[x, 0:32], ref[x, 32:64]], axis=1)


def fold_taps(kernel, folded):
    reach = ((2,), (1, 2), (0, 1), (0,))
    for i in range(4):
        for j in range(0, 4, 2):
            blocks = []
            for jj in (j, j + 1):
                row = []
                for e in range(3):
                    total = None
                    for a in reach[i]:
                        for b in reach[jj]:
                            term = kernel[9 * a + 3 * b + e].astype(F32)
                            total = term if total is None else total + term
                    row.append(total)
                blocks.append(jnp.concatenate(row, axis=1))
            table = jnp.concatenate(blocks, axis=0).T
            high, low = split(table, 2)
            at = 64 * (4 * i + j)
            folded[0:192, at : at + 128] = high
            folded[192:384, at : at + 128] = low


def z_sums(product, rows, store):
    for a in range(3):
        for zz in rows:
            total = None
            for b in range(3):
                zi = Z_LINE[zz][b]
                term = product[64 * (3 * b + a) : 64 * (3 * b + a) + 64, 128 * zi : 128 * zi + 128]
                total = term if total is None else total + term
            store(a, zz, total)


def decode_kernel(z_next, own, z_prev, wall, bias, head, speed_out, lines_out, lines, sums, row_logit):
    spread = spread_matrix()
    for zi, ref in enumerate((z_prev, own, z_next)):
        packed = [ref[x] for x in range(9)]
        rows = jnp.concatenate([half for p in packed for half in (p[:, :64], p[:, 64:])], axis=0)
        fine = jnp.dot(rows, spread, preferred_element_type=F32).astype(BF16)
        for x in range(9):
            for e in range(3):
                piece = fine[64 * x : 64 * x + 64, 128 * e : 128 * e + 128]
                lines[zi, 64 * e : 64 * e + 64, 128 * x : 128 * x + 128] = piece
                if 2 <= x <= 6:
                    lines_out[zi, 64 * e : 64 * e + 64, 128 * (x - 2) : 128 * (x - 1)] = piece

    for first, count in ((0, 2), (2, 2), (4, 2), (6, 3)):
        at = slice(128 * first, 128 * (first + count))
        before = jnp.dot(wall[0:192, :], lines[0, :, at], preferred_element_type=F32)
        middle = jnp.dot(wall[...], lines[1, :, at], preferred_element_type=F32)
        after = jnp.dot(wall[384:576, :], lines[2, :, at], preferred_element_type=F32)
        for i in range(count):
            col = slice(128 * i, 128 * i + 128)
            for a in range(3):
                low, centre, high = [middle[64 * (3 * b + a) : 64 * (3 * b + a) + 64, col] for b in range(3)]
                block = slice(64 * a, 64 * a + 64)
                sums[first + i, 2 * a] = before[block, col] + (centre + high)
                sums[first + i, 2 * a + 1] = (low + centre) + after[block, col]

    def rows(k, carry):
        r = k + 1
        for j in range(2):
            pre = sums[(r - 1) // 2, j] + sums[r // 2, 2 + j] + sums[(r + 1) // 2, 4 + j] + bias[...]
            hidden = (pre * sigmoid(pre)).astype(BF16).astype(F32)
            row_logit[pl.ds(2 * k + j, 1), :] = jnp.sum(hidden * head[...], axis=0, keepdims=True)
        return carry

    lax.fori_loop(0, 16, rows, 0, unroll=2)
    speed = speed_low + speed_span * sigmoid(row_logit[...])
    for s in range(16):
        speed_out[s] = speed


def slopes_kernel(
    lines, wall_in, bias_in, head_in, kernel_in, after, slope_out, folded, wall, bias, head, kernel, sums, sems
):
    copies = start_all(
        [
            pltpu.make_async_copy(source, target, sems.at[i])
            for i, (source, target) in enumerate(
                ((wall_in, wall), (bias_in, bias), (head_in, head), (kernel_in, kernel))
            )
        ]
    )
    wait_all(copies)
    for x in range(5):
        columns = [lines[zi, :, 128 * x : 128 * x + 128] for zi in range(3)]
        product = jnp.dot(wall[...], jnp.concatenate(columns, axis=1), preferred_element_type=F32)

        def store(a, zz, total):
            sums[x, 4 * a + zz] = total

        z_sums(product, range(4), store)

    def rows(k, owned):
        r = k + 1
        for zz in range(4):
            pre = sums[(r - 1) // 2, zz] + sums[r // 2, 4 + zz] + sums[(r + 1) // 2, 8 + zz] + bias[...]
            gate = sigmoid(pre)
            hidden = (pre * gate).astype(BF16).astype(F32)
            slope_out[4 * k + zz] = head[...] * (gate * (1.0 + pre * (1.0 - gate)))
            if owned and zz in (1, 2):
                slope_out[30 + 2 * k + zz - 1] = hidden
            logit = jnp.sum(hidden * head[...], axis=0, keepdims=True)
            slope_out[44, pl.ds(4 * k + zz, 1), :] = logit
        return owned

    rows(0, False)
    lax.fori_loop(1, 7, lambda k, carry: rows(k, True), True)
    rows(7, False)
    slope_out[44, 0:32, :] = sigmoid(slope_out[44, 0:32, :])
    slope_out[44, 32:64, :] = jnp.zeros((32, 128), F32)
    fold_taps(kernel, folded)


def shifts(f):
    z_at = lax.broadcasted_iota(jnp.int32, (32, 128), 0)
    y_at = lax.broadcasted_iota(jnp.int32, (32, 128), 1)
    return (
        jnp.where(z_at < 31, pltpu.roll(f, 31, 0), 0.0),
        jnp.where(z_at > 0, pltpu.roll(f, 1, 0), 0.0),
        jnp.where(y_at < 127, pltpu.roll(f, 127, 1), 0.0),
        jnp.where(y_at > 0, pltpu.roll(f, 1, 1), 0.0),
    )


def windowed(left, own, right, field, offset, first):
    def get(w):
        if w < 6:
            return left[offset + w - first]
        if w < 12:
            return own[6 * field + w - 6]
        return right[offset + w - 12]

    return get


def medium_kernel(
    place,
    wave_now,
    wave_prev,
    adj_next,
    adj_after,
    density,
    receivers_in,
    observed_in,
    after,
    left,
    right,
    own,
    counts_out,
    counts,
    receivers,
    observed,
    sems,
):
    fields = (wave_now.at[0], wave_prev.at[0], adj_next.at[0], adj_after.at[0], density)
    wait_all(
        start_all(
            [pltpu.make_async_copy(f, own.at[pl.ds(6 * i, 6)], sems.at[i]) for i, f in enumerate(fields)]
            + [
                pltpu.make_async_copy(receivers_in, receivers, sems.at[5]),
                pltpu.make_async_copy(observed_in, observed, sems.at[6]),
            ]
        )
    )
    local = receivers[...] - (place[0] * 6 - 3) * 4096
    at_row = lax.broadcasted_iota(jnp.int32, (384, 128), 0) == (local >> 7)
    at_y = lax.broadcasted_iota(jnp.int32, (128, 128), 0) == (local & 127)
    picks = [jnp.where(at_y, 1.0, 0.0).astype(BF16)]
    for n in range(3):
        for piece in split(observed[n], 3):
            picks.append(jnp.where(at_y, piece.astype(F32), 0.0).astype(BF16))
    maps = lax.dot_general(
        jnp.where(at_row, 1.0, 0.0).astype(BF16),
        jnp.concatenate(picks, axis=0),
        NT,
        preferred_element_type=F32,
    )
    counts[0] = maps[:, 0:128]
    for n in range(3):
        at = 128 + 384 * n
        counts[1 + n] = maps[:, at : at + 128] + maps[:, at + 128 : at + 256] + maps[:, at + 256 : at + 384]
    wait_all(start_all([pltpu.make_async_copy(counts, counts_out, sems.at[7])]))


def wave_kernel(
    place,
    source,
    pulses_in,
    left,
    right,
    speeds,
    own,
    counts_in,
    send_out,
    counts,
    pulses,
    faces,
    buoy,
    coef,
    speed,
    u2,
    u3,
    u4,
    laps,
    lam4,
    lam3,
    grads,
    sems,
):
    copies = start_all(
        [
            pltpu.make_async_copy(pulses_in, pulses, sems.at[0]),
            pltpu.make_async_copy(counts_in, counts, sems.at[1]),
        ]
    )
    send = send_out.reshape(512, 128)
    u1 = windowed(left, own, right, 0, 0, 0)
    u0 = windowed(left, own, right, 1, 6, 1)
    lam5 = windowed(left, own, right, 2, 11, 2)
    lam6 = windowed(left, own, right, 3, 15, 3)
    dens = windowed(left, own, right, 4, 18, 0)
    cell = lax.broadcasted_iota(jnp.int32, (32, 128), 0) * 128 + lax.broadcasted_iota(
        jnp.int32, (32, 128), 1
    )

    for w in range(1, 17):
        for j in range(2):
            speed[w, pl.ds(j, 16, 2), :] = speeds[pl.ds(2 * (w - 1) + j, 16, 32), :]
    grads[...] = jnp.zeros_like(grads)
    for w in range(18):
        d = dens(w)
        buoy[w] = jnp.where(d > 0.0, 1.0 / d, 0.0)
    for w in range(1, 17):
        v = speed[w]
        coef[w] = courant * v * v * dens(w)
        centre = buoy[w]
        inside = jnp.where(centre > 0.0, 0.5, 0.0)
        for i, beside in enumerate((buoy[w + 1], buoy[w - 1]) + shifts(centre)):
            faces[i, w] = inside * (centre + beside)
    copies[0].wait()

    def laplace(f, w):
        centre = f(w)
        total = None
        for i, beside in enumerate((f(w + 1), f(w - 1)) + shifts(centre)):
            term = faces[i, w] * (beside - centre)
            total = term if total is None else total + term
        return total

    source_cell = source[0] - (place[0] * 6 - 6) * 4096

    def forward(f, before, n, rows, out):
        for w in rows:
            lap = laplace(f, w)
            if 5 <= w <= 12:
                laps[n, w - 5] = lap
            pulse = jnp.where(cell == source_cell - w * 4096, pulses[0, n], 0.0)
            out[w] = 2.0 * f(w) - before(w) + coef[w] * lap + pulse

    def row_of(ref):
        return lambda w: ref[w]

    forward(u1, u0, 0, range(1, 17), u2)
    forward(row_of(u2), u1, 1, range(2, 16), u3)
    forward(row_of(u3), row_of(u2), 2, range(3, 15), u4)

    def residual(u, n, w):
        at = slice(32 * (w - 3), 32 * (w - 2))
        return counts[0, at, :] * u[w] - counts[1 + n, at, :]

    def backward(f, before, u, n, rows, out):
        for w in rows:
            lap = laplace(lambda v: coef[v] * f(v), w)
            out[w] = 2.0 * f(w) - before(w) + lap + residual(u, n, w)

    copies[1].wait()
    backward(lam5, lam6, u4, 2, range(3, 15), lam4)
    backward(row_of(lam4), lam5, u3, 1, range(4, 14), lam3)
    for w in range(5, 13):
        lap4 = laplace(row_of(u4), w)
        lap = laplace(lambda v: coef[v] * lam3[v], w)
        lam2 = 2.0 * lam3[w] - lam4[w] + lap + residual(u2, 0, w)
        total = lam5(w) * lap4 + lam4[w] * laps[2, w - 5] + lam3[w] * laps[1, w - 5] + lam2 * laps[0, w - 5]
        grads[w - 5, 8:40, :] = total * (2.0 * courant * speed[w] * dens(w))
    for x in range(8):
        for zz in range(4):
            send[pl.ds(4 * x + zz, 16, 32), :] = grads[x, pl.ds(7 + zz, 16, 2), :]


def in_pairs(block):
    at = lax.broadcasted_iota(jnp.int32, (16, 128), 0)
    rest = block - block.astype(BF16).astype(F32)
    return jnp.where(at == 0, block, jnp.where(at == 1, rest, 0.0))


def backward_kernel(
    received, slopes, lines, low_out, parts_out, low, low_wide, terms, logit_grads, sem
):
    total = received[0]
    for s in range(1, 16):
        total = total + received[s]
    squash = slopes[44, 0:32, :]
    logit_grads[...] = total * speed_span * squash * (1.0 - squash)
    head_sum = jnp.zeros((64, 128), F32)
    bias_sum = jnp.zeros((64, 128), F32)
    for x in range(8):
        for zz in range(4):
            grad = logit_grads[4 * x + zz : 4 * x + zz + 1, :]
            pre_grad = grad * slopes[4 * x + zz]
            rounded = pre_grad.astype(BF16)
            low[x, zz] = rounded
            if 1 <= x <= 6 and 1 <= zz <= 2:
                px = (x - 1) % 2
                low_wide[2 * px + zz - 1, :, 64 * (x - 1 - px) : 64 * (x + 1 - px)] = rounded
                head_sum = head_sum + slopes[30 + 2 * x + zz - 1] * grad
                bias_sum = bias_sum + pre_grad

    copy = pltpu.make_async_copy(low, low_out, sem)
    copy.start()

    ones = jnp.ones((8, 128), BF16)
    row = None
    for piece in split(jnp.concatenate([head_sum, bias_sum], axis=0), 3):
        term = lax.dot_general(ones, piece, NT, preferred_element_type=F32)
        row = term if row is None else row + term
    parts_out[864:880, :] = in_pairs(jnp.concatenate([row, row], axis=0)).astype(BF16)
    parts_out[880:1024, :] = jnp.zeros((144, 128), BF16)

    parities = {-1: (0,), 0: (0, 1), 1: (1,)}
    found = {}
    for dx in (-1, 0, 1):
        for dz in (-1, 0, 1):
            combos = [(px, pz) for px in parities[dx] for pz in parities[dz]]
            if len(combos) == 2 and dx == 0:
                grads = jnp.concatenate([low_wide[2 * px + pz] for px, pz in combos], axis=0)
            else:
                first = 2 * combos[0][0] + combos[0][1]
                grads = low_wide[first : first + len(combos)].reshape(64 * len(combos), 384)
            beside = lines[1 + dz, :, 128 * (1 + dx) : 128 * (4 + dx)]
            product = lax.dot_general(grads, beside, NT, preferred_element_type=F32)
            for i, (px, pz) in enumerate(combos):
                found[dx, px, dz, pz] = at = len(found)
                terms[at] = product[64 * i : 64 * i + 64]
    pairs = {-1: ((-1, 0), (0, 1)), 0: ((0, 0), (0, 1)), 1: ((0, 0), (1, 1))}
    for a in (-1, 0, 1):
        for b in (-1, 0, 1):
            tap = None
            for dx, px in pairs[a]:
                for dz, pz in pairs[b]:
                    term = terms[found[dx, px, dz, pz]]
                    tap = term if tap is None else tap + term
            at = 96 * (3 * (a + 1) + b + 1)
            parts_out[at : at + 64, :] = tap[:, :128].astype(BF16)
            both = jnp.concatenate([tap[:32, 128:], tap[32:, 128:]], axis=1)
            parts_out[at + 64 : at + 96, :] = both.astype(BF16)
    copy.wait()


def latent_kernel(low_in, folded, after, latent_out, low, sem):
    copy = pltpu.make_async_copy(low_in, low, sem)
    copy.start()
    copy.wait()
    stacked = []
    for x in range(3):
        around = low[2 * x : 2 * x + 4].reshape(1024, 128)
        product = jnp.dot(folded[...], around, preferred_element_type=F32)
        both = product[:192] + product[192:]
        stacked.append(jnp.concatenate([both[64 * e : 64 * e + 64] for e in range(3)], axis=1))
    stacked = jnp.concatenate(stacked, axis=0)
    spread = spread_matrix()
    result = None
    for piece in split(stacked, 2):
        term = lax.dot_general(piece, spread, NT, preferred_element_type=F32)
        result = term if result is None else result + term
    for x in range(3):
        latent_out[x, 0] = result[64 * x : 64 * x + 64]


def sum_kernel(place, received, out):
    total = received[0].astype(F32)
    for s in range(1, received.shape[0]):
        total = total + received[s].astype(F32)
    if out.dtype == BF16:
        pair = jnp.broadcast_to(total[0:1] + total[1:2], (16, 128))
        total = jnp.where(place[0] == 54, in_pairs(pair), total)
    total = total.astype(out.dtype)
    for s in range(out.shape[0]):
        out[s] = total


def unpack_kernel(rows, kernel_out, head_out, bias_out):
    for tap in range(9):
        at = 96 * tap
        pair = rows[at : at + 64, :].astype(F32)
        kernel_out[3 * tap] = pair[:, :64]
        kernel_out[3 * tap + 1] = pair[:, 64:]
        last = rows[at + 64 : at + 96, :].astype(F32)
        kernel_out[3 * tap + 2, 0:32] = last[:, :64]
        kernel_out[3 * tap + 2, 32:64] = last[:, 64:]
    row = rows[864:880, :].astype(F32)
    row = row[0:1] + row[1:2]
    head_out[...] = row[:, :64]
    bias_out[...] = row[:, 64:]


def shape(dims, dtype=F32):
    return jax.ShapeDtypeStruct(dims, dtype)


VMEM = pl.BlockSpec(memory_space=pltpu.VMEM)
ANY = pl.BlockSpec(memory_space=pl.ANY)
HBM = pl.BlockSpec(memory_space=pltpu.HBM)
SMEM = pl.BlockSpec(memory_space=pltpu.SMEM)


def call(kernel, out_shape, in_specs, scratch=(), megabytes=8, flops=None):
    outs = out_shape if isinstance(out_shape, tuple) else (out_shape,)
    specs = tuple(HBM if hasattr(out, "memory_space") else VMEM for out in outs)
    return pl.pallas_call(
        kernel,
        out_shape=out_shape,
        in_specs=list(in_specs),
        out_specs=specs if isinstance(out_shape, tuple) else VMEM,
        scratch_shapes=list(scratch),
        compiler_params=pltpu.CompilerParams(vmem_limit_bytes=megabytes << 20),
        cost_estimate=flops and pl.CostEstimate(flops=flops, bytes_accessed=0, transcendentals=0),
    )


FIELD = pltpu.VMEM((18, 32, 128), F32)
pack = call(
    pack_kernel,
    (
        shape((24, 32, 128)),
        shape((24, 32, 128)),
        shape((3, 64, 64), BF16),
        shape((576, 192), BF16),
        shape((64, 128)),
        shape((64, 128)),
    ),
    [HBM] * 8 + [VMEM],
    [pltpu.VMEM((27, 64, 64), BF16), pltpu.VMEM((1, 64), F32), pltpu.SemaphoreType.DMA((13,))],
    6,
)
join = call(join_kernel, shape((9, 32, 128), BF16), [VMEM] * 3, (), 2)
decode = call(
    decode_kernel,
    (shape((16, 32, 128)), shape((3, 192, 640), BF16)),
    [VMEM] * 6,
    [
        pltpu.VMEM((3, 192, 1152), BF16),
        pltpu.VMEM((9, 6, 64, 128), F32),
        pltpu.VMEM((32, 128), F32),
    ],
    14,
    500_000_000,
)
slopes = call(
    slopes_kernel,
    (shape((45, 64, 128)), shape((384, 1024), BF16)),
    [VMEM] + [HBM] * 4 + [ANY],
    [
        pltpu.VMEM((576, 192), BF16),
        pltpu.VMEM((64, 128), F32),
        pltpu.VMEM((64, 128), F32),
        pltpu.VMEM((27, 64, 64), BF16),
        pltpu.VMEM((5, 12, 64, 128), F32),
        pltpu.SemaphoreType.DMA((4,)),
    ],
    14,
)
medium = call(
    medium_kernel,
    (shape((30, 32, 128)), pltpu.HBM((4, 384, 128), F32)),
    [SMEM] + [HBM] * 7 + [ANY] * 3,
    [
        pltpu.VMEM((4, 384, 128), F32),
        pltpu.VMEM((1, 128), jnp.int32),
        pltpu.VMEM((3, 1, 128), F32),
        pltpu.SemaphoreType.DMA((8,)),
    ],
    8,
    2_000_000_000,
)
waves = call(
    wave_kernel,
    shape((16, 32, 128)),
    [SMEM] * 2 + [HBM] + [VMEM] * 4 + [HBM],
    [
        pltpu.VMEM((4, 384, 128), F32),
        pltpu.SMEM((1, 3), F32),
        pltpu.VMEM((6, 18, 32, 128), F32),
        FIELD,
        FIELD,
        FIELD,
        FIELD,
        FIELD,
        FIELD,
        pltpu.VMEM((3, 8, 32, 128), F32),
        FIELD,
        FIELD,
        pltpu.VMEM((8, 48, 128), F32),
        pltpu.SemaphoreType.DMA((2,)),
    ],
    14,
)
backward = call(
    backward_kernel,
    (pltpu.HBM((8, 4, 64, 128), BF16), shape((1024, 128), BF16)),
    [VMEM] * 3,
    [
        pltpu.VMEM((8, 4, 64, 128), BF16),
        pltpu.VMEM((4, 64, 384), BF16),
        pltpu.VMEM((16, 64, 192), F32),
        pltpu.VMEM((32, 128), F32),
        pltpu.SemaphoreType.DMA,
    ],
    14,
)
latent_part = call(
    latent_kernel,
    shape((3, 1, 64, 64)),
    [HBM, VMEM, ANY],
    [pltpu.VMEM((8, 4, 64, 128), BF16), pltpu.SemaphoreType.DMA],
    14,
)


def in_hbm(x):
    return pltpu.with_memory_space_constraint(x, pltpu.HBM)


def shifted(block, axes, size):
    low = lax.ppermute(block[0], axes, [(i, i + 1) for i in range(size - 1)])
    high = lax.ppermute(block[1], axes, [(i + 1, i) for i in range(size - 1)])
    return low, high


def per_device(
    latent,
    kernel,
    conv_bias,
    head_weight,
    density,
    wave_prev,
    wave_now,
    adjoint_next,
    adjoint_after,
    source_cell,
    wavelet,
    receiver_cells,
    observed,
):
    place = lax.axis_index(TILE).astype(jnp.int32).reshape(1)
    fields = [in_hbm(f) for f in (wave_now, wave_prev, adjoint_next, adjoint_after, density)]
    taps = in_hbm(kernel)
    coarse = latent.reshape(3, 64, 64)
    low, high = shifted((coarse, coarse), TILE, 32)
    to_next, to_prev, middle, wall, bias, head = pack(
        *fields, in_hbm(coarse), taps, in_hbm(conv_bias.reshape(1, 64)), head_weight.reshape(1, 64)
    )
    nine = join(high, middle, low)
    z_prev, z_next = shifted((nine, nine), SHOT, 16)
    to_next, to_prev, nine = lax.optimization_barrier((to_next, to_prev, nine))
    left, right = shifted((to_next, to_prev), TILE, 32)

    speed, lines = decode(z_next, nine, z_prev, wall, bias, head)
    speeds = lax.all_to_all(speed, SHOT, 0, 0, tiled=True)
    records = jnp.transpose(observed, (1, 0, 2))
    own, counts = medium(
        place, *fields, in_hbm(receiver_cells), in_hbm(records), in_hbm(speed), left, right
    )
    strips = waves(
        place,
        source_cell,
        in_hbm(wavelet),
        left,
        right,
        speeds.reshape(512, 128),
        own,
        in_hbm(counts),
    )
    received = lax.all_to_all(strips, SHOT, 0, 0, tiled=True)
    slope, folded = slopes(lines, in_hbm(wall), in_hbm(bias), in_hbm(head), taps, in_hbm(strips))
    low, parts = backward(received, slope, lines)
    latent_grad = latent_part(in_hbm(low), folded, parts)

    pieces = lax.all_to_all(parts.reshape(64, 16, 128), NEAR, 0, 0, tiled=True)
    piece = lax.axis_index(NEAR).astype(jnp.int32).reshape(1)
    pieces = call(sum_kernel, shape((8, 16, 128)), [SMEM, VMEM])(piece, pieces)
    pieces = lax.all_to_all(pieces, "y", 0, 0, tiled=True)
    pieces = call(sum_kernel, shape((64, 16, 128), BF16), [SMEM, VMEM])(piece, pieces)
    whole = lax.all_to_all(pieces, NEAR, 0, 0, tiled=True)
    kernel_grad, head_grad, bias_grad = call(
        unpack_kernel, (shape((27, 64, 64)), shape((1, 64)), shape((1, 64))), [VMEM]
    )(whole.reshape(1024, 128))
    head_grad = head_grad.reshape(64)
    bias_grad = bias_grad.reshape(64)
    return latent_grad, kernel_grad, head_grad, bias_grad


def solution(mesh):
    fine_mesh = Mesh(mesh.devices.reshape(2, 8, 8, 2, 2), ("xlo", "z", "y", "xhi", "core"))
    return jax.shard_map(
        per_device,
        mesh=fine_mesh,
        in_specs=(
            P(TILE, SHOT, None, None),
            P(),
            P(),
            P(),
            P(TILE, None, None),
            P(SHOT, TILE, None, None),
            P(SHOT, TILE, None, None),
            P(SHOT, TILE, None, None),
            P(SHOT, TILE, None, None),
            P(SHOT),
            P(SHOT, None),
            P(SHOT, None),
            P(SHOT, None, None),
        ),
        out_specs=(P(TILE, SHOT, None, None), P(), P(), P()),
        check_vma=False,
    )
```

```python
import jax
import jax.numpy as jnp
from jax import lax
from jax.experimental import pallas as pl
from jax.experimental.pallas import tpu as pltpu
from jax.sharding import Mesh
from jax.sharding import PartitionSpec as P

SHOT = ("xlo", "z")
TILE = ("y", "xhi", "core")
NEAR = ("xlo", "z", "xhi", "core")
F32 = jnp.float32
BF16 = jnp.bfloat16
courant = 0.005
speed_low = 1.5
speed_span = 3.0
NT = (((1,), (1,)), ((), ()))


def sigmoid(v):
    return 1.0 / (1.0 + jnp.exp(-v))


def split(v, parts):
    out = []
    for _ in range(parts):
        piece = v.astype(BF16)
        out.append(piece)
        v = v - piece.astype(F32)
    return out


def spread_matrix():
    coarse = lax.broadcasted_iota(jnp.int32, (64, 384), 0)
    lane = lax.broadcasted_iota(jnp.int32, (64, 384), 1)
    fine = (lane & 127) + (lane >> 7) - 1
    return jnp.where((fine >> 1) == coarse, 1.0, 0.0).astype(BF16)


Z_LINE = ((0, 0, 1), (0, 1, 1), (1, 1, 2), (1, 2, 2))


def start_all(copies):
    for copy in copies:
        copy.start()
    return copies


def wait_all(copies):
    for copy in copies:
        copy.wait()


def pack_kernel(
    wave_now,
    wave_prev,
    adj_next,
    adj_after,
    density,
    latent,
    kernel_in,
    bias_in,
    head,
    to_next,
    to_prev,
    coarse,
    wall,
    bias_wide,
    head_wide,
    kernel,
    bias,
    sems,
):
    copies = [
        pltpu.make_async_copy(kernel_in, kernel, sems.at[11]),
        pltpu.make_async_copy(bias_in, bias, sems.at[12]),
        pltpu.make_async_copy(latent, coarse, sems.at[10]),
    ]
    fields = ((wave_now, 6), (wave_prev, 5), (adj_next, 4), (adj_after, 3), (density, 6))
    at = 0
    for i, (ref, rows) in enumerate(fields):
        field = ref if i == 4 else ref.at[0]
        here = pl.ds(at, rows)
        copies.append(pltpu.make_async_copy(field.at[pl.ds(6 - rows, rows)], to_next.at[here], sems.at[i]))
        copies.append(pltpu.make_async_copy(field.at[pl.ds(0, rows)], to_prev.at[here], sems.at[5 + i]))
        at += rows
    start_all(copies)
    head_wide[...] = jnp.broadcast_to(head[...].astype(F32), (128, 64)).T
    wait_all(copies[:2])
    bias_wide[...] = jnp.broadcast_to(bias[...], (128, 64)).T
    for a in range(3):
        for b in range(3):
            at = 64 * (3 * b + a)
            taps = [kernel[9 * a + 3 * b + e] for e in range(3)]
            wall[at : at + 64, :] = jnp.concatenate(taps, axis=1)
    wait_all(copies[2:])


def join_kernel(high, middle, low, out):
    for i, ref in enumerate((low, middle, high)):
        for x in range(3):
            out[3 * i + x] = jnp.concatenate([ref[x, 0:32], ref[x, 32:64]], axis=1)


def fold_taps(kernel, folded):
    reach = ((2,), (1, 2), (0, 1), (0,))
    for i in range(4):
        for j in range(0, 4, 2):
            blocks = []
            for jj in (j, j + 1):
                row = []
                for e in range(3):
                    total = None
                    for a in reach[i]:
                        for b in reach[jj]:
                            term = kernel[9 * a + 3 * b + e].astype(F32)
                            total = term if total is None else total + term
                    row.append(total)
                blocks.append(jnp.concatenate(row, axis=1))
            table = jnp.concatenate(blocks, axis=0).T
            high, low = split(table, 2)
            at = 64 * (4 * i + j)
            folded[0:192, at : at + 128] = high
            folded[192:384, at : at + 128] = low


def z_sums(product, rows, store):
    for a in range(3):
        for zz in rows:
            total = None
            for b in range(3):
                zi = Z_LINE[zz][b]
                term = product[64 * (3 * b + a) : 64 * (3 * b + a) + 64, 128 * zi : 128 * zi + 128]
                total = term if total is None else total + term
            store(a, zz, total)


def decode_kernel(z_next, own, z_prev, wall, bias, head, speed_out, lines_out, lines, sums, row_logit):
    spread = spread_matrix()
    for zi, ref in enumerate((z_prev, own, z_next)):
        packed = [ref[x] for x in range(9)]
        rows = jnp.concatenate([half for p in packed for half in (p[:, :64], p[:, 64:])], axis=0)
        fine = jnp.dot(rows, spread, preferred_element_type=F32).astype(BF16)
        for x in range(9):
            for e in range(3):
                piece = fine[64 * x : 64 * x + 64, 128 * e : 128 * e + 128]
                lines[zi, 64 * e : 64 * e + 64, 128 * x : 128 * x + 128] = piece
                if 2 <= x <= 6:
                    lines_out[zi, 64 * e : 64 * e + 64, 128 * (x - 2) : 128 * (x - 1)] = piece

    for first, count in ((0, 2), (2, 2), (4, 2), (6, 3)):
        at = slice(128 * first, 128 * (first + count))
        before = jnp.dot(wall[0:192, :], lines[0, :, at], preferred_element_type=F32)
        middle = jnp.dot(wall[...], lines[1, :, at], preferred_element_type=F32)
        after = jnp.dot(wall[384:576, :], lines[2, :, at], preferred_element_type=F32)
        for i in range(count):
            col = slice(128 * i, 128 * i + 128)
            for a in range(3):
                low, centre, high = [middle[64 * (3 * b + a) : 64 * (3 * b + a) + 64, col] for b in range(3)]
                block = slice(64 * a, 64 * a + 64)
                sums[first + i, 2 * a] = before[block, col] + (centre + high)
                sums[first + i, 2 * a + 1] = (low + centre) + after[block, col]

    def rows(k, carry):
        r = k + 1
        for j in range(2):
            pre = sums[(r - 1) // 2, j] + sums[r // 2, 2 + j] + sums[(r + 1) // 2, 4 + j] + bias[...]
            hidden = (pre * sigmoid(pre)).astype(BF16).astype(F32)
            row_logit[pl.ds(2 * k + j, 1), :] = jnp.sum(hidden * head[...], axis=0, keepdims=True)
        return carry

    lax.fori_loop(0, 16, rows, 0, unroll=2)
    speed = speed_low + speed_span * sigmoid(row_logit[...])
    for s in range(16):
        speed_out[s] = speed


def slopes_kernel(
    lines, wall_in, bias_in, head_in, kernel_in, after, slope_out, folded, wall, bias, head, kernel, sums, sems
):
    copies = start_all(
        [
            pltpu.make_async_copy(source, target, sems.at[i])
            for i, (source, target) in enumerate(
                ((wall_in, wall), (bias_in, bias), (head_in, head), (kernel_in, kernel))
            )
        ]
    )
    wait_all(copies)
    for x in range(5):
        columns = [lines[zi, :, 128 * x : 128 * x + 128] for zi in range(3)]
        product = jnp.dot(wall[...], jnp.concatenate(columns, axis=1), preferred_element_type=F32)

        def store(a, zz, total):
            sums[x, 4 * a + zz] = total

        z_sums(product, range(4), store)

    def rows(k, owned):
        r = k + 1
        for zz in range(4):
            pre = sums[(r - 1) // 2, zz] + sums[r // 2, 4 + zz] + sums[(r + 1) // 2, 8 + zz] + bias[...]
            gate = sigmoid(pre)
            hidden = (pre * gate).astype(BF16).astype(F32)
            slope_out[4 * k + zz] = head[...] * (gate * (1.0 + pre * (1.0 - gate)))
            if owned and zz in (1, 2):
                slope_out[30 + 2 * k + zz - 1] = hidden
            logit = jnp.sum(hidden * head[...], axis=0, keepdims=True)
            slope_out[44, pl.ds(4 * k + zz, 1), :] = logit
        return owned

    rows(0, False)
    lax.fori_loop(1, 7, lambda k, carry: rows(k, True), True)
    rows(7, False)
    slope_out[44, 0:32, :] = sigmoid(slope_out[44, 0:32, :])
    slope_out[44, 32:64, :] = jnp.zeros((32, 128), F32)
    fold_taps(kernel, folded)


def shifts(f):
    z_at = lax.broadcasted_iota(jnp.int32, (32, 128), 0)
    y_at = lax.broadcasted_iota(jnp.int32, (32, 128), 1)
    return (
        jnp.where(z_at < 31, pltpu.roll(f, 31, 0), 0.0),
        jnp.where(z_at > 0, pltpu.roll(f, 1, 0), 0.0),
        jnp.where(y_at < 127, pltpu.roll(f, 127, 1), 0.0),
        jnp.where(y_at > 0, pltpu.roll(f, 1, 1), 0.0),
    )


def windowed(left, own, right, field, offset, first):
    def get(w):
        if w < 6:
            return left[offset + w - first]
        if w < 12:
            return own[6 * field + w - 6]
        return right[offset + w - 12]

    return get


def medium_kernel(
    place,
    wave_now,
    wave_prev,
    adj_next,
    adj_after,
    density,
    receivers_in,
    observed_in,
    after,
    left,
    right,
    own,
    counts_out,
    counts,
    receivers,
    observed,
    sems,
):
    fields = (wave_now.at[0], wave_prev.at[0], adj_next.at[0], adj_after.at[0], density)
    wait_all(
        start_all(
            [pltpu.make_async_copy(f, own.at[pl.ds(6 * i, 6)], sems.at[i]) for i, f in enumerate(fields)]
            + [
                pltpu.make_async_copy(receivers_in, receivers, sems.at[5]),
                pltpu.make_async_copy(observed_in, observed, sems.at[6]),
            ]
        )
    )
    local = receivers[...] - (place[0] * 6 - 3) * 4096
    at_row = lax.broadcasted_iota(jnp.int32, (384, 128), 0) == (local >> 7)
    at_y = lax.broadcasted_iota(jnp.int32, (128, 128), 0) == (local & 127)
    picks = [jnp.where(at_y, 1.0, 0.0).astype(BF16)]
    for n in range(3):
        for piece in split(observed[n], 3):
            picks.append(jnp.where(at_y, piece.astype(F32), 0.0).astype(BF16))
    maps = lax.dot_general(
        jnp.where(at_row, 1.0, 0.0).astype(BF16),
        jnp.concatenate(picks, axis=0),
        NT,
        preferred_element_type=F32,
    )
    counts[0] = maps[:, 0:128]
    for n in range(3):
        at = 128 + 384 * n
        counts[1 + n] = maps[:, at : at + 128] + maps[:, at + 128 : at + 256] + maps[:, at + 256 : at + 384]
    wait_all(start_all([pltpu.make_async_copy(counts, counts_out, sems.at[7])]))


def wave_kernel(
    place,
    source,
    pulses_in,
    left,
    right,
    speeds,
    own,
    counts_in,
    send_out,
    counts,
    pulses,
    faces,
    buoy,
    coef,
    speed,
    u2,
    u3,
    u4,
    laps,
    lam4,
    lam3,
    grads,
    sems,
):
    copies = start_all(
        [
            pltpu.make_async_copy(pulses_in, pulses, sems.at[0]),
            pltpu.make_async_copy(counts_in, counts, sems.at[1]),
        ]
    )
    send = send_out.reshape(512, 128)
    u1 = windowed(left, own, right, 0, 0, 0)
    u0 = windowed(left, own, right, 1, 6, 1)
    lam5 = windowed(left, own, right, 2, 11, 2)
    lam6 = windowed(left, own, right, 3, 15, 3)
    dens = windowed(left, own, right, 4, 18, 0)
    cell = lax.broadcasted_iota(jnp.int32, (32, 128), 0) * 128 + lax.broadcasted_iota(
        jnp.int32, (32, 128), 1
    )

    for w in range(1, 17):
        for j in range(2):
            speed[w, pl.ds(j, 16, 2), :] = speeds[pl.ds(2 * (w - 1) + j, 16, 32), :]
    grads[...] = jnp.zeros_like(grads)
    for w in range(18):
        d = dens(w)
        buoy[w] = jnp.where(d > 0.0, 1.0 / d, 0.0)
    for w in range(1, 17):
        v = speed[w]
        coef[w] = courant * v * v * dens(w)
        centre = buoy[w]
        inside = jnp.where(centre > 0.0, 0.5, 0.0)
        for i, beside in enumerate((buoy[w + 1], buoy[w - 1]) + shifts(centre)):
            faces[i, w] = inside * (centre + beside)
    copies[0].wait()

    def laplace(f, w):
        centre = f(w)
        total = None
        for i, beside in enumerate((f(w + 1), f(w - 1)) + shifts(centre)):
            term = faces[i, w] * (beside - centre)
            total = term if total is None else total + term
        return total

    source_cell = source[0] - (place[0] * 6 - 6) * 4096

    def forward(f, before, n, rows, out):
        for w in rows:
            lap = laplace(f, w)
            if 5 <= w <= 12:
                laps[n, w - 5] = lap
            pulse = jnp.where(cell == source_cell - w * 4096, pulses[0, n], 0.0)
            out[w] = 2.0 * f(w) - before(w) + coef[w] * lap + pulse

    def row_of(ref):
        return lambda w: ref[w]

    forward(u1, u0, 0, range(1, 17), u2)
    forward(row_of(u2), u1, 1, range(2, 16), u3)
    forward(row_of(u3), row_of(u2), 2, range(3, 15), u4)

    def residual(u, n, w):
        at = slice(32 * (w - 3), 32 * (w - 2))
        return counts[0, at, :] * u[w] - counts[1 + n, at, :]

    def backward(f, before, u, n, rows, out):
        for w in rows:
            lap = laplace(lambda v: coef[v] * f(v), w)
            out[w] = 2.0 * f(w) - before(w) + lap + residual(u, n, w)

    copies[1].wait()
    backward(lam5, lam6, u4, 2, range(3, 15), lam4)
    backward(row_of(lam4), lam5, u3, 1, range(4, 14), lam3)
    for w in range(5, 13):
        lap4 = laplace(row_of(u4), w)
        lap = laplace(lambda v: coef[v] * lam3[v], w)
        lam2 = 2.0 * lam3[w] - lam4[w] + lap + residual(u2, 0, w)
        total = lam5(w) * lap4 + lam4[w] * laps[2, w - 5] + lam3[w] * laps[1, w - 5] + lam2 * laps[0, w - 5]
        grads[w - 5, 8:40, :] = total * (2.0 * courant * speed[w] * dens(w))
    for x in range(8):
        for zz in range(4):
            send[pl.ds(4 * x + zz, 16, 32), :] = grads[x, pl.ds(7 + zz, 16, 2), :]


def in_pairs(block):
    at = lax.broadcasted_iota(jnp.int32, (16, 128), 0)
    rest = block - block.astype(BF16).astype(F32)
    return jnp.where(at == 0, block, jnp.where(at == 1, rest, 0.0))


def backward_kernel(
    received, slopes, lines, low_out, parts_out, low, low_wide, terms, logit_grads, sem
):
    total = received[0]
    for s in range(1, 16):
        total = total + received[s]
    squash = slopes[44, 0:32, :]
    logit_grads[...] = total * speed_span * squash * (1.0 - squash)
    head_sum = jnp.zeros((64, 128), F32)
    bias_sum = jnp.zeros((64, 128), F32)
    for x in range(8):
        for zz in range(4):
            grad = logit_grads[4 * x + zz : 4 * x + zz + 1, :]
            pre_grad = grad * slopes[4 * x + zz]
            rounded = pre_grad.astype(BF16)
            low[x, zz] = rounded
            if 1 <= x <= 6 and 1 <= zz <= 2:
                px = (x - 1) % 2
                low_wide[2 * px + zz - 1, :, 64 * (x - 1 - px) : 64 * (x + 1 - px)] = rounded
                head_sum = head_sum + slopes[30 + 2 * x + zz - 1] * grad
                bias_sum = bias_sum + pre_grad

    copy = pltpu.make_async_copy(low, low_out, sem)
    copy.start()

    ones = jnp.ones((8, 128), BF16)
    row = None
    for piece in split(jnp.concatenate([head_sum, bias_sum], axis=0), 3):
        term = lax.dot_general(ones, piece, NT, preferred_element_type=F32)
        row = term if row is None else row + term
    parts_out[864:880, :] = in_pairs(jnp.concatenate([row, row], axis=0)).astype(BF16)
    parts_out[880:1024, :] = jnp.zeros((144, 128), BF16)

    parities = {-1: (0,), 0: (0, 1), 1: (1,)}
    found = {}
    for dx in (-1, 0, 1):
        for dz in (-1, 0, 1):
            combos = [(px, pz) for px in parities[dx] for pz in parities[dz]]
            if len(combos) == 2 and dx == 0:
                grads = jnp.concatenate([low_wide[2 * px + pz] for px, pz in combos], axis=0)
            else:
                first = 2 * combos[0][0] + combos[0][1]
                grads = low_wide[first : first + len(combos)].reshape(64 * len(combos), 384)
            beside = lines[1 + dz, :, 128 * (1 + dx) : 128 * (4 + dx)]
            product = lax.dot_general(grads, beside, NT, preferred_element_type=F32)
            for i, (px, pz) in enumerate(combos):
                found[dx, px, dz, pz] = at = len(found)
                terms[at] = product[64 * i : 64 * i + 64]
    pairs = {-1: ((-1, 0), (0, 1)), 0: ((0, 0), (0, 1)), 1: ((0, 0), (1, 1))}
    for a in (-1, 0, 1):
        for b in (-1, 0, 1):
            tap = None
            for dx, px in pairs[a]:
                for dz, pz in pairs[b]:
                    term = terms[found[dx, px, dz, pz]]
                    tap = term if tap is None else tap + term
            at = 96 * (3 * (a + 1) + b + 1)
            parts_out[at : at + 64, :] = tap[:, :128].astype(BF16)
            both = jnp.concatenate([tap[:32, 128:], tap[32:, 128:]], axis=1)
            parts_out[at + 64 : at + 96, :] = both.astype(BF16)
    copy.wait()


def latent_kernel(low_in, folded, after, latent_out, low, latent, sem):
    copy = pltpu.make_async_copy(low_in, low, sem)
    copy.start()
    copy.wait()
    stacked = []
    for x in range(3):
        around = low[2 * x : 2 * x + 4].reshape(1024, 128)
        product = jnp.dot(folded[...], around, preferred_element_type=F32)
        both = product[:192] + product[192:]
        stacked.append(jnp.concatenate([both[64 * e : 64 * e + 64] for e in range(3)], axis=1))
    stacked = jnp.concatenate(stacked, axis=0)
    spread = spread_matrix()
    result = None
    for piece in split(stacked, 2):
        term = lax.dot_general(piece, spread, NT, preferred_element_type=F32)
        result = term if result is None else result + term
    for x in range(3):
        latent[x, 0] = result[64 * x : 64 * x + 64]
    copy = pltpu.make_async_copy(latent, latent_out, sem)
    copy.start()
    copy.wait()


def sum_kernel(place, received, after, out):
    total = received[0].astype(F32)
    for s in range(1, received.shape[0]):
        total = total + received[s].astype(F32)
    if out.dtype == BF16:
        pair = jnp.broadcast_to(total[0:1] + total[1:2], (16, 128))
        total = jnp.where(place[0] == 54, in_pairs(pair), total)
    total = total.astype(out.dtype)
    for s in range(out.shape[0]):
        out[s] = total


def unpack_kernel(rows, kernel_out, head_out, bias_out):
    for tap in range(9):
        at = 96 * tap
        pair = rows[at : at + 64, :].astype(F32)
        kernel_out[3 * tap] = pair[:, :64]
        kernel_out[3 * tap + 1] = pair[:, 64:]
        last = rows[at + 64 : at + 96, :].astype(F32)
        kernel_out[3 * tap + 2, 0:32] = last[:, :64]
        kernel_out[3 * tap + 2, 32:64] = last[:, 64:]
    row = rows[864:880, :].astype(F32)
    row = row[0:1] + row[1:2]
    head_out[...] = row[:, :64]
    bias_out[...] = row[:, 64:]


def shape(dims, dtype=F32):
    return jax.ShapeDtypeStruct(dims, dtype)


VMEM = pl.BlockSpec(memory_space=pltpu.VMEM)
ANY = pl.BlockSpec(memory_space=pl.ANY)
HBM = pl.BlockSpec(memory_space=pltpu.HBM)
SMEM = pl.BlockSpec(memory_space=pltpu.SMEM)


def call(kernel, out_shape, in_specs, scratch=(), megabytes=8, flops=None):
    outs = out_shape if isinstance(out_shape, tuple) else (out_shape,)
    specs = tuple(HBM if hasattr(out, "memory_space") else VMEM for out in outs)
    return pl.pallas_call(
        kernel,
        out_shape=out_shape,
        in_specs=list(in_specs),
        out_specs=specs if isinstance(out_shape, tuple) else specs[0],
        scratch_shapes=list(scratch),
        compiler_params=pltpu.CompilerParams(vmem_limit_bytes=megabytes << 20),
        cost_estimate=flops and pl.CostEstimate(flops=flops, bytes_accessed=0, transcendentals=0),
    )


FIELD = pltpu.VMEM((18, 32, 128), F32)
pack = call(
    pack_kernel,
    (
        shape((24, 32, 128)),
        shape((24, 32, 128)),
        shape((3, 64, 64), BF16),
        shape((576, 192), BF16),
        shape((64, 128)),
        shape((64, 128)),
    ),
    [HBM] * 8 + [VMEM],
    [pltpu.VMEM((27, 64, 64), BF16), pltpu.VMEM((1, 64), F32), pltpu.SemaphoreType.DMA((13,))],
    6,
)
join = call(join_kernel, shape((9, 32, 128), BF16), [VMEM] * 3, (), 2)
decode = call(
    decode_kernel,
    (shape((16, 32, 128)), shape((3, 192, 640), BF16)),
    [VMEM] * 6,
    [
        pltpu.VMEM((3, 192, 1152), BF16),
        pltpu.VMEM((9, 6, 64, 128), F32),
        pltpu.VMEM((32, 128), F32),
    ],
    14,
    500_000_000,
)
slopes = call(
    slopes_kernel,
    (shape((45, 64, 128)), shape((384, 1024), BF16)),
    [VMEM] + [HBM] * 4 + [ANY],
    [
        pltpu.VMEM((576, 192), BF16),
        pltpu.VMEM((64, 128), F32),
        pltpu.VMEM((64, 128), F32),
        pltpu.VMEM((27, 64, 64), BF16),
        pltpu.VMEM((5, 12, 64, 128), F32),
        pltpu.SemaphoreType.DMA((4,)),
    ],
    14,
)
medium = call(
    medium_kernel,
    (shape((30, 32, 128)), pltpu.HBM((4, 384, 128), F32)),
    [SMEM] + [HBM] * 7 + [ANY] * 3,
    [
        pltpu.VMEM((4, 384, 128), F32),
        pltpu.VMEM((1, 128), jnp.int32),
        pltpu.VMEM((3, 1, 128), F32),
        pltpu.SemaphoreType.DMA((8,)),
    ],
    8,
    2_000_000_000,
)
waves = call(
    wave_kernel,
    shape((16, 32, 128)),
    [SMEM] * 2 + [HBM] + [VMEM] * 4 + [HBM],
    [
        pltpu.VMEM((4, 384, 128), F32),
        pltpu.SMEM((1, 3), F32),
        pltpu.VMEM((6, 18, 32, 128), F32),
        FIELD,
        FIELD,
        FIELD,
        FIELD,
        FIELD,
        FIELD,
        pltpu.VMEM((3, 8, 32, 128), F32),
        FIELD,
        FIELD,
        pltpu.VMEM((8, 48, 128), F32),
        pltpu.SemaphoreType.DMA((2,)),
    ],
    14,
)
backward = call(
    backward_kernel,
    (pltpu.HBM((8, 4, 64, 128), BF16), shape((1024, 128), BF16)),
    [VMEM] * 3,
    [
        pltpu.VMEM((8, 4, 64, 128), BF16),
        pltpu.VMEM((4, 64, 384), BF16),
        pltpu.VMEM((16, 64, 192), F32),
        pltpu.VMEM((32, 128), F32),
        pltpu.SemaphoreType.DMA,
    ],
    14,
)
latent_part = call(
    latent_kernel,
    pltpu.HBM((3, 1, 64, 64), F32),
    [HBM, VMEM, ANY],
    [
        pltpu.VMEM((8, 4, 64, 128), BF16),
        pltpu.VMEM((3, 1, 64, 64), F32),
        pltpu.SemaphoreType.DMA,
    ],
    14,
)


def in_hbm(x):
    return pltpu.with_memory_space_constraint(x, pltpu.HBM)


def shifted(block, axes, size):
    low = lax.ppermute(block[0], axes, [(i, i + 1) for i in range(size - 1)])
    high = lax.ppermute(block[1], axes, [(i + 1, i) for i in range(size - 1)])
    return low, high


def per_device(
    latent,
    kernel,
    conv_bias,
    head_weight,
    density,
    wave_prev,
    wave_now,
    adjoint_next,
    adjoint_after,
    source_cell,
    wavelet,
    receiver_cells,
    observed,
):
    place = lax.axis_index(TILE).astype(jnp.int32).reshape(1)
    fields = [in_hbm(f) for f in (wave_now, wave_prev, adjoint_next, adjoint_after, density)]
    taps = in_hbm(kernel)
    coarse = latent.reshape(3, 64, 64)
    low, high = shifted((coarse, coarse), TILE, 32)
    to_next, to_prev, middle, wall, bias, head = pack(
        *fields, in_hbm(coarse), taps, in_hbm(conv_bias.reshape(1, 64)), head_weight.reshape(1, 64)
    )
    nine = join(high, middle, low)
    z_prev, z_next = shifted((nine, nine), SHOT, 16)
    to_next, to_prev, nine = lax.optimization_barrier((to_next, to_prev, nine))
    left, right = shifted((to_next, to_prev), TILE, 32)

    speed, lines = decode(z_next, nine, z_prev, wall, bias, head)
    speeds = lax.all_to_all(speed, SHOT, 0, 0, tiled=True)
    records = jnp.transpose(observed, (1, 0, 2))
    own, counts = medium(
        place, *fields, in_hbm(receiver_cells), in_hbm(records), in_hbm(speed), left, right
    )
    strips = waves(
        place,
        source_cell,
        in_hbm(wavelet),
        left,
        right,
        speeds.reshape(512, 128),
        own,
        in_hbm(counts),
    )
    received = lax.all_to_all(strips, SHOT, 0, 0, tiled=True)
    slope, folded = slopes(lines, in_hbm(wall), in_hbm(bias), in_hbm(head), taps, in_hbm(strips))
    low, parts = backward(received, slope, lines)
    latent_grad = latent_part(in_hbm(low), folded, parts)

    pieces = lax.all_to_all(parts.reshape(64, 16, 128), NEAR, 0, 0, tiled=True)
    piece = lax.axis_index(NEAR).astype(jnp.int32).reshape(1)
    pieces = call(sum_kernel, shape((8, 16, 128)), [SMEM, VMEM, ANY])(piece, pieces, in_hbm(latent_grad))
    pieces = lax.all_to_all(pieces, "y", 0, 0, tiled=True)
    pieces = call(sum_kernel, shape((64, 16, 128), BF16), [SMEM, VMEM, ANY])(piece, pieces, in_hbm(latent_grad))
    whole = lax.all_to_all(pieces, NEAR, 0, 0, tiled=True)
    kernel_grad, head_grad, bias_grad = call(
        unpack_kernel, (shape((27, 64, 64)), shape((1, 64)), shape((1, 64))), [VMEM]
    )(whole.reshape(1024, 128))
    head_grad = head_grad.reshape(64)
    bias_grad = bias_grad.reshape(64)
    return latent_grad, kernel_grad, head_grad, bias_grad


def solution(mesh):
    fine_mesh = Mesh(mesh.devices.reshape(2, 8, 8, 2, 2), ("xlo", "z", "y", "xhi", "core"))
    return jax.shard_map(
        per_device,
        mesh=fine_mesh,
        in_specs=(
            P(TILE, SHOT, None, None),
            P(),
            P(),
            P(),
            P(TILE, None, None),
            P(SHOT, TILE, None, None),
            P(SHOT, TILE, None, None),
            P(SHOT, TILE, None, None),
            P(SHOT, TILE, None, None),
            P(SHOT),
            P(SHOT, None),
            P(SHOT, None),
            P(SHOT, None, None),
        ),
        out_specs=(P(TILE, SHOT, None, None), P(), P(), P()),
        check_vma=False,
    )
```
